128 devices in a mesh: lat: 16 (over z_lo, x, core), lon: 8 (over z_hi, y).
Axes of the slice: x: 4, y: 4, z: 4 (z_hi: 2, z_lo: 2; z = z_hi * 2 + z_lo), core: 2. Of those that a mesh axis runs over, the one named last changes fastest.
Arguments:
- tokens: bfloat16 [8, 96, 192, 192], P(None, 'lat', 'lon'), may hold values from -6 to 6
- lat_valid: int32 [96], P('lat'), may hold values from 0 to 1, as said below
- gain_attn: bfloat16 [192], replicated, may hold values from 0.099609375 to 1.8984375
- w_qkv: bfloat16 [192, 576], replicated, may hold values from -0.4375 to 0.4375
- w_proj: bfloat16 [192, 192], replicated, may hold values from -0.4375 to 0.4375
- gain_mlp: bfloat16 [192], replicated, may hold values from 0.099609375 to 1.8984375
- w_up: bfloat16 [192, 768], replicated, may hold values from -0.4375 to 0.4375
- w_down: bfloat16 [768, 192], replicated, may hold values from -0.21875 to 0.21875
- bias_table: float32 [64, 6, 3312], P('lat'), may hold values from -6 to 6
- index_table: int32 [144, 144], replicated, may hold values from 0 to 3311, as said below
- cotangent: bfloat16 [8, 96, 192, 192], P(None, 'lat', 'lon'), may hold values from -6 to 6
Outputs:
- updated: bfloat16 [8, 96, 192, 192], P(None, 'lat', 'lon')
- d_tokens: bfloat16 [8, 96, 192, 192], P(None, 'lat', 'lon')
- d_gain_attn: float32 [192], replicated
- d_qkv: float32 [192, 576], replicated
- d_proj: float32 [192, 192], replicated
- d_gain_mlp: float32 [192], replicated
- d_up: float32 [192, 768], replicated
- d_down: float32 [768, 192], replicated
- d_bias_table: float32 [64, 6, 3312], P('lat')
The draws below stay inside these ranges and needn't reach their ends.
Inputs may be any that keep to these rules, and one draw needn't show every extreme that they name: `lat_valid`: 1 on every row but the last 1 to 5 rows, which are 0. `index_table`: every row of the bias table is named by some entry.
All inputs are finite; a program needn't handle non-finite values.
Results may differ from the reference program's by a relative error of at most 0.025.
Values may be sent and summed in bfloat16 or wider, within the bound.
A program may use at most 192 MiB of HBM per device.

```python
import jax
import jax.numpy as jnp
from jax import lax

C = 192
HEADS = 6
HIDDEN_SIZE = 768
LEVELS = 8
WIN_Z = 2
WIN_LAT = 6
WIN_LON = 12
LAT = 96
LON = 192
POS = 3312
TYPES = 64


def draw_lat_valid(key, part):
    key = jax.random.fold_in(key, 11)
    padded = jax.random.randint(key, (), 1, 6, dtype=jnp.int32)
    return (jnp.arange(LAT, dtype=jnp.int32) < LAT - padded).astype(jnp.int32)


def draw_index_table(key, part):
    key = jax.random.fold_in(key, 23)
    positions = jnp.arange(WIN_Z * WIN_LAT * WIN_LON, dtype=jnp.int32)
    in_depth = positions // (WIN_LAT * WIN_LON)
    in_row = positions // WIN_LON % WIN_LAT
    in_col = positions % WIN_LON
    col_span = 2 * WIN_LON - 1
    base_index = in_col[:, None] - in_col[None, :] + WIN_LON - 1 + col_span * (in_row[:, None] + WIN_LAT * in_row[None, :]) + col_span * WIN_LAT * WIN_LAT * (in_depth[:, None] + WIN_Z * in_depth[None, :])
    shuffled = jax.random.permutation(key, POS).astype(jnp.int32)
    return shuffled[base_index]


def steps_of(rng, shape, split, smallest, top_value):
    loudness = 1.0
    for axis_at, blocks in split:
        steps = jax.random.uniform(jax.random.fold_in(jax.random.fold_in(rng, 6), axis_at), (blocks,), jnp.float32, smallest / len(split), top_value / len(split))
        loudness = loudness * jnp.repeat(jnp.exp(steps), shape[axis_at] // blocks).reshape((-1,) + (1,) * (len(shape) - 1 - axis_at))
    return loudness


def gaussian(own_key, shape, width, most, shards=(), kind=jnp.bfloat16):
    gain = steps_of(own_key, shape, shards, -0.22, 0.18) if shards else 1.0
    drawn = jax.random.normal(own_key, shape, jnp.float32) * width * gain
    return jnp.minimum(jnp.maximum(drawn, -most), most).astype(kind)


def setup_inputs(seed: int = 0) -> dict:
    splits = jax.random.split(jax.random.key(seed), 12)
    return {
        "tokens": gaussian(splits[0], (LEVELS, LAT, LON, C), 1.0, 6.0, ((1, 16), (2, 8))),
        "lat_valid": draw_lat_valid(jax.random.fold_in(splits[11], 71), 0),
        "gain_attn": jnp.clip(1.0 + 0.18 * jax.random.normal(splits[2], (C,), jnp.float32), 0.099609375, 1.8984375).astype(jnp.bfloat16),
        "w_qkv": gaussian(splits[3], (C, 3 * C), C ** -0.5, 0.4375),
        "w_proj": gaussian(splits[4], (C, C), C ** -0.5, 0.4375),
        "gain_mlp": jnp.clip(1.0 + 0.18 * jax.random.normal(splits[5], (C,), jnp.float32), 0.099609375, 1.8984375).astype(jnp.bfloat16),
        "w_up": gaussian(splits[6], (C, HIDDEN_SIZE), C ** -0.5, 0.4375),
        "w_down": gaussian(splits[7], (HIDDEN_SIZE, C), HIDDEN_SIZE ** -0.5, 0.21875),
        "bias_table": gaussian(splits[8], (TYPES, HEADS, POS), 1.0, 6.0, ((0, 16),), jnp.float32),
        "index_table": draw_index_table(jax.random.fold_in(splits[11], 71), 0),
        "cotangent": gaussian(splits[10], (LEVELS, LAT, LON, C), 1.0, 6.0, ((1, 16), (2, 8))),
    }


norm_eps = 1e-05

def product(form, left, right):
    return jnp.einsum(form, left.astype(jnp.float32), right.astype(jnp.float32))

def layer_norm(inputs, norm_gain):
    inputs = inputs.astype(jnp.float32)
    center = inputs - lax.optimization_barrier(jnp.mean(inputs, axis=-1, keepdims=True))
    rscale = lax.rsqrt(lax.optimization_barrier(jnp.mean(center * center, axis=-1, keepdims=True)) + norm_eps)
    return center * rscale * norm_gain.astype(jnp.float32)

def norm_back(inputs, norm_gain, incoming):
    inputs = inputs.astype(jnp.float32)
    center = inputs - lax.optimization_barrier(jnp.mean(inputs, axis=-1, keepdims=True))
    rscale = lax.rsqrt(lax.optimization_barrier(jnp.mean(center * center, axis=-1, keepdims=True)) + norm_eps)
    normed = center * rscale
    scaled = incoming * norm_gain.astype(jnp.float32)
    d_inputs = rscale * (scaled - lax.optimization_barrier(jnp.mean(scaled, axis=-1, keepdims=True)) - normed * lax.optimization_barrier(jnp.mean(scaled * normed, axis=-1, keepdims=True)))
    d_gain = lax.optimization_barrier(jnp.sum((incoming * normed).reshape(-1, inputs.shape[-1]), axis=0))
    return (d_inputs, d_gain)

def to_windows(grid_field):
    levels, row_count, col_count, channels = grid_field.shape
    blocks = grid_field.reshape(levels // WIN_Z, WIN_Z, row_count // WIN_LAT, WIN_LAT, col_count // WIN_LON, WIN_LON, channels)
    blocks = blocks.transpose(0, 2, 4, 1, 3, 5, 6)
    return blocks.reshape(levels // WIN_Z, row_count // WIN_LAT, col_count // WIN_LON, WIN_Z * WIN_LAT * WIN_LON, channels)

def from_windows(blocks, levels, row_count, col_count):
    channels = blocks.shape[-1]
    blocks = blocks.reshape(levels // WIN_Z, row_count // WIN_LAT, col_count // WIN_LON, WIN_Z, WIN_LAT, WIN_LON, channels)
    return blocks.transpose(0, 3, 1, 4, 2, 5, 6).reshape(levels, row_count, col_count, channels)

def window_regions(zone_count, last_band):
    positions = jnp.arange(WIN_Z * WIN_LAT * WIN_LON, dtype=jnp.int32)
    in_depth = positions // (WIN_LAT * WIN_LON)
    in_row = positions // WIN_LON % WIN_LAT
    zone_index = jnp.arange(zone_count, dtype=jnp.int32)[:, None]
    level_part = jnp.where(zone_index == zone_count - 1, 1 + (in_depth[None, :] >= WIN_Z - WIN_Z // 2).astype(jnp.int32), 0)
    row_part = jnp.where(last_band, 1 + (in_row >= WIN_LAT - WIN_LAT // 2).astype(jnp.int32), 0)
    region = 3 * level_part + row_part[None, :]
    return (region[:, :, None] == region[:, None, :]).astype(jnp.float32)

def attend(windows, w_qkv, w_proj, pos_bias, allowed):
    window_count, places, channels = windows.shape
    head_count = pos_bias.shape[0]
    head_width = channels // head_count
    triple = product('bpc,cd->bpd', windows, w_qkv).astype(jnp.bfloat16)
    parted = triple.reshape(window_count, places, 3, head_count, head_width)
    queries, key_part, values = (parted[:, :, 0], parted[:, :, 1], parted[:, :, 2])
    scores = product('bqhd,bkhd->bhqk', queries, key_part) * head_width ** (-0.5) + pos_bias[None]
    weights = jnp.exp(scores) * allowed[None, None]
    chances = (weights / lax.optimization_barrier(jnp.sum(weights, axis=-1, keepdims=True))).astype(jnp.bfloat16)
    merged = product('bhqk,bkhd->bqhd', chances, values).astype(jnp.bfloat16).reshape(window_count, places, channels)
    attended = product('bpc,cd->bpd', merged, w_proj).astype(jnp.bfloat16)
    return (attended, triple, chances, merged)

def attend_back(incoming, windows, triple, chances, merged, w_qkv, w_proj):
    window_count, places, channels = windows.shape
    head_count = chances.shape[1]
    head_width = channels // head_count
    d_proj = product('bpc,bpd->cd', merged, incoming)
    d_merged = product('bpd,cd->bpc', incoming, w_proj).astype(jnp.bfloat16).reshape(window_count, places, head_count, head_width)
    parted = triple.reshape(window_count, places, 3, head_count, head_width)
    queries, key_part, values = (parted[:, :, 0], parted[:, :, 1], parted[:, :, 2])
    d_chances = product('bqhd,bkhd->bhqk', d_merged, values)
    d_values = product('bhqk,bqhd->bkhd', chances, d_merged)
    chance_f = chances.astype(jnp.float32)
    d_scores = chance_f * (d_chances - lax.optimization_barrier(jnp.sum(chance_f * d_chances, axis=-1, keepdims=True)))
    scaled = (d_scores * head_width ** (-0.5)).astype(jnp.bfloat16)
    d_queries = product('bhqk,bkhd->bqhd', scaled, key_part)
    d_keys = product('bhqk,bqhd->bkhd', scaled, queries)
    d_triple = jnp.stack([d_queries, d_keys, d_values], axis=2).astype(jnp.bfloat16).reshape(window_count, places, 3 * channels)
    d_qkv = product('bpc,bpd->cd', windows, d_triple)
    d_windows = product('bpd,cd->bpc', d_triple, w_qkv).astype(jnp.bfloat16)
    return (d_windows, d_qkv, d_proj, lax.optimization_barrier(jnp.sum(d_scores, axis=0)))

def table_grad(score_sums, index_flat, entries):
    zone_count, head_count = (score_sums.shape[0], score_sums.shape[1])
    flat_scores = score_sums.reshape(zone_count * head_count, -1).T
    summed = jax.ops.segment_sum(flat_scores, index_flat, num_segments=entries)
    return summed.T.reshape(zone_count, head_count, entries)

def mlp_block(residual, gain_mlp, w_up, w_down):
    second_norm = layer_norm(residual, gain_mlp).astype(jnp.bfloat16)
    hidden_pre = jnp.dot(second_norm, w_up, preferred_element_type=jnp.float32)
    hidden = jax.nn.gelu(hidden_pre).astype(jnp.bfloat16)
    lifted = jnp.dot(hidden, w_down, preferred_element_type=jnp.float32)
    return (second_norm, hidden_pre, hidden, lifted)

def mlp_back(second_norm, hidden_pre, hidden, residual, gain_mlp, w_up, w_down, upstream):
    d_down = jnp.dot(hidden.T, upstream, preferred_element_type=jnp.float32)
    d_hidden = jnp.dot(upstream, w_down.T, preferred_element_type=jnp.float32)
    d_pre = jax.vjp(jax.nn.gelu, hidden_pre)[1](d_hidden)[0].astype(jnp.bfloat16)
    d_up = jnp.dot(second_norm.T, d_pre, preferred_element_type=jnp.float32)
    d_norm = jnp.dot(d_pre, w_up.T, preferred_element_type=jnp.float32)
    d_resid, d_gain = norm_back(residual, gain_mlp, d_norm)
    return (d_resid + upstream.astype(jnp.float32), d_up, d_down, d_gain)

def reference(tokens, lat_valid, gain_attn, w_qkv, w_proj, gain_mlp, w_up, w_down, bias_table, index_table, cotangent):
    levels, row_count, col_count, channels = tokens.shape
    zone_count = levels // WIN_Z
    band_count = row_count // WIN_LAT
    places = WIN_Z * WIN_LAT * WIN_LON
    entries = bias_table.shape[2]
    grad_scale = float(levels * row_count * col_count) ** (-0.5)
    offsets = (WIN_Z // 2, WIN_LAT // 2, WIN_LON // 2)
    back_offsets = (-(WIN_Z // 2), -(WIN_LAT // 2), -(WIN_LON // 2))
    keep_rows = (lat_valid > 0)[None, :, None, None]
    inputs = jnp.where(keep_rows, tokens, jnp.zeros_like(tokens))
    upstream = jnp.where(keep_rows, cotangent, jnp.zeros_like(cotangent))
    first_norm = layer_norm(inputs, gain_attn).astype(jnp.bfloat16)
    shifted = jnp.roll(first_norm, back_offsets, axis=(0, 1, 2))
    index_flat = index_table.reshape(-1).astype(jnp.int32)
    band_ids = jnp.arange(band_count, dtype=jnp.int32)

    def band_inputs(band):
        piece = lax.dynamic_slice_in_dim(shifted, band * WIN_LAT, WIN_LAT, 1)
        table_rows = lax.dynamic_slice_in_dim(bias_table, band * zone_count, zone_count, 0)
        pos_bias = jnp.take(table_rows, index_flat, axis=2).reshape(zone_count, -1, places, places)
        allowed = window_regions(zone_count, band == band_count - 1)
        return (to_windows(piece)[:, 0], pos_bias, allowed)

    def band_forward(band):
        windows, pos_bias, allowed = band_inputs(band)

        def zone_forward(zone_parts):
            return attend(zone_parts[0], w_qkv, w_proj, zone_parts[1], zone_parts[2])[0]
        return lax.map(zone_forward, (windows, pos_bias, allowed))
    attended = lax.map(band_forward, band_ids).transpose(1, 0, 2, 3, 4)
    attn_out = jnp.roll(from_windows(attended, levels, row_count, col_count), offsets, axis=(0, 1, 2))
    residual = (inputs.astype(jnp.float32) + attn_out.astype(jnp.float32)).astype(jnp.bfloat16)

    def band_mlp(band):
        res_band = lax.dynamic_slice_in_dim(residual, band * WIN_LAT, WIN_LAT, 1)
        up_band = lax.dynamic_slice_in_dim(upstream, band * WIN_LAT, WIN_LAT, 1)
        keep_band = lax.dynamic_slice_in_dim(keep_rows, band * WIN_LAT, WIN_LAT, 1)
        flat_res = res_band.reshape(-1, channels)
        second_norm, hidden_pre, hidden, lifted = mlp_block(flat_res, gain_mlp, w_up, w_down)
        upd_band = jnp.where(keep_band, res_band.astype(jnp.float32) + lifted.reshape(res_band.shape), 0.0).astype(jnp.bfloat16)
        d_res, d_up, d_down, d_gain = mlp_back(second_norm, hidden_pre, hidden, flat_res, gain_mlp, w_up, w_down, up_band.reshape(-1, channels))
        return (upd_band, d_res.reshape(res_band.shape), d_up, d_down, d_gain)
    upd_bands, d_res_bands, d_up_p, d_down_p, d_gain_mlp_p = lax.map(band_mlp, band_ids)
    updated = upd_bands.transpose(1, 0, 2, 3, 4).reshape(levels, row_count, col_count, channels)
    d_residual = d_res_bands.transpose(1, 0, 2, 3, 4).reshape(levels, row_count, col_count, channels)
    d_shifted = jnp.roll(d_residual.astype(jnp.bfloat16), back_offsets, axis=(0, 1, 2))

    def band_backward(band):
        windows, pos_bias, allowed = band_inputs(band)
        d_band = to_windows(lax.dynamic_slice_in_dim(d_shifted, band * WIN_LAT, WIN_LAT, 1))[:, 0]

        def zone_back(zone_parts):
            attended_z, triple, chances, merged = attend(zone_parts[0], w_qkv, w_proj, zone_parts[1], zone_parts[2])
            return attend_back(zone_parts[3], zone_parts[0], triple, chances, merged, w_qkv, w_proj)
        d_wins, d_qkv_z, d_proj_z, d_score_z = lax.map(zone_back, (windows, pos_bias, allowed, d_band))
        return (d_wins, lax.optimization_barrier(jnp.sum(d_qkv_z, axis=0)), lax.optimization_barrier(jnp.sum(d_proj_z, axis=0)), table_grad(d_score_z, index_flat, entries))
    d_wins, d_qkv_b, d_proj_b, d_table_b = lax.map(band_backward, band_ids)
    d_first = jnp.roll(from_windows(d_wins.transpose(1, 0, 2, 3, 4), levels, row_count, col_count), offsets, axis=(0, 1, 2))
    d_inputs, d_gain_attn = norm_back(inputs, gain_attn, d_first.astype(jnp.float32))
    d_tokens = jnp.where(keep_rows, d_residual + d_inputs, 0.0).astype(jnp.bfloat16)
    d_table = d_table_b.reshape(band_count * zone_count, -1, entries) * grad_scale
    return (updated, d_tokens, d_gain_attn * grad_scale, lax.optimization_barrier(jnp.sum(d_qkv_b, axis=0)) * grad_scale, lax.optimization_barrier(jnp.sum(d_proj_b, axis=0)) * grad_scale, lax.optimization_barrier(jnp.sum(d_gain_mlp_p, axis=0)) * grad_scale, lax.optimization_barrier(jnp.sum(d_up_p, axis=0)) * grad_scale, lax.optimization_barrier(jnp.sum(d_down_p, axis=0)) * grad_scale, d_table)
```

```python
import functools
import jax
import jax.numpy as jnp
from jax import lax
from jax.sharding import PartitionSpec as P
from jax.experimental import pallas as pl
from jax.experimental.pallas import tpu as pltpu

WIN_Z = 2
WIN_LAT = 6
WIN_LON = 12
PLACES = 144
HEADS = 6
WIDTH = 32
CH = 192
HIDDEN = 768
WINDOWS = 8
TOKENS = 1152
ZONES = 4
ROWS = ZONES * HEADS
ENTRIES = 3312
HI = 13
GROUPS = 18
SPAN = 1152
LOG2E = 1.4426950408889634
SCALE = 32**-0.5
NORM_EPS = 1e-05
F32 = jnp.float32
BF16 = jnp.bfloat16


def dot(left, right, left_dim=1, right_dim=0):
    return lax.dot_general(
        left, right, (((left_dim,), (right_dim,)), ((), ())), preferred_element_type=F32
    )


def entry_lanes(idx_ref, group):
    start = pl.multiple_of(group * 8, 8)
    main = idx_ref[pl.ds(start, 8), 0:128]
    rest = idx_ref[pl.ds(start, 8), 128:256].astype(F32)
    rest = pltpu.roll(rest, 0, 1, stride=16, stride_axis=0)
    place = lax.broadcasted_iota(jnp.int32, (8, 128), 0)
    lane = lax.broadcasted_iota(jnp.int32, (8, 128), 1)
    rest = jnp.sum(jnp.where(lane // 16 == place, rest, 0.0), axis=0, keepdims=True)
    rows = [main[i : i + 1] for i in range(8)] + [rest.astype(jnp.int32)]
    return jnp.concatenate(rows, axis=1)


def low_onehot(entries):
    low = jnp.broadcast_to(entries & 255, (256, SPAN))
    at = lax.broadcasted_iota(jnp.int32, (256, SPAN), 0)
    return jnp.where(low == at, 1.0, 0.0).astype(BF16)


def transposed_index(idx_in, idx_ref):
    idx_ref[:, 128:256] = jnp.zeros((PLACES, 128), jnp.int32)
    flipped = jnp.transpose(idx_in[...].astype(F32)).astype(jnp.int32)
    idx_ref[:, 0:PLACES] = flipped


def region_of(place, last_zone, last_band):
    depth = place // (WIN_LAT * WIN_LON)
    row = place // WIN_LON % WIN_LAT
    level = jnp.where(depth >= WIN_Z - WIN_Z // 2, 2, 1) * last_zone
    band = jnp.where(row >= WIN_LAT - WIN_LAT // 2, 2, 1) * last_band
    return 3 * level + band


def gather_kernel(last_ref, table_ref, idx_in, bias_ref, idx_ref, t2_ref):
    transposed_index(idx_in, idx_ref)
    for hi in range(HI):
        wide = min(256, ENTRIES - hi * 256)
        for zone in range(ZONES):
            part = table_ref[zone, :, hi * 256 : hi * 256 + wide] * LOG2E
            if wide < 256:
                part = jnp.concatenate([part, jnp.zeros((HEADS, 256 - wide), F32)], axis=1)
            t2_ref[hi * ROWS + zone * HEADS : hi * ROWS + (zone + 1) * HEADS, :] = part
    last_band = last_ref[0]

    def step(group, carry):
        entries = entry_lanes(idx_ref, group)
        onehot = low_onehot(entries)
        found = dot(t2_ref[...].astype(BF16), onehot)
        high = jnp.broadcast_to(entries >> 8, (ROWS, SPAN))
        bias = jnp.where(high == 0, found[0:ROWS], 0.0)
        for hi in range(1, HI):
            bias = jnp.where(high == hi, found[hi * ROWS : (hi + 1) * ROWS], bias)
        lane = lax.broadcasted_iota(jnp.int32, (ROWS, 128), 1)
        zone3 = (lax.broadcasted_iota(jnp.int32, (ROWS, 128), 0) >= ROWS - HEADS).astype(jnp.int32)
        rest = bias[:, 1024:1152]
        for i in range(8):
            key = group * 8 + i
            key_region = region_of(jnp.full((ROWS, 128), key, jnp.int32), zone3, last_band)
            main_ok = region_of(lane, zone3, last_band) == key_region
            rest_ok = region_of((lane & 15) + 128, zone3, last_band) == key_region
            main_i = jnp.where(main_ok, bias[:, i * 128 : (i + 1) * 128], -1e30)
            rest_i = rest if i == 0 else pltpu.roll(rest, 128 - 16 * i, 1)
            rest_i = jnp.where(rest_ok, rest_i, -1e30)
            bias_ref[0, pl.ds(key, ROWS, stride=PLACES), :] = main_i
            bias_ref[1, pl.ds(key, ROWS, stride=PLACES), :] = rest_i
        return carry

    lax.fori_loop(0, GROUPS, step, 0)


def scatter_kernel(ds_ref, idx_in, out_ref, idx_ref, acc_ref):
    transposed_index(idx_in, idx_ref)
    acc_ref[...] = jnp.zeros_like(acc_ref)
    lane = lax.broadcasted_iota(jnp.int32, (ROWS, 128), 1)

    def step(group, carry):
        entries = entry_lanes(idx_ref, group)
        onehot = low_onehot(entries)
        mains, rest = [], jnp.zeros((ROWS, 128), F32)
        for i in range(8):
            key = group * 8 + i
            mains.append(ds_ref[0, pl.ds(key, ROWS, stride=PLACES), :])
            rest_i = ds_ref[1, pl.ds(key, ROWS, stride=PLACES), :]
            if i:
                rest_i = pltpu.roll(rest_i, 16 * i, 1)
            rest = jnp.where(lane // 16 == i, rest_i, rest)
        grads = jnp.concatenate(mains + [rest], axis=1)
        high = jnp.broadcast_to(entries >> 8, (ROWS, SPAN))
        parts = [jnp.where(high == hi, grads, 0.0) for hi in range(HI)]
        left = jnp.concatenate(parts, axis=0).astype(BF16)
        acc_ref[...] += dot(left, onehot, 1, 1)
        return carry

    lax.fori_loop(0, GROUPS, step, 0)
    out_ref[...] = acc_ref[...]


def normed(values):
    center = values - jnp.mean(values, axis=-1, keepdims=True)
    rscale = lax.rsqrt(jnp.mean(center * center, axis=-1, keepdims=True) + NORM_EPS)
    return center * rscale, rscale


def norm_back(unit, rscale, gain, incoming):
    scaled = incoming * gain
    d_inputs = rscale * (
        scaled
        - jnp.mean(scaled, axis=-1, keepdims=True)
        - unit * jnp.mean(scaled * unit, axis=-1, keepdims=True)
    )
    return d_inputs, jnp.sum(incoming * unit, axis=0, keepdims=True)


def main_kernel(
    grad_scale,
    xw_ref,
    cw_ref,
    bias_ref,
    g1_ref,
    wqkv_ref,
    wproj_ref,
    g2_ref,
    wup_ref,
    wdown_ref,
    upd_ref,
    dtok_ref,
    dgain_ref,
    dqkv_ref,
    dproj_ref,
    dup_ref,
    ddown_ref,
    ds_ref,
    wqkvt_s,
    soft_s,
    trip_s,
    mrg_s,
    inv_s,
    first_s,
    resid_s,
    dres_s,
    dtrip_s,
):
    wqkvt_s[...] = jnp.transpose(wqkv_ref[...].astype(F32)).astype(BF16)
    g1 = g1_ref[...].astype(F32)
    g2 = g2_ref[...].astype(F32)

    def forward(w, carry):
        rows = pl.ds(pl.multiple_of(w * PLACES, PLACES), PLACES)
        x = xw_ref[rows, :].astype(F32)
        first = (normed(x)[0] * g1).astype(BF16)
        first_s[rows, :] = first
        triple = dot(wqkvt_s[...], first, 1, 1)
        trip_s[w, 0:CH] = (triple[0:CH] * (SCALE * LOG2E)).astype(BF16)
        trip_s[w, CH : 3 * CH] = triple[CH : 3 * CH].astype(BF16)
        zone = w // 2
        for h in range(HEADS):
            query = trip_s[w, h * WIDTH : (h + 1) * WIDTH]
            keys = trip_s[w, CH + h * WIDTH : CH + (h + 1) * WIDTH]
            values = trip_s[w, 2 * CH + h * WIDTH : 2 * CH + (h + 1) * WIDTH]
            at = pl.ds(pl.multiple_of((zone * HEADS + h) * PLACES, PLACES), PLACES)
            bias = jnp.concatenate([bias_ref[0, at, :], bias_ref[1, at, 0:16]], axis=1)
            scores = dot(keys, query, 0, 0) + bias
            weights = jnp.exp2(scores - jnp.max(scores, axis=0, keepdims=True))
            inv = 1.0 / jnp.sum(weights, axis=0, keepdims=True)
            weights = weights.astype(BF16)
            soft_s[w * HEADS + h] = weights
            inv_s[w, h : h + 1] = inv
            mrg_s[w, h * WIDTH : (h + 1) * WIDTH] = (dot(values, weights) * inv).astype(BF16)
        attended = dot(mrg_s[w], wproj_ref[...], 0, 0).astype(BF16).astype(F32)
        resid_s[rows, :] = (x + attended).astype(BF16)
        return carry

    lax.fori_loop(0, WINDOWS, forward, 0)

    dgain_ref[...] = jnp.zeros_like(dgain_ref)
    dqkv_ref[...] = jnp.zeros_like(dqkv_ref)
    dproj_ref[...] = jnp.zeros_like(dproj_ref)
    dup_ref[...] = jnp.zeros_like(dup_ref)
    ddown_ref[...] = jnp.zeros_like(ddown_ref)

    chunk = 384

    def feed_forward(c, carry):
        rows = pl.ds(pl.multiple_of(c * chunk, chunk), chunk)
        resid = resid_s[rows, :].astype(F32)
        up = cw_ref[rows, :]
        unit, rscale = normed(resid)
        second = unit * g2
        second_b = second.astype(BF16)
        pre = dot(second_b, wup_ref[...])
        c0, c1 = 0.7978845608028654, 0.7978845608028654 * 0.044715
        sq = pre * pre
        tanh = jnp.tanh(pre * (c0 + c1 * sq))
        half = 0.5 + 0.5 * tanh
        hidden = (pre * half).astype(BF16)
        slope = half + half * (1.0 - tanh) * pre * (c0 + (3.0 * c1) * sq)
        upd_ref[rows, :] = (resid + dot(hidden, wdown_ref[...])).astype(BF16)
        upt = jnp.transpose(up.astype(F32)).astype(BF16)
        ddown_ref[...] += dot(upt, hidden)
        d_pre = (slope * dot(up, wdown_ref[...], 1, 1)).astype(BF16)
        dup_ref[...] += dot(jnp.transpose(second).astype(BF16), d_pre)
        d_norm = dot(d_pre, wup_ref[...], 1, 1)
        d_in, d_gain = norm_back(unit, rscale, g2, d_norm)
        dres_s[rows, :] = d_in + up.astype(F32)
        dgain_ref[1:2] += d_gain
        return carry

    lax.fori_loop(0, TOKENS // chunk, feed_forward, 0)

    def backward(zone, carry):
        for side in range(2):
            w = zone * 2 + side
            rows = pl.ds(pl.multiple_of(w * PLACES, PLACES), PLACES)
            d_win = dres_s[rows, :].astype(BF16)
            dproj_ref[...] += dot(mrg_s[w], d_win)
            d_merged = dot(wproj_ref[...], d_win, 1, 1)
            for h in range(HEADS):
                at_q = slice(h * WIDTH, (h + 1) * WIDTH)
                at_k = slice(CH + h * WIDTH, CH + (h + 1) * WIDTH)
                at_v = slice(2 * CH + h * WIDTH, 2 * CH + (h + 1) * WIDTH)
                weights = soft_s[w * HEADS + h]
                inv = inv_s[w, h : h + 1]
                d_m = d_merged[h * WIDTH : (h + 1) * WIDTH] * inv
                lean = jnp.sum(d_m * mrg_s[w, at_q].astype(F32), axis=0, keepdims=True)
                d_mb = d_m.astype(BF16)
                d_chances = dot(trip_s[w, at_v], d_mb, 0, 0)
                d_scores = weights.astype(F32) * (d_chances - lean)
                at = pl.ds(pl.multiple_of((zone * HEADS + h) * PLACES, PLACES), PLACES)
                if side == 0:
                    ds_ref[0, at, :] = d_scores[:, 0:128]
                    ds_ref[1, at, 0:16] = d_scores[:, 128:PLACES]
                else:
                    ds_ref[0, at, :] += d_scores[:, 0:128]
                    ds_ref[1, at, 0:16] += d_scores[:, 128:PLACES]
                scaled = d_scores.astype(BF16)
                dtrip_s[at_q] = (dot(trip_s[w, at_k], scaled) * SCALE).astype(BF16)
                dtrip_s[at_k] = (dot(trip_s[w, at_q], scaled, 1, 1) * (1 / LOG2E)).astype(BF16)
                dtrip_s[at_v] = dot(d_mb, weights, 1, 1).astype(BF16)
            first_t = jnp.transpose(first_s[rows, :].astype(F32)).astype(BF16)
            d_triple = dtrip_s[...]
            dqkv_ref[...] += dot(first_t, d_triple, 1, 1)
            d_first = dot(d_triple, wqkvt_s[...], 0, 0).astype(BF16).astype(F32)
            unit, rscale = normed(xw_ref[rows, :].astype(F32))
            d_in, d_gain = norm_back(unit, rscale, g1, d_first)
            dtok_ref[rows, :] = (dres_s[rows, :] + d_in).astype(BF16)
            dgain_ref[0:1] += d_gain
        return carry

    lax.fori_loop(0, ZONES, backward, 0)
    for ref in (dgain_ref, dqkv_ref, dproj_ref, dup_ref, ddown_ref):
        ref[...] = ref[...] * grad_scale


VMEM_SPEC = pl.BlockSpec(memory_space=pltpu.VMEM)
LIMIT = 56 * 1024 * 1024


def vm(shape, dtype):
    return pltpu.VMEM(shape, dtype)


def bias_of(last, table, index_table):
    return pl.pallas_call(
        gather_kernel,
        out_shape=jax.ShapeDtypeStruct((2, ROWS * PLACES, 128), F32),
        in_specs=[pl.BlockSpec(memory_space=pltpu.SMEM), VMEM_SPEC, VMEM_SPEC],
        out_specs=VMEM_SPEC,
        scratch_shapes=[vm((PLACES, 256), jnp.int32), vm((HI * ROWS, 256), F32)],
        compiler_params=pltpu.CompilerParams(vmem_limit_bytes=LIMIT),
    )(last, table, index_table)


def table_sums(d_scores, index_table):
    return pl.pallas_call(
        scatter_kernel,
        out_shape=jax.ShapeDtypeStruct((HI * ROWS, 256), F32),
        in_specs=[VMEM_SPEC, VMEM_SPEC],
        out_specs=VMEM_SPEC,
        scratch_shapes=[vm((PLACES, 256), jnp.int32), vm((HI * ROWS, 256), F32)],
        compiler_params=pltpu.CompilerParams(vmem_limit_bytes=LIMIT),
    )(d_scores, index_table)


def block_pass(grad_scale, *args):
    sd = jax.ShapeDtypeStruct
    return pl.pallas_call(
        functools.partial(main_kernel, grad_scale),
        out_shape=[
            sd((TOKENS, CH), BF16),
            sd((TOKENS, CH), BF16),
            sd((8, CH), F32),
            sd((CH, 3 * CH), F32),
            sd((CH, CH), F32),
            sd((CH, HIDDEN), F32),
            sd((CH, HIDDEN), F32),
            sd((2, ROWS * PLACES, 128), F32),
        ],
        in_specs=[VMEM_SPEC] * 9,
        out_specs=[VMEM_SPEC] * 8,
        scratch_shapes=[
            vm((3 * CH, CH), BF16),
            vm((WINDOWS * HEADS, PLACES, PLACES), BF16),
            vm((WINDOWS, 3 * CH, PLACES), BF16),
            vm((WINDOWS, CH, PLACES), BF16),
            vm((WINDOWS, 8, PLACES), F32),
            vm((TOKENS, CH), BF16),
            vm((TOKENS, CH), BF16),
            vm((TOKENS, CH), F32),
            vm((3 * CH, PLACES), BF16),
        ],
        compiler_params=pltpu.CompilerParams(vmem_limit_bytes=LIMIT),
    )(*args)


def shifted(value, axis, steps):
    count = lax.axis_size(axis)
    pairs = [(source, (source + steps) % count) for source in range(count)]
    return lax.ppermute(value, axis, pairs)


def to_windows(grid_field):
    levels, row_count, col_count, channels = grid_field.shape
    blocks = grid_field.reshape(levels // 2, 2, 6, col_count // 12, 12, channels)
    return blocks.transpose(0, 3, 1, 2, 4, 5).reshape(TOKENS, channels)


def from_windows(blocks, levels, row_count, col_count):
    blocks = blocks.reshape(4, 2, 2, 6, 12, -1)
    return blocks.transpose(0, 2, 3, 1, 4, 5).reshape(levels, row_count, col_count, -1)


def into_shifted(grid_field):
    lower_rows = shifted(grid_field[:, :3], "lat", -1)
    grid_field = jnp.concatenate([grid_field[:, 3:], lower_rows], axis=1)
    next_cols = shifted(grid_field[:, :, :6], "lon", -1)
    grid_field = jnp.concatenate([grid_field[:, :, 6:], next_cols], axis=2)
    return jnp.roll(grid_field, -1, axis=0)


def from_shifted(grid_field):
    grid_field = jnp.roll(grid_field, 1, axis=0)
    upper_rows = shifted(grid_field[:, 3:], "lat", 1)
    grid_field = jnp.concatenate([upper_rows, grid_field[:, :3]], axis=1)
    prev_cols = shifted(grid_field[:, :, 18:], "lon", 1)
    return jnp.concatenate([prev_cols, grid_field[:, :, :18]], axis=2)


def per_device(
    tokens,
    lat_valid,
    gain_attn,
    w_qkv,
    w_proj,
    gain_mlp,
    w_up,
    w_down,
    bias_table,
    index_table,
    cotangent,
):
    levels, row_count, col_count, channels = tokens.shape
    lat_count = lax.axis_size("lat")
    last = (lax.axis_index("lat") == lat_count - 1).astype(jnp.int32).reshape(1)
    grad_scale = float(levels * row_count * col_count * lat_count * lax.axis_size("lon")) ** (-0.5)
    keep_rows = (lat_valid > 0)[None, :, None, None]
    inputs = jnp.where(keep_rows, tokens, jnp.zeros_like(tokens))
    upstream = jnp.where(keep_rows, cotangent, jnp.zeros_like(cotangent))
    both = into_shifted(jnp.concatenate([inputs, upstream], axis=-1))
    bias = bias_of(last, bias_table, index_table)
    upd, dtok, d_gains, d_qkv, d_proj, d_up, d_down_t, d_scores = block_pass(
        grad_scale,
        to_windows(both[..., :CH]),
        to_windows(both[..., CH:]),
        bias,
        gain_attn.reshape(1, CH),
        w_qkv,
        w_proj,
        gain_mlp.reshape(1, CH),
        w_up,
        w_down,
    )
    sums = table_sums(d_scores, index_table) * grad_scale
    sums = sums.reshape(HI, ROWS, 256).transpose(1, 0, 2).reshape(ROWS, HI * 256)[:, :ENTRIES]
    d_table = lax.psum(sums.reshape(ZONES, HEADS, ENTRIES).astype(BF16), "lon").astype(F32)
    back = from_shifted(
        from_windows(jnp.concatenate([upd, dtok], axis=-1), levels, row_count, col_count)
    )
    back = jnp.where(keep_rows, back, jnp.zeros_like(back))
    d_gains, d_qkv, d_proj, d_up, d_down_t = lax.psum(
        (d_gains, d_qkv, d_proj, d_up, d_down_t), ("lat", "lon")
    )
    return (
        back[..., :CH],
        back[..., CH:],
        d_gains[0],
        d_qkv,
        d_proj,
        d_gains[1],
        d_up,
        d_down_t.T,
        d_table,
    )


def solution(mesh):
    field = P(None, "lat", "lon", None)
    in_specs = (field, P("lat"), P(), P(), P(), P(), P(), P(), P("lat"), P(), field)
    out_specs = (field, field, P(), P(), P(), P(), P(), P(), P("lat"))
    return jax.shard_map(
        per_device, mesh=mesh, in_specs=in_specs, out_specs=out_specs, check_vma=False
    )
```

```python
import functools
import jax
import jax.numpy as jnp
from jax import lax
from jax.sharding import PartitionSpec as P
from jax.experimental import pallas as pl
from jax.experimental.pallas import tpu as pltpu

WIN_Z = 2
WIN_LAT = 6
WIN_LON = 12
PLACES = 144
HEADS = 6
WIDTH = 32
CH = 192
HIDDEN = 768
WINDOWS = 8
TOKENS = 1152
ZONES = 4
ROWS = ZONES * HEADS
ENTRIES = 3312
HI = 13
GROUPS = 18
SPAN = 1152
LOG2E = 1.4426950408889634
SCALE = 32**-0.5
NORM_EPS = 1e-05
F32 = jnp.float32
BF16 = jnp.bfloat16


def dot(left, right, left_dim=1, right_dim=0):
    return lax.dot_general(
        left, right, (((left_dim,), (right_dim,)), ((), ())), preferred_element_type=F32
    )


def entry_lanes(idx_ref, group):
    start = pl.multiple_of(group * 8, 8)
    main = idx_ref[pl.ds(start, 8), 0:128]
    rest = idx_ref[pl.ds(start, 8), 128:256].astype(F32)
    rest = pltpu.roll(rest, 0, 1, stride=16, stride_axis=0)
    place = lax.broadcasted_iota(jnp.int32, (8, 128), 0)
    lane = lax.broadcasted_iota(jnp.int32, (8, 128), 1)
    rest = jnp.sum(jnp.where(lane // 16 == place, rest, 0.0), axis=0, keepdims=True)
    rows = [main[i : i + 1] for i in range(8)] + [rest.astype(jnp.int32)]
    return jnp.concatenate(rows, axis=1)


def low_onehot(entries):
    low = jnp.broadcast_to(entries & 255, (256, SPAN))
    at = lax.broadcasted_iota(jnp.int32, (256, SPAN), 0)
    return jnp.where(low == at, 1.0, 0.0).astype(BF16)


def transposed_index(idx_in, idx_ref):
    idx_ref[:, 128:256] = jnp.zeros((PLACES, 128), jnp.int32)
    flipped = jnp.transpose(idx_in[...].astype(F32)).astype(jnp.int32)
    idx_ref[:, 0:PLACES] = flipped


def region_of(place, last_zone, last_band):
    depth = place // (WIN_LAT * WIN_LON)
    row = place // WIN_LON % WIN_LAT
    level = jnp.where(depth >= WIN_Z - WIN_Z // 2, 2, 1) * last_zone
    band = jnp.where(row >= WIN_LAT - WIN_LAT // 2, 2, 1) * last_band
    return 3 * level + band


def gather_bias(last_band, table_ref, idx_in, bias_ref, idx_ref, t2_ref):
    transposed_index(idx_in, idx_ref)
    for hi in range(HI):
        wide = min(256, ENTRIES - hi * 256)
        for zone in range(ZONES):
            part = table_ref[zone, :, hi * 256 : hi * 256 + wide] * LOG2E
            if wide < 256:
                part = jnp.concatenate([part, jnp.zeros((HEADS, 256 - wide), F32)], axis=1)
            t2_ref[hi * ROWS + zone * HEADS : hi * ROWS + (zone + 1) * HEADS, :] = part

    def step(group, carry):
        entries = entry_lanes(idx_ref, group)
        onehot = low_onehot(entries)
        found = dot(t2_ref[...].astype(BF16), onehot)
        high = jnp.broadcast_to(entries >> 8, (ROWS, SPAN))
        bias = jnp.where(high == 0, found[0:ROWS], 0.0)
        for hi in range(1, HI):
            bias = jnp.where(high == hi, found[hi * ROWS : (hi + 1) * ROWS], bias)
        lane = lax.broadcasted_iota(jnp.int32, (ROWS, 128), 1)
        zone3 = (lax.broadcasted_iota(jnp.int32, (ROWS, 128), 0) >= ROWS - HEADS).astype(jnp.int32)
        rest = bias[:, 1024:1152]
        for i in range(8):
            key = group * 8 + i
            key_region = region_of(jnp.full((ROWS, 128), key, jnp.int32), zone3, last_band)
            main_ok = region_of(lane, zone3, last_band) == key_region
            rest_ok = region_of((lane & 15) + 128, zone3, last_band) == key_region
            main_i = jnp.where(main_ok, bias[:, i * 128 : (i + 1) * 128], -1e30)
            rest_i = rest if i == 0 else pltpu.roll(rest, 128 - 16 * i, 1)
            rest_i = jnp.where(rest_ok, rest_i, -1e30)
            bias_ref[0, pl.ds(key, ROWS, stride=PLACES), :] = main_i
            bias_ref[1, pl.ds(key, ROWS, stride=PLACES), :] = rest_i
        return carry

    lax.fori_loop(0, GROUPS, step, 0)


def scatter_setup(idx_in, idx_ref, acc_ref):
    transposed_index(idx_in, idx_ref)
    acc_ref[...] = jnp.zeros_like(acc_ref)


def scatter_step(ds_ref, idx_ref, acc_ref, group, carry):
    entries = entry_lanes(idx_ref, group)
    onehot = low_onehot(entries)
    lane = lax.broadcasted_iota(jnp.int32, (ROWS, 128), 1)
    mains, rest = [], jnp.zeros((ROWS, 128), F32)
    for i in range(8):
        key = group * 8 + i
        mains.append(ds_ref[0, pl.ds(key, ROWS, stride=PLACES), :])
        rest_i = ds_ref[1, pl.ds(key, ROWS, stride=PLACES), :]
        if i:
            rest_i = pltpu.roll(rest_i, 16 * i, 1)
        rest = jnp.where(lane // 16 == i, rest_i, rest)
    grads = jnp.concatenate(mains + [rest], axis=1)
    high = jnp.broadcast_to(entries >> 8, (ROWS, SPAN))
    parts = [jnp.where(high == hi, grads, 0.0) for hi in range(HI)]
    left = jnp.concatenate(parts, axis=0).astype(BF16)
    acc_ref[...] += dot(left, onehot, 1, 1)
    return carry


def normed(values):
    center = values - jnp.mean(values, axis=-1, keepdims=True)
    rscale = lax.rsqrt(jnp.mean(center * center, axis=-1, keepdims=True) + NORM_EPS)
    return center * rscale, rscale


def norm_back(unit, rscale, gain, incoming):
    scaled = incoming * gain
    d_inputs = rscale * (
        scaled
        - jnp.mean(scaled, axis=-1, keepdims=True)
        - unit * jnp.mean(scaled * unit, axis=-1, keepdims=True)
    )
    return d_inputs, jnp.sum(incoming * unit, axis=0, keepdims=True)


def main_kernel(
    grad_scale,
    xw_ref,
    cw_ref,
    bias_ref,
    g1_ref,
    wqkv_ref,
    wproj_ref,
    g2_ref,
    wup_ref,
    wdown_ref,
    upd_ref,
    dtok_ref,
    dgain_ref,
    dqkv_ref,
    dproj_ref,
    dup_ref,
    ddown_ref,
    ds_ref,
    wqkvt_s,
    soft_s,
    trip_s,
    mrg_s,
    inv_s,
    first_s,
    resid_s,
    dres_s,
    dtrip_s,
):
    wqkvt_s[...] = jnp.transpose(wqkv_ref[...].astype(F32)).astype(BF16)
    g1 = g1_ref[...].astype(F32)
    g2 = g2_ref[...].astype(F32)

    def forward(w, carry):
        rows = pl.ds(pl.multiple_of(w * PLACES, PLACES), PLACES)
        x = xw_ref[rows, :].astype(F32)
        first = (normed(x)[0] * g1).astype(BF16)
        first_s[rows, :] = first
        triple = dot(wqkvt_s[...], first, 1, 1)
        trip_s[w, 0:CH] = (triple[0:CH] * (SCALE * LOG2E)).astype(BF16)
        trip_s[w, CH : 3 * CH] = triple[CH : 3 * CH].astype(BF16)
        zone = w // 2
        for h in range(HEADS):
            query = trip_s[w, h * WIDTH : (h + 1) * WIDTH]
            keys = trip_s[w, CH + h * WIDTH : CH + (h + 1) * WIDTH]
            values = trip_s[w, 2 * CH + h * WIDTH : 2 * CH + (h + 1) * WIDTH]
            at = pl.ds(pl.multiple_of((zone * HEADS + h) * PLACES, PLACES), PLACES)
            bias = jnp.concatenate([bias_ref[0, at, :], bias_ref[1, at, 0:16]], axis=1)
            scores = dot(keys, query, 0, 0) + bias
            weights = jnp.exp2(scores - jnp.max(scores, axis=0, keepdims=True))
            inv = 1.0 / jnp.sum(weights, axis=0, keepdims=True)
            weights = weights.astype(BF16)
            soft_s[w * HEADS + h] = weights
            inv_s[w, h : h + 1] = inv
            mrg_s[w, h * WIDTH : (h + 1) * WIDTH] = (dot(values, weights) * inv).astype(BF16)
        attended = dot(mrg_s[w], wproj_ref[...], 0, 0).astype(BF16).astype(F32)
        resid_s[rows, :] = (x + attended).astype(BF16)
        return carry

    lax.fori_loop(0, WINDOWS, forward, 0)

    dgain_ref[...] = jnp.zeros_like(dgain_ref)
    dqkv_ref[...] = jnp.zeros_like(dqkv_ref)
    dproj_ref[...] = jnp.zeros_like(dproj_ref)
    dup_ref[...] = jnp.zeros_like(dup_ref)
    ddown_ref[...] = jnp.zeros_like(ddown_ref)

    chunk = 384

    def feed_forward(c, carry):
        rows = pl.ds(pl.multiple_of(c * chunk, chunk), chunk)
        resid = resid_s[rows, :].astype(F32)
        up = cw_ref[rows, :]
        unit, rscale = normed(resid)
        second = unit * g2
        second_b = second.astype(BF16)
        pre = dot(second_b, wup_ref[...])
        c0, c1 = 0.7978845608028654, 0.7978845608028654 * 0.044715
        sq = pre * pre
        tanh = jnp.tanh(pre * (c0 + c1 * sq))
        half = 0.5 + 0.5 * tanh
        hidden = (pre * half).astype(BF16)
        slope = half + half * (1.0 - tanh) * pre * (c0 + (3.0 * c1) * sq)
        upd_ref[rows, :] = (resid + dot(hidden, wdown_ref[...])).astype(BF16)
        upt = jnp.transpose(up.astype(F32)).astype(BF16)
        ddown_ref[...] += dot(upt, hidden)
        d_pre = (slope * dot(up, wdown_ref[...], 1, 1)).astype(BF16)
        dup_ref[...] += dot(jnp.transpose(second).astype(BF16), d_pre)
        d_norm = dot(d_pre, wup_ref[...], 1, 1)
        d_in, d_gain = norm_back(unit, rscale, g2, d_norm)
        dres_s[rows, :] = d_in + up.astype(F32)
        dgain_ref[1:2] += d_gain
        return carry

    lax.fori_loop(0, TOKENS // chunk, feed_forward, 0)

    def backward(zone, carry):
        for side in range(2):
            w = zone * 2 + side
            rows = pl.ds(pl.multiple_of(w * PLACES, PLACES), PLACES)
            d_win = dres_s[rows, :].astype(BF16)
            dproj_ref[...] += dot(mrg_s[w], d_win)
            d_merged = dot(wproj_ref[...], d_win, 1, 1)
            for h in range(HEADS):
                at_q = slice(h * WIDTH, (h + 1) * WIDTH)
                at_k = slice(CH + h * WIDTH, CH + (h + 1) * WIDTH)
                at_v = slice(2 * CH + h * WIDTH, 2 * CH + (h + 1) * WIDTH)
                weights = soft_s[w * HEADS + h]
                inv = inv_s[w, h : h + 1]
                d_m = d_merged[h * WIDTH : (h + 1) * WIDTH] * inv
                lean = jnp.sum(d_m * mrg_s[w, at_q].astype(F32), axis=0, keepdims=True)
                d_mb = d_m.astype(BF16)
                d_chances = dot(trip_s[w, at_v], d_mb, 0, 0)
                d_scores = weights.astype(F32) * (d_chances - lean)
                at = pl.ds(pl.multiple_of((zone * HEADS + h) * PLACES, PLACES), PLACES)
                if side == 0:
                    ds_ref[0, at, :] = d_scores[:, 0:128]
                    ds_ref[1, at, 0:16] = d_scores[:, 128:PLACES]
                else:
                    ds_ref[0, at, :] += d_scores[:, 0:128]
                    ds_ref[1, at, 0:16] += d_scores[:, 128:PLACES]
                scaled = d_scores.astype(BF16)
                dtrip_s[at_q] = (dot(trip_s[w, at_k], scaled) * SCALE).astype(BF16)
                dtrip_s[at_k] = (dot(trip_s[w, at_q], scaled, 1, 1) * (1 / LOG2E)).astype(BF16)
                dtrip_s[at_v] = dot(d_mb, weights, 1, 1).astype(BF16)
            first_t = jnp.transpose(first_s[rows, :].astype(F32)).astype(BF16)
            d_triple = dtrip_s[...]
            dqkv_ref[...] += dot(first_t, d_triple, 1, 1)
            d_first = dot(d_triple, wqkvt_s[...], 0, 0).astype(BF16).astype(F32)
            unit, rscale = normed(xw_ref[rows, :].astype(F32))
            d_in, d_gain = norm_back(unit, rscale, g1, d_first)
            dtok_ref[rows, :] = (dres_s[rows, :] + d_in).astype(BF16)
            dgain_ref[0:1] += d_gain
        return carry

    lax.fori_loop(0, ZONES, backward, 0)
    for ref in (dgain_ref, dqkv_ref, dproj_ref, dup_ref, ddown_ref):
        ref[...] = ref[...] * grad_scale


VMEM_SPEC = pl.BlockSpec(memory_space=pltpu.VMEM)
LIMIT = 56 * 1024 * 1024


def vm(shape, dtype):
    return pltpu.VMEM(shape, dtype)


def block_pass(grad_scale, *args):
    sd = jax.ShapeDtypeStruct
    return pl.pallas_call(
        functools.partial(main_kernel, grad_scale),
        out_shape=[
            sd((TOKENS, CH), BF16),
            sd((TOKENS, CH), BF16),
            sd((8, CH), F32),
            sd((CH, 3 * CH), F32),
            sd((CH, CH), F32),
            sd((CH, HIDDEN), F32),
            sd((CH, HIDDEN), F32),
            sd((2, ROWS * PLACES, 128), F32),
        ],
        in_specs=[VMEM_SPEC] * 9,
        out_specs=[VMEM_SPEC] * 8,
        scratch_shapes=[
            vm((3 * CH, CH), BF16),
            vm((WINDOWS * HEADS, PLACES, PLACES), BF16),
            vm((WINDOWS, 3 * CH, PLACES), BF16),
            vm((WINDOWS, CH, PLACES), BF16),
            vm((WINDOWS, 8, PLACES), F32),
            vm((TOKENS, CH), BF16),
            vm((TOKENS, CH), BF16),
            vm((TOKENS, CH), F32),
            vm((3 * CH, PLACES), BF16),
        ],
        compiler_params=pltpu.CompilerParams(vmem_limit_bytes=LIMIT),
    )(*args)


MESH = pl.DeviceIdType.MESH
BAND_ROWS, SIDE_ROWS = 112, 48


def remote(src, dst, send, recv, device):
    return pltpu.make_async_remote_copy(
        src_ref=src, dst_ref=dst, send_sem=send, recv_sem=recv, device_id=device, device_id_type=MESH
    )


def places():
    lat, lon = lax.axis_index("lat"), lax.axis_index("lon")
    up, down = lax.rem(lat + 1, 16), lax.rem(lat + 15, 16)
    right, left = lax.rem(lon + 1, 8), lax.rem(lon + 7, 8)
    after = [(up, lon), (lat, right), (up, right)]
    before = [(down, lon), (lat, left), (down, left)]
    return after, before


def greet(devices):
    barrier = pltpu.get_barrier_semaphore()
    for device in devices:
        pl.semaphore_signal(barrier, inc=1, device_id=device, device_id_type=MESH)
    pl.semaphore_wait(barrier, len(devices))


def cut_pieces(fields, valid, win, band, side, corner):
    def zone_step(zone, carry):
        for f, field in enumerate(fields):
            for depth in range(2):
                level = lax.rem(2 * zone + depth + 1, 8)
                for i in range(6):
                    row = field[level, i].astype(F32) * valid[i]
                    if i < 3:
                        at = depth * 3 + i
                        band[f, zone, at * 18 : at * 18 + 18] = row[6:24]
                        corner[f, zone, at * 6 : at * 6 + 6] = row[0:6]
                    else:
                        at = depth * 3 + i - 3
                        side[f, zone, at * 6 : at * 6 + 6] = row[0:6]
                        at = (depth * 6 + i - 3) * 12
                        win[f, 2 * zone, at : at + 12] = row[6:18]
                        win[f, 2 * zone + 1, at : at + 6] = row[18:24]
        return carry

    lax.fori_loop(0, ZONES, zone_step, 0)


def add_pieces(win, band, side, corner):
    def zone_step(zone, carry):
        for f in range(2):
            band_v = band[f, zone].astype(F32)
            side_v = side[f, zone].astype(F32)
            corner_v = corner[f, zone].astype(F32)
            for depth in range(2):
                for i in range(3):
                    piece = depth * 3 + i
                    at = (depth * 6 + i) * 12
                    win[f, 2 * zone + 1, at + 6 : at + 12] = side_v[piece * 6 : piece * 6 + 6]
                    at = (depth * 6 + i + 3) * 12
                    win[f, 2 * zone, at : at + 12] = band_v[piece * 18 : piece * 18 + 12]
                    win[f, 2 * zone + 1, at : at + 6] = band_v[piece * 18 + 12 : piece * 18 + 18]
                    win[f, 2 * zone + 1, at + 6 : at + 12] = corner_v[piece * 6 : piece * 6 + 6]
        return carry

    lax.fori_loop(0, ZONES, zone_step, 0)


def cut_back(fields, grid, band, side, corner):
    def zone_step(zone, carry):
        for f, field in enumerate(fields):
            near = field[2 * zone].astype(F32)
            far = field[2 * zone + 1].astype(F32)
            for depth in range(2):
                level = lax.rem(2 * zone + depth + 1, 8)
                for i in range(6):
                    at = (depth * 6 + i) * 12
                    left, mid, right = near[at : at + 12], far[at : at + 6], far[at + 6 : at + 12]
                    if i < 3:
                        piece = depth * 3 + i
                        grid[f, level, i + 3, 6:18] = left
                        grid[f, level, i + 3, 18:24] = mid
                        side[f, zone, piece * 6 : piece * 6 + 6] = right
                    else:
                        piece = depth * 3 + i - 3
                        band[f, zone, piece * 18 : piece * 18 + 12] = left
                        band[f, zone, piece * 18 + 12 : piece * 18 + 18] = mid
                        corner[f, zone, piece * 6 : piece * 6 + 6] = right
        return carry

    lax.fori_loop(0, ZONES, zone_step, 0)


def add_back(grid, band, side, corner):
    def zone_step(zone, carry):
        for f in range(2):
            band_v = band[f, zone].astype(F32)
            side_v = side[f, zone].astype(F32)
            corner_v = corner[f, zone].astype(F32)
            for depth in range(2):
                level = lax.rem(2 * zone + depth + 1, 8)
                for i in range(3):
                    piece = depth * 3 + i
                    grid[f, level, i, 6:24] = band_v[piece * 18 : piece * 18 + 18]
                    grid[f, level, i, 0:6] = corner_v[piece * 6 : piece * 6 + 6]
                    grid[f, level, i + 3, 0:6] = side_v[piece * 6 : piece * 6 + 6]
        return carry

    lax.fori_loop(0, ZONES, zone_step, 0)


def piece_scratch():
    out = []
    for kind in (F32, BF16, BF16):
        for rows in (BAND_ROWS, SIDE_ROWS, SIDE_ROWS):
            out.append(vm((2, ZONES, rows, CH), kind))
    return out


def clear(refs):
    for ref in refs:
        ref[...] = jnp.zeros_like(ref)


def shift_in_kernel(
    valid_ref, tok_ref, cot_ref, table_ref, idx_in, xw_ref, cw_ref, bias_ref, idx_ref, t2_ref, win,
    band, side, corner, band_s, side_s, corner_s, band_r, side_r, corner_r, sems,
):
    after, before = places()
    clear((band, side, corner))
    valid = [valid_ref[i].astype(F32) for i in range(6)]
    cut_pieces((tok_ref, cot_ref), valid, win, band, side, corner)
    for source, target in ((band, band_s), (side, side_s), (corner, corner_s)):
        target[...] = source[...].astype(BF16)
    greet(after + before)
    pairs = ((band_s, band_r), (side_s, side_r), (corner_s, corner_r))
    copies = [
        remote(src, dst, sems.at[0, i], sems.at[1, i], before[i])
        for i, (src, dst) in enumerate(pairs)
    ]
    for copy in copies:
        copy.start()
    last_band = (lax.axis_index("lat") == 15).astype(jnp.int32)
    gather_bias(last_band, table_ref, idx_in, bias_ref, idx_ref, t2_ref)
    for copy in copies:
        copy.wait()
    add_pieces(win, band_r, side_r, corner_r)
    xw_ref[...] = win[0].reshape(TOKENS, CH).astype(BF16)
    cw_ref[...] = win[1].reshape(TOKENS, CH).astype(BF16)


def shift_in(valid, tokens, cotangent, table, index_table):
    sd = jax.ShapeDtypeStruct
    return pl.pallas_call(
        shift_in_kernel,
        out_shape=[
            sd((TOKENS, CH), BF16),
            sd((TOKENS, CH), BF16),
            sd((2, ROWS * PLACES, 128), F32),
        ],
        in_specs=[pl.BlockSpec(memory_space=pltpu.SMEM)] + [VMEM_SPEC] * 4,
        out_specs=[VMEM_SPEC] * 3,
        scratch_shapes=[
            vm((PLACES, 256), jnp.int32),
            vm((HI * ROWS, 256), F32),
            vm((2, WINDOWS, PLACES, CH), F32),
            *piece_scratch(),
            pltpu.SemaphoreType.DMA((2, 3)),
        ],
        compiler_params=pltpu.CompilerParams(
            vmem_limit_bytes=LIMIT, collective_id=0, has_side_effects=True
        ),
    )(valid, tokens, cotangent, table, index_table)


TILES = 224
HALF = 112
STREAMS = ((0, 4), (64, 3))


def reduce_kernel(
    grad_scale, valid_ref, upd_ref, dtok_ref, dgain_ref, dqkv_ref, dproj_ref, dup_ref, ddown_ref,
    ds_ref, idx_in,
    updo_ref, dtoko_ref, gain_ref, qkvo_ref, projo_ref, upo_ref, downo_ref, table_ref,
    idx_ref, acc_ref, grid, band, side, corner, band_s, side_s, corner_s, band_r, side_r, corner_r,
    part, core_r, first_r, second_r, depth_r, full, tab_s, tab_r, tab_full,
    halo_sems, core_sems, first_sems, second_sems, depth_sems, tab_sems,
):
    lat, lon = lax.axis_index("lat"), lax.axis_index("lon")
    core, x, z_lo = lat % 2, lat // 2 % 4, lat // 8
    y, z_hi = lon % 4, lon // 4
    z = z_hi * 2 + z_lo

    def device(core=core, x=x, y=y, z=z):
        return (z % 2 * 4 + x) * 2 + core, z // 2 * 4 + y

    sibling = device(core=1 - core)
    along_x = [device(x=lax.rem(x + d, 4)) for d in range(1, 4)]
    along_y = [device(y=lax.rem(y + d, 4)) for d in range(1, 4)]
    along_z = [device(z=lax.rem(z + d, 4)) for d in range(1, 4)]
    along_lon = [(lat, lax.rem(lon + d, 8)) for d in range(1, 8)]
    after, before = places()
    greet([sibling] + along_x + along_y + along_z + along_lon + after + before)

    def put(tile, value):
        part[tile : tile + 12] = value.astype(BF16).reshape(12, 16, 128)

    for i in range(6):
        put(12 * i, dup_ref[:, 128 * i : 128 * i + 128])
        put(72 + 12 * i, ddown_ref[:, 128 * i : 128 * i + 128])
    for i in range(4):
        put(144 + 12 * i, dqkv_ref[:, 128 * i : 128 * i + 128])
    put(192, jnp.concatenate([dqkv_ref[:, 512:576], dproj_ref[:, 0:64]], axis=1))
    put(204, dproj_ref[:, 64:192])
    gains = jnp.concatenate([dgain_ref[:, 128:192], jnp.zeros((8, 64), F32)], axis=1)
    part[216] = jnp.concatenate([dgain_ref[:, 0:128], gains], axis=0).astype(BF16)
    part[217:TILES] = jnp.zeros((TILES - 217, 16, 128), BF16)

    mine = core * HALF
    core_copy = remote(
        part.at[pl.ds((1 - core) * HALF, HALF)], core_r, core_sems.at[0], core_sems.at[1], sibling
    )
    core_copy.start()

    clear((band, side, corner))
    cut_back((upd_ref, dtok_ref), grid, band, side, corner)
    for source, target in ((band, band_s), (side, side_s), (corner, corner_s)):
        target[...] = source[...].astype(BF16)
    pairs = ((band_s, band_r), (side_s, side_r), (corner_s, corner_r))
    halo = [
        remote(src, dst, halo_sems.at[0, i], halo_sems.at[1, i], after[i])
        for i, (src, dst) in enumerate(pairs)
    ]

    core_copy.wait()
    half = pl.ds(mine, HALF)
    part[half] = (part[half].astype(F32) + core_r[...].astype(F32)).astype(BF16)

    orders = ((along_x, x, along_y, y), (along_y, y, along_x, x))

    def scatter_phase(level, received, sems, starts, counts):
        copies = []
        for s in range(2):
            partners, me = orders[s][2 * level], orders[s][2 * level + 1]
            for d in range(1, 4):
                there = lax.rem(me + d, 4)
                source = part.at[pl.ds(starts[s] + there * counts[s], counts[s])]
                target = received[s].at[d - 1]
                copy = remote(
                    source, target, sems.at[0, s, d - 1], sems.at[1, s, d - 1], partners[d - 1]
                )
                copy.start()
                copies.append(copy)
        return copies

    def sum_phase(level, received, starts, counts):
        out = []
        for s in range(2):
            at = starts[s] + orders[s][2 * level + 1] * counts[s]
            own = pl.ds(at, counts[s])
            total = part[own].astype(F32)
            for d in range(3):
                total += received[s][d].astype(F32)
            part[own] = total.astype(BF16)
            out.append(at)
        return out

    starts = [mine + STREAMS[s][0] for s in range(2)]
    wide = [4 * STREAMS[s][1] for s in range(2)]
    narrow = [STREAMS[s][1] for s in range(2)]
    copies = scatter_phase(0, first_r, first_sems, starts, wide)
    for copy in halo:
        copy.start()

    scatter_setup(idx_in, idx_ref, acc_ref)
    lax.fori_loop(0, 9, functools.partial(scatter_step, ds_ref, idx_ref, acc_ref), 0)

    for copy in copies:
        copy.wait()
    starts1 = sum_phase(0, first_r, starts, wide)
    copies = scatter_phase(1, second_r, second_sems, starts1, narrow)

    lax.fori_loop(9, GROUPS, functools.partial(scatter_step, ds_ref, idx_ref, acc_ref), 0)
    tab_s[...] = jnp.zeros_like(tab_s)
    for hi in range(0, HI, 2):
        rows = min(48, (HI - hi) * ROWS)
        tab_s[hi // 2, 0:rows] = (acc_ref[hi * ROWS : hi * ROWS + rows] * grad_scale).astype(BF16)
    tab_copies = []
    for d in range(1, 8):
        copy = remote(
            tab_s.at[lax.rem(lon + d, 8)],
            tab_r.at[d - 1],
            tab_sems.at[0, d - 1],
            tab_sems.at[1, d - 1],
            along_lon[d - 1],
        )
        copy.start()
        tab_copies.append(copy)

    for copy in copies:
        copy.wait()
    starts2 = sum_phase(1, second_r, starts1, narrow)

    copies = []
    for s in range(2):
        depth_r[s][pl.ds(z, 1)] = part[pl.ds(starts2[s], narrow[s])][None]
    for s in range(2):
        for d in range(1, 4):
            copy = remote(
                part.at[pl.ds(starts2[s], narrow[s])],
                depth_r[s].at[z],
                depth_sems.at[0, s, d - 1],
                depth_sems.at[1, s, d - 1],
                along_z[d - 1],
            )
            copy.start()
            copies.append(copy)
    for copy in tab_copies:
        copy.wait()
    total = tab_s[lon].astype(F32)
    for d in range(7):
        total += tab_r[d].astype(F32)
    tab_full[lon] = total.astype(BF16)
    tab_copies = []
    for d in range(1, 8):
        copy = remote(
            tab_full.at[lon],
            tab_full.at[lon],
            tab_sems.at[2, d - 1],
            tab_sems.at[3, d - 1],
            along_lon[d - 1],
        )
        copy.start()
        tab_copies.append(copy)
    for copy in copies:
        copy.wait()
    for s in range(2):
        total = depth_r[s][0].astype(F32)
        for d in range(1, 4):
            total += depth_r[s][d].astype(F32)
        full[pl.ds(starts2[s], narrow[s])] = total.astype(BF16)

    def gather_phase(level, sems, begin, counts):
        copies = []
        for s in range(2):
            partners = orders[s][2 * level]
            for d in range(1, 4):
                region = full.at[pl.ds(begin[s], counts[s])]
                copy = remote(
                    region, region, sems.at[2, s, d - 1], sems.at[3, s, d - 1], partners[d - 1]
                )
                copy.start()
                copies.append(copy)
        return copies

    copies = gather_phase(1, second_sems, starts2, narrow)
    for copy in halo:
        copy.wait()
    add_back(grid, band_r, side_r, corner_r)
    for copy in copies:
        copy.wait()
    copies = gather_phase(0, first_sems, starts1, wide)
    for i in range(6):
        valid = valid_ref[i].astype(F32)
        updo_ref[:, i] = (grid[0, :, i] * valid).astype(BF16)
        dtoko_ref[:, i] = (grid[1, :, i] * valid).astype(BF16)
    for copy in copies:
        copy.wait()
    region = full.at[pl.ds(mine, HALF)]
    core_copy = remote(region, region, core_sems.at[2], core_sems.at[3], sibling)
    core_copy.start()
    for copy in tab_copies:
        copy.wait()
    for hi in range(HI):
        wide_hi = min(256, ENTRIES - hi * 256)
        block = tab_full[hi // 2].astype(F32)[hi % 2 * ROWS : (hi % 2 + 1) * ROWS]
        for zone in range(ZONES):
            table_ref[zone, :, hi * 256 : hi * 256 + wide_hi] = block[
                zone * HEADS : (zone + 1) * HEADS, 0:wide_hi
            ]
    core_copy.wait()

    def get(tile):
        return full[tile : tile + 12].reshape(192, 128).astype(F32)

    for i in range(6):
        upo_ref[:, 128 * i : 128 * i + 128] = get(12 * i)
        downo_ref[128 * i : 128 * i + 128, :] = jnp.transpose(get(72 + 12 * i))
    for i in range(4):
        qkvo_ref[:, 128 * i : 128 * i + 128] = get(144 + 12 * i)
    mixed = get(192)
    qkvo_ref[:, 512:576] = mixed[:, 0:64]
    projo_ref[...] = jnp.concatenate([mixed[:, 64:128], get(204)], axis=1)
    gains = full[216].astype(F32)
    gain_ref[...] = jnp.concatenate([gains[0:8], gains[8:16, 0:64]], axis=1)


def reduce_all(grad_scale, *args):
    sd = jax.ShapeDtypeStruct
    sem = pltpu.SemaphoreType.DMA
    return pl.pallas_call(
        functools.partial(reduce_kernel, grad_scale),
        out_shape=[
            sd((8, 6, 24, CH), BF16),
            sd((8, 6, 24, CH), BF16),
            sd((8, CH), F32),
            sd((CH, 3 * CH), F32),
            sd((CH, CH), F32),
            sd((CH, HIDDEN), F32),
            sd((HIDDEN, CH), F32),
            sd((ZONES, HEADS, ENTRIES), F32),
        ],
        in_specs=[pl.BlockSpec(memory_space=pltpu.SMEM)] + [VMEM_SPEC] * 9,
        out_specs=[VMEM_SPEC] * 8,
        scratch_shapes=[
            vm((PLACES, 256), jnp.int32),
            vm((HI * ROWS, 256), F32),
            vm((2, 8, 6, 24, CH), F32),
            *piece_scratch(),
            vm((TILES, 16, 128), BF16),
            vm((HALF, 16, 128), BF16),
            [vm((3, 4 * n, 16, 128), BF16) for _, n in STREAMS],
            [vm((3, n, 16, 128), BF16) for _, n in STREAMS],
            [vm((4, n, 16, 128), BF16) for _, n in STREAMS],
            vm((TILES, 16, 128), BF16),
            vm((8, 48, 256), BF16),
            vm((7, 48, 256), BF16),
            vm((8, 48, 256), BF16),
            sem((2, 3)),
            sem((4,)),
            sem((4, 2, 3)),
            sem((4, 2, 3)),
            sem((2, 2, 3)),
            sem((4, 7)),
        ],
        compiler_params=pltpu.CompilerParams(
            vmem_limit_bytes=LIMIT, collective_id=1, has_side_effects=True
        ),
    )(*args)


def per_device(
    tokens,
    lat_valid,
    gain_attn,
    w_qkv,
    w_proj,
    gain_mlp,
    w_up,
    w_down,
    bias_table,
    index_table,
    cotangent,
):
    levels, row_count, col_count, channels = tokens.shape
    grad_scale = float(levels * row_count * col_count * 128) ** (-0.5)
    xw, cw, bias = shift_in(lat_valid, tokens, cotangent, bias_table, index_table)
    upd, dtok, d_gains, d_qkv, d_proj, d_up, d_down_t, d_scores = block_pass(
        grad_scale,
        xw,
        cw,
        bias,
        gain_attn.reshape(1, CH),
        w_qkv,
        w_proj,
        gain_mlp.reshape(1, CH),
        w_up,
        w_down,
    )
    updated, d_tokens, d_gains, d_qkv, d_proj, d_up, d_down, d_table = reduce_all(
        grad_scale,
        lat_valid,
        upd.reshape(WINDOWS, PLACES, CH),
        dtok.reshape(WINDOWS, PLACES, CH),
        d_gains,
        d_qkv,
        d_proj,
        d_up,
        d_down_t,
        d_scores,
        index_table,
    )
    return updated, d_tokens, d_gains[0], d_qkv, d_proj, d_gains[1], d_up, d_down, d_table


def solution(mesh):
    field = P(None, "lat", "lon", None)
    in_specs = (field, P("lat"), P(), P(), P(), P(), P(), P(), P("lat"), P(), field)
    out_specs = (field, field, P(), P(), P(), P(), P(), P(), P("lat"))
    return jax.shard_map(
        per_device, mesh=mesh, in_specs=in_specs, out_specs=out_specs, check_vma=False
    )
```

```python
import functools
import jax
import jax.numpy as jnp
from jax import lax
from jax.sharding import PartitionSpec as P
from jax.experimental import pallas as pl
from jax.experimental.pallas import tpu as pltpu

WIN_Z = 2
WIN_LAT = 6
WIN_LON = 12
PLACES = 144
HEADS = 6
WIDTH = 32
CH = 192
HIDDEN = 768
WINDOWS = 8
TOKENS = 1152
ZONES = 4
ROWS = ZONES * HEADS
ENTRIES = 3312
HI = 13
PAIRS = 7
GROUPS = 18
SPAN = 1152
LOG2E = 1.4426950408889634
SCALE = 32**-0.5
NORM_EPS = 1e-05
F32 = jnp.float32
BF16 = jnp.bfloat16


def dot(left, right, left_dim=1, right_dim=0):
    return lax.dot_general(
        left, right, (((left_dim,), (right_dim,)), ((), ())), preferred_element_type=F32
    )


def entry_lanes(idx_ref, group):
    start = pl.multiple_of(group * 8, 8)
    main = idx_ref[pl.ds(start, 8), 0:128]
    rest = idx_ref[pl.ds(start, 8), 128:256].astype(F32)
    rest = pltpu.roll(rest, 0, 1, stride=16, stride_axis=0)
    place = lax.broadcasted_iota(jnp.int32, (8, 128), 0)
    lane = lax.broadcasted_iota(jnp.int32, (8, 128), 1)
    rest = jnp.sum(jnp.where(lane // 16 == place, rest, 0.0), axis=0, keepdims=True)
    rows = [main[i : i + 1] for i in range(8)] + [rest.astype(jnp.int32)]
    return jnp.concatenate(rows, axis=1)


def low_onehot(entries):
    low = jnp.broadcast_to((entries & 255).astype(F32).astype(BF16), (256, SPAN))
    at = lax.broadcasted_iota(jnp.int32, (256, SPAN), 0).astype(F32).astype(BF16)
    return jnp.where(low == at, jnp.ones((), BF16), jnp.zeros((), BF16))


def transposed_index(idx_in, idx_ref):
    idx_ref[:, 128:256] = jnp.zeros((PLACES, 128), jnp.int32)
    idx_ref[:, 0:PLACES] = jnp.transpose(idx_in[...].astype(F32)).astype(jnp.int32)


def region_of(place, last_zone, last_band):
    depth = place // (WIN_LAT * WIN_LON)
    row = place // WIN_LON % WIN_LAT
    level = jnp.where(depth >= WIN_Z - WIN_Z // 2, 2, 1) * last_zone
    band = jnp.where(row >= WIN_LAT - WIN_LAT // 2, 2, 1) * last_band
    return 3 * level + band


def gather_bias(table_ref, idx_in, bias_ref, idx_ref, t2_ref, hot_ref):
    last_band = (lax.axis_index("lat") == 15).astype(jnp.int32)
    transposed_index(idx_in, idx_ref)
    for hi in range(HI):
        wide = min(256, ENTRIES - hi * 256)
        for head in range(HEADS):
            part = table_ref[head, :, hi * 256 : hi * 256 + wide] * LOG2E
            if wide < 256:
                part = jnp.concatenate([part, jnp.zeros((ZONES, 256 - wide), F32)], axis=1)
            t2_ref[hi * ROWS + head * ZONES : hi * ROWS + (head + 1) * ZONES, :] = part

    def step(group, carry):
        entries = entry_lanes(idx_ref, group)
        onehot = low_onehot(entries)
        hot_ref[group] = onehot
        found = dot(t2_ref[...].astype(BF16), onehot)
        high = jnp.broadcast_to(entries >> 8, (ROWS, SPAN))
        bias = jnp.where(high == 0, found[0:ROWS], 0.0)
        for hi in range(1, HI):
            bias = jnp.where(high == hi, found[hi * ROWS : (hi + 1) * ROWS], bias)
        lane = lax.broadcasted_iota(jnp.int32, (ROWS, 128), 1)
        zone3 = (lax.broadcasted_iota(jnp.int32, (ROWS, 128), 0) % ZONES == ZONES - 1).astype(
            jnp.int32
        )
        main_region = region_of(lane, zone3, last_band)
        rest_region = region_of((lane & 15) + 128, zone3, last_band)
        rest = bias[:, 1024:1152]
        for i in range(8):
            key = group * 8 + i
            key_region = region_of(jnp.full((ROWS, 128), key, jnp.int32), zone3, last_band)
            main_i = jnp.where(
                main_region == key_region, bias[:, i * 128 : (i + 1) * 128], -1e30
            )
            rest_i = rest if i == 0 else pltpu.roll(rest, 128 - 16 * i, 1)
            rest_i = jnp.where(rest_region == key_region, rest_i, -1e30)
            bias_ref[0, pl.ds(key, ROWS, stride=PLACES), :] = main_i
            bias_ref[1, pl.ds(key, ROWS, stride=PLACES), :] = rest_i
        return carry

    lax.fori_loop(0, GROUPS, step, 0)


def scatter_step(ds_ref, idx_ref, hot_ref, acc_ref, group, carry):
    entries = entry_lanes(idx_ref, group)
    lane = lax.broadcasted_iota(jnp.int32, (ROWS, 128), 1)
    mains, rest = [], jnp.zeros((ROWS, 128), F32)
    for i in range(8):
        key = group * 8 + i
        mains.append(ds_ref[0, pl.ds(key, ROWS, stride=PLACES), :])
        rest_i = ds_ref[1, pl.ds(key, ROWS, stride=PLACES), :]
        if i:
            rest_i = pltpu.roll(rest_i, 16 * i, 1)
        rest = jnp.where(lane // 16 == i, rest_i, rest)
    grads = jnp.concatenate(mains + [rest], axis=1)
    grads = jnp.concatenate([grads, grads], axis=0).astype(BF16)
    high = jnp.broadcast_to((entries >> 8).astype(F32), (ROWS, SPAN))
    high = jnp.concatenate([high, high - 1.0], axis=0).astype(BF16)
    zero = jnp.zeros((), BF16)
    parts = [jnp.where(high == jnp.full((), 2 * i, BF16), grads, zero) for i in range(PAIRS)]
    acc_ref[...] += dot(jnp.concatenate(parts, axis=0), hot_ref[group], 1, 1)
    return carry


def normed(values):
    center = values - jnp.mean(values, axis=-1, keepdims=True)
    rscale = lax.rsqrt(jnp.mean(center * center, axis=-1, keepdims=True) + NORM_EPS)
    return center * rscale, rscale


def norm_back(unit, rscale, gain, incoming):
    scaled = incoming * gain
    d_inputs = rscale * (
        scaled
        - jnp.mean(scaled, axis=-1, keepdims=True)
        - unit * jnp.mean(scaled * unit, axis=-1, keepdims=True)
    )
    return d_inputs, jnp.sum(incoming * unit, axis=0, keepdims=True)


VMEM_SPEC = pl.BlockSpec(memory_space=pltpu.VMEM)
LIMIT = 60 * 1024 * 1024


def vm(shape, dtype):
    return pltpu.VMEM(shape, dtype)


MESH = pl.DeviceIdType.MESH
BAND_ROWS, SIDE_ROWS = 112, 48


def remote(src, dst, send, recv, device):
    return pltpu.make_async_remote_copy(
        src_ref=src, dst_ref=dst, send_sem=send, recv_sem=recv, device_id=device, device_id_type=MESH
    )


def places():
    lat, lon = lax.axis_index("lat"), lax.axis_index("lon")
    up, down = lax.rem(lat + 1, 16), lax.rem(lat + 15, 16)
    right, left = lax.rem(lon + 1, 8), lax.rem(lon + 7, 8)
    after = [(up, lon), (lat, right), (up, right)]
    before = [(down, lon), (lat, left), (down, left)]
    return after, before


def cut_pieces(fields, valid, win, band, side, corner):
    def zone_step(zone, carry):
        for f, field in enumerate(fields):
            for depth in range(2):
                level = lax.rem(2 * zone + depth + 1, 8)
                for i in range(6):
                    row = field[level, i].astype(F32) * valid[i]
                    if i < 3:
                        at = depth * 3 + i
                        band[f, zone, at * 18 : at * 18 + 18] = row[6:24]
                        corner[f, zone, at * 6 : at * 6 + 6] = row[0:6]
                    else:
                        at = depth * 3 + i - 3
                        side[f, zone, at * 6 : at * 6 + 6] = row[0:6]
                        at = (depth * 6 + i - 3) * 12
                        win[f, 2 * zone, at : at + 12] = row[6:18]
                        win[f, 2 * zone + 1, at : at + 6] = row[18:24]
        return carry

    lax.fori_loop(0, ZONES, zone_step, 0)


def add_pieces(win, band, side, corner):
    def zone_step(zone, carry):
        for f in range(2):
            band_v = band[f, zone].astype(F32)
            side_v = side[f, zone].astype(F32)
            corner_v = corner[f, zone].astype(F32)
            for depth in range(2):
                for i in range(3):
                    piece = depth * 3 + i
                    at = (depth * 6 + i) * 12
                    win[f, 2 * zone + 1, at + 6 : at + 12] = side_v[piece * 6 : piece * 6 + 6]
                    at = (depth * 6 + i + 3) * 12
                    win[f, 2 * zone, at : at + 12] = band_v[piece * 18 : piece * 18 + 12]
                    win[f, 2 * zone + 1, at : at + 6] = band_v[piece * 18 + 12 : piece * 18 + 18]
                    win[f, 2 * zone + 1, at + 6 : at + 12] = corner_v[piece * 6 : piece * 6 + 6]
        return carry

    lax.fori_loop(0, ZONES, zone_step, 0)


def cut_back(field, f, grid, band, side, corner):
    def zone_step(zone, carry):
        near = field[2 * zone]
        far = field[2 * zone + 1]
        for depth in range(2):
            level = lax.rem(2 * zone + depth + 1, 8)
            for i in range(6):
                at = (depth * 6 + i) * 12
                left, mid, right = near[at : at + 12], far[at : at + 6], far[at + 6 : at + 12]
                if i < 3:
                    piece = depth * 3 + i
                    grid[f, level, i + 3, 6:18] = left
                    grid[f, level, i + 3, 18:24] = mid
                    side[f, zone, piece * 6 : piece * 6 + 6] = right
                else:
                    piece = depth * 3 + i - 3
                    band[f, zone, piece * 18 : piece * 18 + 12] = left
                    band[f, zone, piece * 18 + 12 : piece * 18 + 18] = mid
                    corner[f, zone, piece * 6 : piece * 6 + 6] = right
        return carry

    lax.fori_loop(0, ZONES, zone_step, 0)


def add_back(grid, band, side, corner):
    def zone_step(zone, carry):
        for f in range(2):
            band_v = band[f, zone].astype(F32)
            side_v = side[f, zone].astype(F32)
            corner_v = corner[f, zone].astype(F32)
            for depth in range(2):
                level = lax.rem(2 * zone + depth + 1, 8)
                for i in range(3):
                    piece = depth * 3 + i
                    grid[f, level, i, 6:24] = band_v[piece * 18 : piece * 18 + 18]
                    grid[f, level, i, 0:6] = corner_v[piece * 6 : piece * 6 + 6]
                    grid[f, level, i + 3, 0:6] = side_v[piece * 6 : piece * 6 + 6]
        return carry

    lax.fori_loop(0, ZONES, zone_step, 0)


def piece_scratch():
    out = []
    for kind in (F32, BF16, BF16, BF16, BF16):
        for rows in (BAND_ROWS, SIDE_ROWS, SIDE_ROWS):
            out.append(vm((2, ZONES, rows, CH), kind))
    return out


TILES = 224
EARLY = (0, 64, ((0, 2), (32, 2)))
LATE = (128, 48, ((0, 2), (32, 1)))


class AllReduce:
    def __init__(self, plan, part, full, spot, bufs):
        self.base, self.half, self.streams = plan
        self.part, self.full, self.spot = part, full, spot
        self.core_r, self.first_r, self.second_r, self.depth_r = bufs[:4]
        self.core_sems, self.first_sems, self.second_sems, self.depth_sems = bufs[4:]
        self.mine = self.base + spot.core * self.half
        axes = ((spot.along_x, spot.x), (spot.along_y, spot.y))
        self.orders = (axes, axes[::-1])
        self.starts = [[self.mine + first for first, _ in self.streams]]
        self.counts = [[4 * n for _, n in self.streams], [n for _, n in self.streams]]
        for level in range(2):
            self.starts.append(
                [
                    self.starts[level][s] + self.orders[s][level][1] * self.counts[level][s]
                    for s in range(2)
                ]
            )

    def core_copy(self):
        other = self.base + (1 - self.spot.core) * self.half
        source = self.part.at[pl.ds(other, self.half)]
        return remote(
            source, self.core_r, self.core_sems.at[0], self.core_sems.at[1], self.spot.sibling
        )

    def core_back(self):
        region = self.full.at[pl.ds(self.mine, self.half)]
        return remote(
            region, region, self.core_sems.at[2], self.core_sems.at[3], self.spot.sibling
        )

    def level(self, level):
        return (self.first_r, self.first_sems) if level == 0 else (self.second_r, self.second_sems)

    def scatter(self, level):
        received, sems = self.level(level)
        copies = []
        for s in range(2):
            partners, me = self.orders[s][level]
            count = self.counts[level][s]
            for d in range(3):
                at = self.starts[level][s] + lax.rem(me + d + 1, 4) * count
                source = self.part.at[pl.ds(at, count)]
                copies.append(
                    remote(
                        source, received[s].at[d], sems.at[0, s, d], sems.at[1, s, d], partners[d]
                    )
                )
        return copies

    def gather(self, level):
        _, sems = self.level(level)
        copies = []
        for s in range(2):
            region = self.full.at[pl.ds(self.starts[level + 1][s], self.counts[level][s])]
            for d in range(3):
                partner = self.orders[s][level][0][d]
                copies.append(
                    remote(region, region, sems.at[2, s, d], sems.at[3, s, d], partner)
                )
        return copies

    def depth(self):
        copies = []
        for s in range(2):
            source = self.part.at[pl.ds(self.starts[2][s], self.counts[1][s])]
            target = self.depth_r[s].at[self.spot.z]
            for d in range(3):
                sems = self.depth_sems
                copies.append(
                    remote(source, target, sems.at[0, s, d], sems.at[1, s, d], self.spot.along_z[d])
                )
        return copies

    def add(self, level):
        received, _ = self.level(level)
        for s in range(2):
            own = pl.ds(self.starts[level + 1][s], self.counts[level][s])
            total = self.part[own].astype(F32)
            for d in range(3):
                total += received[s][d].astype(F32)
            self.part[own] = total.astype(BF16)

    def step(self, number):
        if number == 0:
            self.core_copy().start()
        elif number == 1:
            self.core_copy().wait()
            own = pl.ds(self.mine, self.half)
            total = self.part[own].astype(F32) + self.core_r[...].astype(F32)
            self.part[own] = total.astype(BF16)
            start(self.scatter(0))
        elif number == 2:
            finish(self.scatter(0))
            self.add(0)
            start(self.scatter(1))
        elif number == 3:
            finish(self.scatter(1))
            self.add(1)
            for s in range(2):
                own = pl.ds(self.starts[2][s], self.counts[1][s])
                self.depth_r[s][pl.ds(self.spot.z, 1)] = self.part[own][None]
            start(self.depth())
        elif number == 4:
            finish(self.depth())
            for s in range(2):
                total = self.depth_r[s][0].astype(F32)
                for d in range(1, 4):
                    total += self.depth_r[s][d].astype(F32)
                self.full[pl.ds(self.starts[2][s], self.counts[1][s])] = total.astype(BF16)
            start(self.gather(1))
        elif number == 5:
            finish(self.gather(1))
            start(self.gather(0))
        elif number == 6:
            finish(self.gather(0))
            self.core_back().start()
        else:
            self.core_back().wait()


def all_reduce_scratch(plan):
    _, half, streams = plan
    sem = pltpu.SemaphoreType.DMA
    return [
        vm((half, 16, 128), BF16),
        [vm((3, 4 * n, 16, 128), BF16) for _, n in streams],
        [vm((3, n, 16, 128), BF16) for _, n in streams],
        [vm((4, n, 16, 128), BF16) for _, n in streams],
        sem((4,)),
        sem((4, 2, 3)),
        sem((4, 2, 3)),
        sem((2, 2, 3)),
    ]


def start(copies):
    for copy in copies:
        copy.start()


def finish(copies):
    for copy in copies:
        copy.wait()


class Spot:
    def __init__(self):
        lat, lon = lax.axis_index("lat"), lax.axis_index("lon")
        self.lat, self.lon = lat, lon
        self.core, self.x, z_lo = lat % 2, lat // 2 % 4, lat // 8
        self.y, z_hi = lon % 4, lon // 4
        self.z = z_hi * 2 + z_lo
        self.sibling = self.device(core=1 - self.core)
        self.along_x = [self.device(x=lax.rem(self.x + d, 4)) for d in range(1, 4)]
        self.along_y = [self.device(y=lax.rem(self.y + d, 4)) for d in range(1, 4)]
        self.along_z = [self.device(z=lax.rem(self.z + d, 4)) for d in range(1, 4)]
        self.along_lon = [(lat, lax.rem(lon + d, 8)) for d in range(1, 8)]
        self.after, self.before = places()
        self.all = [self.sibling] + self.along_x + self.along_y + self.along_z
        self.all += self.along_lon + self.after + self.before

    def device(self, core=None, x=None, y=None, z=None):
        core = self.core if core is None else core
        x = self.x if x is None else x
        y = self.y if y is None else y
        z = self.z if z is None else z
        return (z % 2 * 4 + x) * 2 + core, z // 2 * 4 + y


def put(part, tile, value):
    part[tile : tile + 12] = value.astype(BF16).reshape(12, 16, 128)


def block_kernel(
    grad_scale, valid_ref, tok_ref, cot_ref, table_ref, idx_in, g1_ref, wqkv_ref, wproj_ref,
    g2_ref, wup_ref, wdown_ref,
    updo_ref, dtoko_ref, full_ref, tab_ref,
    idx_ref, t2_ref, hot_ref, bias_ref, ds_ref, acc_ref, win, grid,
    band, side, corner, band_s, side_s, corner_s, band_r, side_r, corner_r,
    band_s2, side_s2, corner_s2, band_r2, side_r2, corner_r2,
    wqkvt_s, soft_s, trip_s, mrg_s, inv_s, first_s, resid_s, dres_s, dtrip_s, upd_s, dtok_s,
    dgain_s, dqkv_s, dproj_s, dup_s, ddown_s,
    part, full, early_bufs, late_bufs, tab_s, tab_r, tab_full, halo_sems, back_sems, tab_sems,
):
    spot = Spot()
    barrier = pltpu.get_barrier_semaphore()
    for device in spot.all:
        pl.semaphore_signal(barrier, inc=1, device_id=device, device_id_type=MESH)
    valid = [valid_ref[i].astype(F32) for i in range(6)]
    cut_pieces((tok_ref, cot_ref), valid, win, band, side, corner)
    for source, target in ((band, band_s), (side, side_s), (corner, corner_s)):
        target[...] = source[...].astype(BF16)
    pl.semaphore_wait(barrier, len(spot.all))
    pairs = ((band_s, band_r), (side_s, side_r), (corner_s, corner_r))
    halo = [
        remote(src, dst, halo_sems.at[0, i], halo_sems.at[1, i], spot.before[i])
        for i, (src, dst) in enumerate(pairs)
    ]
    start(halo)
    gather_bias(table_ref, idx_in, bias_ref, idx_ref, t2_ref, hot_ref)
    wqkvt_s[...] = jnp.transpose(wqkv_ref[...].astype(F32)).astype(BF16)
    g1 = g1_ref[...].astype(F32).reshape(1, CH)
    g2 = g2_ref[...].astype(F32).reshape(1, CH)
    for ref in (dgain_s, dqkv_s, dproj_s, dup_s, ddown_s, acc_ref, ds_ref):
        ref[...] = jnp.zeros_like(ref)
    finish(halo)
    add_pieces(win, band_r, side_r, corner_r)

    def forward(w, carry):
        x = win[0, w]
        first = (normed(x)[0] * g1).astype(BF16)
        first_s[w] = first
        triple = dot(wqkvt_s[...], first, 1, 1)
        trip_s[w, 0:CH] = (triple[0:CH] * (SCALE * LOG2E)).astype(BF16)
        trip_s[w, CH : 3 * CH] = triple[CH : 3 * CH].astype(BF16)
        zone = w // 2
        for h in range(HEADS):
            query = trip_s[w, h * WIDTH : (h + 1) * WIDTH]
            keys = trip_s[w, CH + h * WIDTH : CH + (h + 1) * WIDTH]
            values = trip_s[w, 2 * CH + h * WIDTH : 2 * CH + (h + 1) * WIDTH]
            at = pl.ds(pl.multiple_of((h * ZONES + zone) * PLACES, PLACES), PLACES)
            bias = jnp.concatenate([bias_ref[0, at, :], bias_ref[1, at, 0:16]], axis=1)
            scores = dot(keys, query, 0, 0) + bias
            weights = jnp.exp2(scores - jnp.max(scores, axis=0, keepdims=True))
            inv = 1.0 / jnp.sum(weights, axis=0, keepdims=True)
            weights = weights.astype(BF16)
            soft_s[w * HEADS + h] = weights
            inv_s[w, h : h + 1] = inv
            mrg_s[w, h * WIDTH : (h + 1) * WIDTH] = (dot(values, weights) * inv).astype(BF16)
        attended = dot(mrg_s[w], wproj_ref[...], 0, 0).astype(BF16).astype(F32)
        resid_s[w] = (x + attended).astype(BF16)
        return carry

    lax.fori_loop(0, WINDOWS, forward, 0)

    many = 4
    chunk = many * PLACES

    def feed_forward(c, carry):
        here = pl.ds(c * many, many)
        resid = resid_s[here].reshape(chunk, CH).astype(F32)
        up_f = win[1, here].reshape(chunk, CH)
        up = up_f.astype(BF16)
        unit, rscale = normed(resid)
        second = unit * g2
        pre = dot(second.astype(BF16), wup_ref[...])
        c0, c1 = 0.7978845608028654, 0.7978845608028654 * 0.044715
        sq = pre * pre
        tanh = jnp.tanh(pre * (c0 + c1 * sq))
        half = 0.5 + 0.5 * tanh
        hidden = (pre * half).astype(BF16)
        slope = half + half * (1.0 - tanh) * pre * (c0 + (3.0 * c1) * sq)
        upd_s[here] = (resid + dot(hidden, wdown_ref[...], 1, 1)).reshape(many, PLACES, CH)
        ddown_s[...] += dot(jnp.transpose(up_f).astype(BF16), hidden)
        d_pre = (slope * dot(up, wdown_ref[...])).astype(BF16)
        dup_s[...] += dot(jnp.transpose(second).astype(BF16), d_pre)
        d_norm = dot(d_pre, wup_ref[...], 1, 1)
        d_in, d_gain = norm_back(unit, rscale, g2, d_norm)
        dres_s[here] = (d_in + up_f).reshape(many, PLACES, CH)
        dgain_s[1:2] += d_gain
        return carry

    lax.fori_loop(0, WINDOWS // many, feed_forward, 0)

    for i in range(6):
        put(part, 12 * i, dup_s[:, 128 * i : 128 * i + 128] * grad_scale)
        put(part, 72 + 12 * i, ddown_s[:, 128 * i : 128 * i + 128] * grad_scale)
    early = AllReduce(EARLY, part, full, spot, early_bufs)
    late = AllReduce(LATE, part, full, spot, late_bufs)
    early.step(0)

    cut_back(upd_s, 0, grid, band, side, corner)
    back_pairs = ((band, band_s2, band_r2), (side, side_s2, side_r2), (corner, corner_s2, corner_r2))

    def back_copies(f):
        return [
            remote(
                src.at[f], dst.at[f], back_sems.at[0, f, i], back_sems.at[1, f, i], spot.after[i]
            )
            for i, (_, src, dst) in enumerate(back_pairs)
        ]

    for source, target, _ in back_pairs:
        target[0] = source[0].astype(BF16)
    start(back_copies(0))

    def backward(zone, carry):
        for part_of_zone in range(2):
            w = zone * 2 + part_of_zone
            d_win = dres_s[w].astype(BF16)
            dproj_s[...] += dot(mrg_s[w], d_win)
            d_merged = dot(wproj_ref[...], d_win, 1, 1)
            for h in range(HEADS):
                at_q = slice(h * WIDTH, (h + 1) * WIDTH)
                at_k = slice(CH + h * WIDTH, CH + (h + 1) * WIDTH)
                at_v = slice(2 * CH + h * WIDTH, 2 * CH + (h + 1) * WIDTH)
                weights = soft_s[w * HEADS + h]
                inv = inv_s[w, h : h + 1]
                d_m = d_merged[h * WIDTH : (h + 1) * WIDTH] * inv
                lean = jnp.sum(d_m * mrg_s[w, at_q].astype(F32), axis=0, keepdims=True)
                d_mb = d_m.astype(BF16)
                d_chances = dot(trip_s[w, at_v], d_mb, 0, 0)
                d_scores = weights.astype(F32) * (d_chances - lean)
                at = pl.ds(pl.multiple_of((h * ZONES + zone) * PLACES, PLACES), PLACES)
                ds_ref[0, at, :] += d_scores[:, 0:128]
                ds_ref[1, at, 0:16] += d_scores[:, 128:PLACES]
                scaled = d_scores.astype(BF16)
                dtrip_s[at_q] = (dot(trip_s[w, at_k], scaled) * SCALE).astype(BF16)
                dtrip_s[at_k] = (dot(trip_s[w, at_q], scaled, 1, 1) * (1 / LOG2E)).astype(BF16)
                dtrip_s[at_v] = dot(d_mb, weights, 1, 1).astype(BF16)
            first_t = jnp.transpose(first_s[w].astype(F32)).astype(BF16)
            d_triple = dtrip_s[...]
            dqkv_s[...] += dot(first_t, d_triple, 1, 1)
            d_first = dot(d_triple, wqkvt_s[...], 0, 0).astype(BF16).astype(F32)
            unit, rscale = normed(win[0, w])
            d_in, d_gain = norm_back(unit, rscale, g1, d_first)
            dtok_s[w] = dres_s[w] + d_in
            dgain_s[0:1] += d_gain
        for i in range(4):
            pl.when(zone == i)(functools.partial(early.step, i + 1))
        return carry

    lax.fori_loop(0, ZONES, backward, 0)

    for i in range(4):
        put(part, 144 + 12 * i, dqkv_s[:, 128 * i : 128 * i + 128] * grad_scale)
    mixed = jnp.concatenate([dqkv_s[:, 512:576], dproj_s[:, 0:64]], axis=1)
    put(part, 192, mixed * grad_scale)
    put(part, 204, dproj_s[:, 64:192] * grad_scale)
    gains = jnp.concatenate([dgain_s[:, 128:192], jnp.zeros((8, 64), F32)], axis=1)
    gains = jnp.concatenate([dgain_s[:, 0:128], gains], axis=0) * grad_scale
    part[216] = gains.astype(BF16)
    part[217:TILES] = jnp.zeros((TILES - 217, 16, 128), BF16)
    late.step(0)
    cut_back(dtok_s, 1, grid, band, side, corner)
    for source, target, _ in back_pairs:
        target[1] = source[1].astype(BF16)

    def scatter_groups(turn, carry):
        step = functools.partial(scatter_step, ds_ref, idx_ref, hot_ref, acc_ref)
        lax.fori_loop(turn * 3, turn * 3 + 3, step, 0)
        for i in range(6):

            def serve(i=i):
                if i < 3:
                    early.step(i + 5)
                late.step(i + 1)
                if i == 0:
                    start(back_copies(1))

            pl.when(turn == i)(serve)
        return carry

    lax.fori_loop(0, 6, scatter_groups, 0)

    lon = spot.lon
    for i in range(PAIRS):
        tab_s[i] = (acc_ref[48 * i : 48 * i + 48] * grad_scale).astype(BF16)
    tab_s[PAIRS] = jnp.zeros((48, 256), BF16)
    copies = [
        remote(
            tab_s.at[lax.rem(lon + d + 1, 8)],
            tab_r.at[d],
            tab_sems.at[0, d],
            tab_sems.at[1, d],
            spot.along_lon[d],
        )
        for d in range(7)
    ]
    start(copies)
    finish(back_copies(0))
    finish(back_copies(1))
    add_back(grid, band_r2, side_r2, corner_r2)
    finish(copies)
    total = tab_s[lon].astype(F32)
    for d in range(7):
        total += tab_r[d].astype(F32)
    tab_full[lon] = total.astype(BF16)
    copies = [
        remote(
            tab_full.at[lon],
            tab_full.at[lon],
            tab_sems.at[2, d],
            tab_sems.at[3, d],
            spot.along_lon[d],
        )
        for d in range(7)
    ]
    start(copies)
    for i in range(6):
        updo_ref[:, i] = (grid[0, :, i] * valid[i]).astype(BF16)
        dtoko_ref[:, i] = (grid[1, :, i] * valid[i]).astype(BF16)
    late.step(7)
    full_ref[...] = full[...]
    finish(copies)
    tab_ref[...] = tab_full[...]


def block_pass(grad_scale, *args):
    sd = jax.ShapeDtypeStruct
    sem = pltpu.SemaphoreType.DMA
    return pl.pallas_call(
        functools.partial(block_kernel, grad_scale),
        out_shape=[
            sd((8, 6, 24, CH), BF16),
            sd((8, 6, 24, CH), BF16),
            sd((TILES, 16, 128), BF16),
            sd((8, 48, 256), BF16),
        ],
        in_specs=[pl.BlockSpec(memory_space=pltpu.SMEM)] + [VMEM_SPEC] * 10,
        out_specs=[VMEM_SPEC] * 4,
        scratch_shapes=[
            vm((PLACES, 256), jnp.int32),
            vm((HI * ROWS, 256), F32),
            vm((GROUPS, 256, SPAN), BF16),
            vm((2, ROWS * PLACES, 128), F32),
            vm((2, ROWS * PLACES, 128), F32),
            vm((PAIRS * 48, 256), F32),
            vm((2, WINDOWS, PLACES, CH), F32),
            vm((2, 8, 6, 24, CH), F32),
            *piece_scratch(),
            vm((3 * CH, CH), BF16),
            vm((WINDOWS * HEADS, PLACES, PLACES), BF16),
            vm((WINDOWS, 3 * CH, PLACES), BF16),
            vm((WINDOWS, CH, PLACES), BF16),
            vm((WINDOWS, 8, PLACES), F32),
            vm((WINDOWS, PLACES, CH), BF16),
            vm((WINDOWS, PLACES, CH), BF16),
            vm((WINDOWS, PLACES, CH), F32),
            vm((3 * CH, PLACES), BF16),
            vm((WINDOWS, PLACES, CH), F32),
            vm((WINDOWS, PLACES, CH), F32),
            vm((8, CH), F32),
            vm((CH, 3 * CH), F32),
            vm((CH, CH), F32),
            vm((CH, HIDDEN), F32),
            vm((CH, HIDDEN), F32),
            vm((TILES, 16, 128), BF16),
            vm((TILES, 16, 128), BF16),
            all_reduce_scratch(EARLY),
            all_reduce_scratch(LATE),
            vm((8, 48, 256), BF16),
            vm((7, 48, 256), BF16),
            vm((8, 48, 256), BF16),
            sem((2, 3)),
            sem((2, 2, 3)),
            sem((4, 7)),
        ],
        compiler_params=pltpu.CompilerParams(
            vmem_limit_bytes=LIMIT, collective_id=0, has_side_effects=True
        ),
    )(*args)


def write_kernel(
    upd_ref, dtok_ref, full_ref, tab_ref,
    updo_ref, dtoko_ref, gain1_ref, qkv_ref, proj_ref, gain2_ref, up_ref, down_ref, table_ref,
):
    updo_ref[...] = upd_ref[...]
    dtoko_ref[...] = dtok_ref[...]

    def get(tile):
        return full_ref[tile : tile + 12].reshape(192, 128).astype(F32)

    for i in range(6):
        up_ref[:, 128 * i : 128 * i + 128] = get(12 * i)
        down_ref[:, 128 * i : 128 * i + 128] = get(72 + 12 * i)
    for i in range(4):
        qkv_ref[:, 128 * i : 128 * i + 128] = get(144 + 12 * i)
    mixed = get(192)
    qkv_ref[:, 512:576] = mixed[:, 0:64]
    proj_ref[...] = jnp.concatenate([mixed[:, 64:128], get(204)], axis=1)
    gains = full_ref[216].astype(F32)
    gains = jnp.concatenate([gains[0:8], gains[8:16, 0:64]], axis=1)
    gain1_ref[...] = gains[0]
    gain2_ref[...] = gains[1]
    for hi in range(HI):
        wide = min(256, ENTRIES - hi * 256)
        block = tab_ref[hi // 2].astype(F32)[hi % 2 * ROWS : (hi % 2 + 1) * ROWS]
        for head in range(HEADS):
            table_ref[head, :, hi * 256 : hi * 256 + wide] = block[
                head * ZONES : (head + 1) * ZONES, 0:wide
            ]


def write_out(*args):
    sd = jax.ShapeDtypeStruct
    return pl.pallas_call(
        write_kernel,
        out_shape=[
            sd((8, 6, 24, CH), BF16),
            sd((8, 6, 24, CH), BF16),
            sd((CH,), F32),
            sd((CH, 3 * CH), F32),
            sd((CH, CH), F32),
            sd((CH,), F32),
            sd((CH, HIDDEN), F32),
            sd((CH, HIDDEN), F32),
            sd((HEADS, ZONES, ENTRIES), F32),
        ],
        in_specs=[VMEM_SPEC] * 4,
        out_specs=[VMEM_SPEC] * 9,
        compiler_params=pltpu.CompilerParams(vmem_limit_bytes=LIMIT),
    )(*args)


def per_device(
    tokens,
    lat_valid,
    gain_attn,
    w_qkv,
    w_proj,
    gain_mlp,
    w_up,
    w_down,
    bias_table,
    index_table,
    cotangent,
):
    levels, row_count, col_count, channels = tokens.shape
    grad_scale = float(levels * row_count * col_count * 128) ** (-0.5)
    parts = block_pass(
        grad_scale,
        lat_valid,
        tokens,
        cotangent,
        bias_table.transpose(1, 0, 2),
        index_table,
        gain_attn,
        w_qkv,
        w_proj,
        gain_mlp,
        w_up,
        w_down.T,
    )
    updated, d_tokens, d_gain1, d_qkv, d_proj, d_gain2, d_up, d_down, d_table = write_out(*parts)
    d_table = d_table.transpose(1, 0, 2)
    return updated, d_tokens, d_gain1, d_qkv, d_proj, d_gain2, d_up, d_down.T, d_table


def solution(mesh):
    field = P(None, "lat", "lon", None)
    in_specs = (field, P("lat"), P(), P(), P(), P(), P(), P(), P("lat"), P(), field)
    out_specs = (field, field, P(), P(), P(), P(), P(), P(), P("lat"))
    return jax.shard_map(
        per_device, mesh=mesh, in_specs=in_specs, out_specs=out_specs, check_vma=False
    )
```

```python
import functools
import jax
import jax.numpy as jnp
from jax import lax
from jax.sharding import PartitionSpec as P
from jax.experimental import pallas as pl
from jax.experimental.pallas import tpu as pltpu

WIN_Z = 2
WIN_LAT = 6
WIN_LON = 12
PLACES = 144
HEADS = 6
WIDTH = 32
CH = 192
HIDDEN = 768
WINDOWS = 8
TOKENS = 1152
ZONES = 4
ROWS = ZONES * HEADS
ENTRIES = 3312
HI = 13
PAIRS = 7
GROUPS = 18
SPAN = 1152
LOG2E = 1.4426950408889634
SCALE = 32**-0.5
NORM_EPS = 1e-05
F32 = jnp.float32
BF16 = jnp.bfloat16


def dot(left, right, left_dim=1, right_dim=0):
    return lax.dot_general(
        left, right, (((left_dim,), (right_dim,)), ((), ())), preferred_element_type=F32
    )


def entry_lanes(idx_ref, group):
    start = pl.multiple_of(group * 8, 8)
    main = idx_ref[pl.ds(start, 8), 0:128]
    rest = idx_ref[pl.ds(start, 8), 128:256].astype(F32)
    rest = pltpu.roll(rest, 0, 1, stride=16, stride_axis=0)
    place = lax.broadcasted_iota(jnp.int32, (8, 128), 0)
    lane = lax.broadcasted_iota(jnp.int32, (8, 128), 1)
    rest = jnp.sum(jnp.where(lane // 16 == place, rest, 0.0), axis=0, keepdims=True)
    rows = [main[i : i + 1] for i in range(8)] + [rest.astype(jnp.int32)]
    return jnp.concatenate(rows, axis=1)


def low_onehot(entries):
    low = jnp.broadcast_to((entries & 255).astype(F32).astype(BF16), (256, SPAN))
    at = lax.broadcasted_iota(jnp.int32, (256, SPAN), 0).astype(F32).astype(BF16)
    return jnp.where(low == at, jnp.ones((), BF16), jnp.zeros((), BF16))


def transposed_index(idx_in, idx_ref):
    idx_ref[:, 128:256] = jnp.zeros((PLACES, 128), jnp.int32)
    idx_ref[:, 0:PLACES] = jnp.transpose(idx_in[...].astype(F32)).astype(jnp.int32)


def region_of(place, last_zone, last_band):
    depth = place // (WIN_LAT * WIN_LON)
    row = place // WIN_LON % WIN_LAT
    level = jnp.where(depth >= WIN_Z - WIN_Z // 2, 2, 1) * last_zone
    band = jnp.where(row >= WIN_LAT - WIN_LAT // 2, 2, 1) * last_band
    return 3 * level + band


def gather_bias(table_ref, idx_in, bias_ref, idx_ref, t2_ref, hot_ref):
    last_band = (lax.axis_index("lat") == 15).astype(jnp.int32)
    transposed_index(idx_in, idx_ref)
    for hi in range(HI):
        wide = min(256, ENTRIES - hi * 256)
        for head in range(HEADS):
            part = table_ref[head, :, hi * 256 : hi * 256 + wide] * LOG2E
            if wide < 256:
                part = jnp.concatenate([part, jnp.zeros((ZONES, 256 - wide), F32)], axis=1)
            t2_ref[hi * ROWS + head * ZONES : hi * ROWS + (head + 1) * ZONES, :] = part

    def step(group, carry):
        entries = entry_lanes(idx_ref, group)
        onehot = low_onehot(entries)
        hot_ref[group] = onehot
        found = dot(t2_ref[...].astype(BF16), onehot)
        high = jnp.broadcast_to(entries >> 8, (ROWS, SPAN))
        bias = jnp.where(high == 0, found[0:ROWS], 0.0)
        for hi in range(1, HI):
            bias = jnp.where(high == hi, found[hi * ROWS : (hi + 1) * ROWS], bias)
        lane = lax.broadcasted_iota(jnp.int32, (ROWS, 128), 1)
        zone3 = (lax.broadcasted_iota(jnp.int32, (ROWS, 128), 0) % ZONES == ZONES - 1).astype(
            jnp.int32
        )
        main_region = region_of(lane, zone3, last_band)
        rest_region = region_of((lane & 15) + 128, zone3, last_band)
        rest = bias[:, 1024:1152]
        for i in range(8):
            key = group * 8 + i
            key_region = region_of(jnp.full((ROWS, 128), key, jnp.int32), zone3, last_band)
            main_i = jnp.where(
                main_region == key_region, bias[:, i * 128 : (i + 1) * 128], -1e30
            )
            rest_i = rest if i == 0 else pltpu.roll(rest, 128 - 16 * i, 1)
            rest_i = jnp.where(rest_region == key_region, rest_i, -1e30)
            bias_ref[0, pl.ds(key, ROWS, stride=PLACES), :] = main_i
            bias_ref[1, pl.ds(key, ROWS, stride=PLACES), :] = rest_i
        return carry

    lax.fori_loop(0, GROUPS, step, 0)


def scatter_step(ds_ref, idx_ref, hot_ref, acc_ref, group, carry):
    entries = entry_lanes(idx_ref, group)
    lane = lax.broadcasted_iota(jnp.int32, (ROWS, 128), 1)
    mains, rest = [], jnp.zeros((ROWS, 128), F32)
    for i in range(8):
        key = group * 8 + i
        mains.append(ds_ref[0, pl.ds(key, ROWS, stride=PLACES), :])
        rest_i = ds_ref[1, pl.ds(key, ROWS, stride=PLACES), :]
        if i:
            rest_i = pltpu.roll(rest_i, 16 * i, 1)
        rest = jnp.where(lane // 16 == i, rest_i, rest)
    grads = jnp.concatenate(mains + [rest], axis=1)
    grads = jnp.concatenate([grads, grads], axis=0).astype(BF16)
    high = jnp.broadcast_to((entries >> 8).astype(F32), (ROWS, SPAN))
    high = jnp.concatenate([high, high - 1.0], axis=0).astype(BF16)
    zero = jnp.zeros((), BF16)
    parts = [jnp.where(high == jnp.full((), 2 * i, BF16), grads, zero) for i in range(PAIRS)]
    acc_ref[...] += dot(jnp.concatenate(parts, axis=0), hot_ref[group], 1, 1)
    return carry


def normed(values):
    center = values - jnp.mean(values, axis=-1, keepdims=True)
    rscale = lax.rsqrt(jnp.mean(center * center, axis=-1, keepdims=True) + NORM_EPS)
    return center * rscale, rscale


def norm_back(unit, rscale, gain, incoming):
    scaled = incoming * gain
    d_inputs = rscale * (
        scaled
        - jnp.mean(scaled, axis=-1, keepdims=True)
        - unit * jnp.mean(scaled * unit, axis=-1, keepdims=True)
    )
    return d_inputs


VMEM_SPEC = pl.BlockSpec(memory_space=pltpu.VMEM)
LIMIT = 60 * 1024 * 1024


def vm(shape, dtype):
    return pltpu.VMEM(shape, dtype)


MESH = pl.DeviceIdType.MESH
BAND_ROWS, SIDE_ROWS = 224, 80


def remote(src, dst, send, recv, device):
    return pltpu.make_async_remote_copy(
        src_ref=src, dst_ref=dst, send_sem=send, recv_sem=recv, device_id=device, device_id_type=MESH
    )


def places():
    lat, lon = lax.axis_index("lat"), lax.axis_index("lon")
    up, down = lax.rem(lat + 1, 16), lax.rem(lat + 15, 16)
    right, left = lax.rem(lon + 1, 8), lax.rem(lon + 7, 8)
    after = [(up, lon), (lat, right), (up, right)]
    before = [(down, lon), (lat, left), (down, left)]
    return after, before


def spot_of(zone, piece, count):
    at = (zone % 2 * 6 + piece) * count
    return slice(at, at + count), slice(zone // 2 * CH, (zone // 2 + 1) * CH)


def cut_pieces(field, f, valid, win, band, side, corner):
    for zone in range(ZONES):
        for depth in range(2):
            level = (2 * zone + depth + 1) % 8
            for i in range(6):
                row = field[level, i].astype(F32) * valid[i]
                piece = depth * 3 + i % 3
                if i < 3:
                    band[f, *spot_of(zone, piece, 18)] = row[6:24]
                    corner[f, *spot_of(zone, piece, 6)] = row[0:6]
                else:
                    side[f, *spot_of(zone, piece, 6)] = row[0:6]
                    at = (depth * 6 + i - 3) * 12
                    win[f, 2 * zone, at : at + 12] = row[6:18]
                    win[f, 2 * zone + 1, at : at + 6] = row[18:24]


def add_pieces(win, band, side, corner):
    for f in range(2):
        band_v = band[f].astype(F32)
        side_v = side[f].astype(F32)
        corner_v = corner[f].astype(F32)
        for zone in range(ZONES):
            for depth in range(2):
                for i in range(3):
                    piece = depth * 3 + i
                    at = (depth * 6 + i) * 12
                    win[f, 2 * zone + 1, at + 6 : at + 12] = side_v[spot_of(zone, piece, 6)]
                    at = (depth * 6 + i + 3) * 12
                    rows = band_v[spot_of(zone, piece, 18)]
                    win[f, 2 * zone, at : at + 12] = rows[0:12]
                    win[f, 2 * zone + 1, at : at + 6] = rows[12:18]
                    win[f, 2 * zone + 1, at + 6 : at + 12] = corner_v[spot_of(zone, piece, 6)]


def cut_back(field, f, grid, band, side, corner):
    for zone in range(ZONES):
        near = field[2 * zone]
        far = field[2 * zone + 1]
        for depth in range(2):
            level = (2 * zone + depth + 1) % 8
            for i in range(6):
                at = (depth * 6 + i) * 12
                piece = depth * 3 + i % 3
                if i < 3:
                    grid[f, level, i + 3, 6:18] = near[at : at + 12]
                    grid[f, level, i + 3, 18:24] = far[at : at + 6]
                    side[f, *spot_of(zone, piece, 6)] = far[at + 6 : at + 12]
                else:
                    rows, lanes = spot_of(zone, piece, 18)
                    band[f, rows.start : rows.start + 12, lanes] = near[at : at + 12]
                    band[f, rows.start + 12 : rows.stop, lanes] = far[at : at + 6]
                    corner[f, *spot_of(zone, piece, 6)] = far[at + 6 : at + 12]


def add_back(f, grid, band, side, corner):
    band_v = band[f].astype(F32)
    side_v = side[f].astype(F32)
    corner_v = corner[f].astype(F32)
    for zone in range(ZONES):
        for depth in range(2):
            level = (2 * zone + depth + 1) % 8
            for i in range(3):
                piece = depth * 3 + i
                grid[f, level, i, 6:24] = band_v[spot_of(zone, piece, 18)]
                grid[f, level, i, 0:6] = corner_v[spot_of(zone, piece, 6)]
                grid[f, level, i + 3, 0:6] = side_v[spot_of(zone, piece, 6)]


def piece_scratch():
    out = []
    for kind in (F32, BF16, BF16, BF16, BF16):
        for rows in (BAND_ROWS, SIDE_ROWS, SIDE_ROWS):
            out.append(vm((2, rows, 2 * CH), kind))
    return out


TILES = 224
EARLY = (0, 64, 4)
LATE = (128, 48, 3)


class AllReduce:
    def __init__(self, plan, part, full, spot, bufs):
        self.base, self.half, self.count = plan
        self.part, self.full, self.spot = part, full, spot
        self.core_r, self.plane_r, self.depth_r = bufs[:3]
        self.core_sems, self.plane_sems, self.depth_sems = bufs[3:]
        self.mine = self.base + spot.core * self.half
        self.own = pl.ds(self.mine + spot.seat * self.count, self.count)

    def core_copy(self):
        other = self.base + (1 - self.spot.core) * self.half
        source = self.part.at[pl.ds(other, self.half)]
        return remote(
            source, self.core_r, self.core_sems.at[0], self.core_sems.at[1], self.spot.sibling
        )

    def core_back(self):
        region = self.full.at[pl.ds(self.mine, self.half)]
        return remote(
            region, region, self.core_sems.at[2], self.core_sems.at[3], self.spot.sibling
        )

    def scatter(self):
        copies = []
        for i, (seat, device) in enumerate(self.spot.plane):
            source = self.part.at[pl.ds(self.mine + seat * self.count, self.count)]
            sems = self.plane_sems
            copies.append(
                remote(source, self.plane_r.at[i], sems.at[0, i], sems.at[1, i], device)
            )
        return copies

    def gather(self):
        region, sems = self.full.at[self.own], self.plane_sems
        return [
            remote(region, region, sems.at[2, i], sems.at[3, i], device)
            for i, (_, device) in enumerate(self.spot.plane)
        ]

    def depth(self):
        source, sems = self.part.at[self.own], self.depth_sems
        target = self.depth_r.at[self.spot.z]
        return [
            remote(source, target, sems.at[0, d], sems.at[1, d], self.spot.along_z[d])
            for d in range(3)
        ]

    def step(self, number):
        if number == 0:
            self.core_copy().start()
        elif number == 1:
            self.core_copy().wait()
            half = pl.ds(self.mine, self.half)
            total = self.part[half].astype(F32) + self.core_r[...].astype(F32)
            self.part[half] = total.astype(BF16)
            start(self.scatter())
        elif number == 2:
            finish(self.scatter())
            total = self.part[self.own].astype(F32)
            for i in range(15):
                total += self.plane_r[i].astype(F32)
            total = total.astype(BF16)
            self.part[self.own] = total
            self.depth_r[pl.ds(self.spot.z, 1)] = total[None]
            start(self.depth())
        elif number == 3:
            finish(self.depth())
            total = self.depth_r[0].astype(F32)
            for d in range(1, 4):
                total += self.depth_r[d].astype(F32)
            self.full[self.own] = total.astype(BF16)
            start(self.gather())
        elif number == 4:
            finish(self.gather())
            self.core_back().start()
        else:
            self.core_back().wait()


def all_reduce_scratch(plan):
    _, half, count = plan
    sem = pltpu.SemaphoreType.DMA
    return [
        vm((half, 16, 128), BF16),
        vm((15, count, 16, 128), BF16),
        vm((4, count, 16, 128), BF16),
        sem((4,)),
        sem((4, 15)),
        sem((2, 3)),
    ]


def start(copies):
    for copy in copies:
        copy.start()


def finish(copies):
    for copy in copies:
        copy.wait()


class Spot:
    def __init__(self):
        lat, lon = lax.axis_index("lat"), lax.axis_index("lon")
        self.lat, self.lon = lat, lon
        self.core, self.x, z_lo = lat % 2, lat // 2 % 4, lat // 8
        self.y, z_hi = lon % 4, lon // 4
        self.z = z_hi * 2 + z_lo
        self.sibling = self.device(core=1 - self.core)
        self.seat = self.x * 4 + self.y
        self.plane = []
        for d in range(1, 16):
            x, y = lax.rem(self.x + d // 4, 4), lax.rem(self.y + d % 4, 4)
            self.plane.append((x * 4 + y, self.device(x=x, y=y)))
        self.along_z = [self.device(z=lax.rem(self.z + d, 4)) for d in range(1, 4)]
        self.along_lon = [(lat, lax.rem(lon + d, 8)) for d in range(1, 8)]
        self.after, self.before = places()
        far = [(lat, (1 - z_hi) * 4 + lax.rem(self.y + d, 4)) for d in range(1, 4)]
        self.all = [self.sibling] + [device for _, device in self.plane] + self.along_z + far
        self.all += [self.after[0], self.after[2], self.before[0], self.before[2]]

    def device(self, core=None, x=None, y=None, z=None):
        core = self.core if core is None else core
        x = self.x if x is None else x
        y = self.y if y is None else y
        z = self.z if z is None else z
        return (z % 2 * 4 + x) * 2 + core, z // 2 * 4 + y


def put(part, tile, value):
    part[tile : tile + 12] = value.astype(BF16).reshape(12, 16, 128)


def block_kernel(
    grad_scale, valid_ref, tok_ref, cot_ref, table_ref, idx_in, g1_ref, wqkv_ref, wproj_ref,
    g2_ref, wup_ref, wdown_ref,
    updo_ref, dtoko_ref, full_ref, tab_ref,
    idx_ref, t2_ref, hot_ref, bias_ref, acc_ref, win, grid,
    band, side, corner, band_s, side_s, corner_s, band_r, side_r, corner_r,
    band_s2, side_s2, corner_s2, band_r2, side_r2, corner_r2,
    wqkvt_s, soft_s, trip_s, mrg_s, inv_s, first_s, resid_s, dres_s, dtrip_s, dsoft_s, dmrg_s, upd_s,
    dqkv_s, dproj_s, dup_s, ddown_s,
    part, full, early_bufs, late_bufs, tab_s, tab_r, tab_full, halo_sems, back_sems, tab_sems,
):
    ds_ref = bias_ref
    spot = Spot()
    barrier = pltpu.get_barrier_semaphore()
    for device in spot.all:
        pl.semaphore_signal(barrier, inc=1, device_id=device, device_id_type=MESH)
    valid = [valid_ref[i].astype(F32) for i in range(6)]
    cut_pieces(tok_ref, 0, valid, win, band, side, corner)
    cut_pieces(cot_ref, 1, valid, win, band, side, corner)
    for source, target in ((band, band_s), (side, side_s), (corner, corner_s)):
        target[...] = source[...].astype(BF16)
    pl.semaphore_wait(barrier, len(spot.all))
    pairs = ((band_s, band_r), (side_s, side_r), (corner_s, corner_r))
    halo = [
        remote(src, dst, halo_sems.at[0, i], halo_sems.at[1, i], spot.before[i])
        for i, (src, dst) in enumerate(pairs)
    ]
    start(halo)
    gather_bias(table_ref, idx_in, bias_ref, idx_ref, t2_ref, hot_ref)
    wqkvt_s[...] = jnp.transpose(wqkv_ref[...].astype(F32)).astype(BF16)
    g1 = g1_ref[...].astype(F32).reshape(1, CH)
    g2 = g2_ref[...].astype(F32).reshape(1, CH)
    for ref in (dqkv_s, dproj_s, dup_s, ddown_s, acc_ref):
        ref[...] = jnp.zeros_like(ref)
    finish(halo)
    add_pieces(win, band_r, side_r, corner_r)

    def forward(zone, carry):
        windows = [zone * 2, zone * 2 + 1]
        triples, scores, softs = [], [], []
        for w in windows:
            first = (normed(win[0, w])[0] * g1).astype(BF16)
            first_s[w] = first
            triple = dot(wqkvt_s[...], first, 1, 1)
            queries = (triple[0:CH] * (SCALE * LOG2E)).astype(BF16)
            triples.append(jnp.concatenate([queries, triple[CH : 3 * CH].astype(BF16)], axis=0))
        for triple in triples:
            for h in range(HEADS):
                query = triple[h * WIDTH : (h + 1) * WIDTH]
                keys = triple[CH + h * WIDTH : CH + (h + 1) * WIDTH]
                at = pl.ds(pl.multiple_of((h * ZONES + zone) * PLACES, PLACES), PLACES)
                bias = jnp.concatenate([bias_ref[0, at, :], bias_ref[1, at, 0:16]], axis=1)
                scores.append(dot(keys, query, 0, 0) + bias)
        for score in scores:
            weights = jnp.exp2(score - jnp.max(score, axis=0, keepdims=True))
            softs.append((weights.astype(BF16), 1.0 / jnp.sum(weights, axis=0, keepdims=True)))
        for side, w in enumerate(windows):
            merged = []
            for h in range(HEADS):
                weights, inv = softs[side * HEADS + h]
                values = triples[side][2 * CH + h * WIDTH : 2 * CH + (h + 1) * WIDTH]
                merged.append((dot(values, weights) * inv).astype(BF16))
            merged = jnp.concatenate(merged, axis=0)
            mrg_s[w] = merged
            attended = dot(merged, wproj_ref[...], 0, 0).astype(BF16).astype(F32)
            resid_s[w] = (win[0, w] + attended).astype(BF16)
        for side, w in enumerate(windows):
            trip_s[w] = triples[side]
            for h in range(HEADS):
                weights, inv = softs[side * HEADS + h]
                soft_s[w * HEADS + h] = weights
                inv_s[w, h : h + 1] = inv
        return carry

    lax.fori_loop(0, ZONES, forward, 0)

    many = 4
    chunk = many * PLACES

    def feed_forward(c, carry):
        here = pl.ds(c * many, many)
        resid = resid_s[here].reshape(chunk, CH).astype(F32)
        up_f = win[1, here].reshape(chunk, CH)
        up = up_f.astype(BF16)
        unit, rscale = normed(resid)
        second = unit * g2
        pre = dot(second.astype(BF16), wup_ref[...])
        c0, c1 = 0.7978845608028654, 0.7978845608028654 * 0.044715
        sq = pre * pre
        tanh = jnp.tanh(pre * (c0 + c1 * sq))
        half = 0.5 + 0.5 * tanh
        hidden = (pre * half).astype(BF16)
        slope = half + half * (1.0 - tanh) * pre * (c0 + (3.0 * c1) * sq)
        upd_s[here] = (resid + dot(hidden, wdown_ref[...], 1, 1)).reshape(many, PLACES, CH)
        ddown_s[...] += dot(jnp.transpose(up_f).astype(BF16), hidden)
        d_pre = (slope * dot(up, wdown_ref[...])).astype(BF16)
        dup_s[...] += dot(jnp.transpose(second).astype(BF16), d_pre)
        d_norm = dot(d_pre, wup_ref[...], 1, 1)
        d_in = norm_back(unit, rscale, g2, d_norm)
        dres_s[here] = (d_in + up_f).reshape(many, PLACES, CH)
        return carry

    lax.fori_loop(0, WINDOWS // many, feed_forward, 0)

    for i in range(6):
        put(part, 12 * i, dup_s[:, 128 * i : 128 * i + 128] * grad_scale)
        put(part, 72 + 12 * i, ddown_s[:, 128 * i : 128 * i + 128] * grad_scale)
    early = AllReduce(EARLY, part, full, spot, early_bufs)
    late = AllReduce(LATE, part, full, spot, late_bufs)
    early.step(0)

    cut_back(upd_s, 0, grid, band, side, corner)
    back_pairs = ((band, band_s2, band_r2), (side, side_s2, side_r2), (corner, corner_s2, corner_r2))

    def back_copies(f):
        return [
            remote(
                src.at[f], dst.at[f], back_sems.at[0, f, i], back_sems.at[1, f, i], spot.after[i]
            )
            for i, (_, src, dst) in enumerate(back_pairs)
        ]

    for source, target, _ in back_pairs:
        target[0] = source[0].astype(BF16)
    start(back_copies(0))

    def backward_scores(zone, carry):
        windows = [zone * 2, zone * 2 + 1]
        leans, d_scores = [], []
        for w in windows:
            d_merged = dot(wproj_ref[...], dres_s[w].astype(BF16), 1, 1)
            for h in range(HEADS):
                at = slice(h * WIDTH, (h + 1) * WIDTH)
                d_m = d_merged[at] * inv_s[w, h : h + 1]
                lean = jnp.sum(d_m * mrg_s[w, at].astype(F32), axis=0, keepdims=True)
                leans.append((d_m.astype(BF16), lean))
        for side, w in enumerate(windows):
            for h in range(HEADS):
                d_m, lean = leans[side * HEADS + h]
                values = trip_s[w, 2 * CH + h * WIDTH : 2 * CH + (h + 1) * WIDTH]
                d_chances = dot(values, d_m, 0, 0)
                d_scores.append(soft_s[w * HEADS + h].astype(F32) * (d_chances - lean))
        for h in range(HEADS):
            at = pl.ds(pl.multiple_of((h * ZONES + zone) * PLACES, PLACES), PLACES)
            both = d_scores[h] + d_scores[HEADS + h]
            ds_ref[0, at, :] = both[:, 0:128]
            ds_ref[1, at, 0:16] = both[:, 128:PLACES]
        for side, w in enumerate(windows):
            for h in range(HEADS):
                dsoft_s[w * HEADS + h] = d_scores[side * HEADS + h].astype(BF16)
                dmrg_s[w, h * WIDTH : (h + 1) * WIDTH] = leans[side * HEADS + h][0]
        pl.when(zone == 1)(functools.partial(early.step, 1))
        return carry

    lax.fori_loop(0, ZONES, backward_scores, 0)

    def scatter_groups(turn, carry):
        step = functools.partial(scatter_step, ds_ref, idx_ref, hot_ref, acc_ref)
        lax.fori_loop(turn * 3, turn * 3 + 3, step, 0)
        pl.when(turn == 1)(functools.partial(early.step, 2))
        pl.when(turn == 4)(functools.partial(early.step, 3))
        return carry

    lax.fori_loop(0, 6, scatter_groups, 0)

    lon = spot.lon
    for i in range(PAIRS):
        tab_s[i] = (acc_ref[48 * i : 48 * i + 48] * grad_scale).astype(BF16)
    tab_s[PAIRS] = jnp.zeros((48, 256), BF16)

    def table_scatter():
        return [
            remote(
                tab_s.at[lax.rem(lon + d + 1, 8)],
                tab_r.at[d],
                tab_sems.at[0, d],
                tab_sems.at[1, d],
                spot.along_lon[d],
            )
            for d in range(7)
        ]

    def table_gather():
        return [
            remote(
                tab_full.at[lon],
                tab_full.at[lon],
                tab_sems.at[2, d],
                tab_sems.at[3, d],
                spot.along_lon[d],
            )
            for d in range(7)
        ]

    start(table_scatter())

    def backward_triple(zone, carry):
        windows = [zone * 2, zone * 2 + 1]
        for w in windows:
            out = []
            for h in range(HEADS):
                keys = trip_s[w, CH + h * WIDTH : CH + (h + 1) * WIDTH]
                out.append((dot(keys, dsoft_s[w * HEADS + h]) * SCALE).astype(BF16))
            for h in range(HEADS):
                query = trip_s[w, h * WIDTH : (h + 1) * WIDTH]
                d_keys = dot(query, dsoft_s[w * HEADS + h], 1, 1)
                out.append((d_keys * (1 / LOG2E)).astype(BF16))
            for h in range(HEADS):
                d_m = dmrg_s[w, h * WIDTH : (h + 1) * WIDTH]
                out.append(dot(d_m, soft_s[w * HEADS + h], 1, 1).astype(BF16))
            d_triple = jnp.concatenate(out, axis=0)
            first_t = jnp.transpose(first_s[w].astype(F32)).astype(BF16)
            dqkv_s[...] += dot(first_t, d_triple, 1, 1)
            dproj_s[...] += dot(mrg_s[w], dres_s[w].astype(BF16))
            dtrip_s[w] = d_triple
        pl.when(zone == 1)(functools.partial(early.step, 4))
        return carry

    lax.fori_loop(0, ZONES, backward_triple, 0)

    for i in range(4):
        put(part, 144 + 12 * i, dqkv_s[:, 128 * i : 128 * i + 128] * grad_scale)
    mixed = jnp.concatenate([dqkv_s[:, 512:576], dproj_s[:, 0:64]], axis=1)
    put(part, 192, mixed * grad_scale)
    put(part, 204, dproj_s[:, 64:192] * grad_scale)
    part[216:TILES] = jnp.zeros((TILES - 216, 16, 128), BF16)
    late.step(0)
    finish(table_scatter())
    total = tab_s[lon].astype(F32)
    for d in range(7):
        total += tab_r[d].astype(F32)
    tab_full[lon] = total.astype(BF16)
    start(table_gather())

    def backward_norm(zone, carry):
        for w in (zone * 2, zone * 2 + 1):
            d_first = dot(dtrip_s[w], wqkvt_s[...], 0, 0).astype(BF16).astype(F32)
            unit, rscale = normed(win[0, w])
            d_in = norm_back(unit, rscale, g1, d_first)
            upd_s[w] = dres_s[w] + d_in
        return carry

    lax.fori_loop(0, 2, backward_norm, 0)
    late.step(1)
    lax.fori_loop(2, ZONES, backward_norm, 0)
    cut_back(upd_s, 1, grid, band, side, corner)
    for source, target, _ in back_pairs:
        target[1] = source[1].astype(BF16)
    start(back_copies(1))
    early.step(5)
    finish(back_copies(0))
    add_back(0, grid, band_r2, side_r2, corner_r2)
    for i in range(6):
        updo_ref[:, i] = (grid[0, :, i] * valid[i]).astype(BF16)
    late.step(2)
    finish(back_copies(1))
    add_back(1, grid, band_r2, side_r2, corner_r2)
    late.step(3)
    for i in range(6):
        dtoko_ref[:, i] = (grid[1, :, i] * valid[i]).astype(BF16)
    full_ref[0:128] = full[0:128]
    finish(table_gather())
    tab_ref[...] = tab_full[...]
    late.step(4)
    late.step(5)
    full_ref[128:TILES] = full[128:TILES]


def block_pass(grad_scale, *args):
    sd = jax.ShapeDtypeStruct
    sem = pltpu.SemaphoreType.DMA
    return pl.pallas_call(
        functools.partial(block_kernel, grad_scale),
        out_shape=[
            sd((8, 6, 24, CH), BF16),
            sd((8, 6, 24, CH), BF16),
            sd((TILES, 16, 128), BF16),
            sd((8, 48, 256), BF16),
        ],
        in_specs=[pl.BlockSpec(memory_space=pltpu.SMEM)] + [VMEM_SPEC] * 10,
        out_specs=[VMEM_SPEC] * 4,
        scratch_shapes=[
            vm((PLACES, 256), jnp.int32),
            vm((HI * ROWS, 256), F32),
            vm((GROUPS, 256, SPAN), BF16),
            vm((2, ROWS * PLACES, 128), F32),
            vm((PAIRS * 48, 256), F32),
            vm((2, WINDOWS, PLACES, CH), F32),
            vm((2, 8, 6, 24, CH), F32),
            *piece_scratch(),
            vm((3 * CH, CH), BF16),
            vm((WINDOWS * HEADS, PLACES, PLACES), BF16),
            vm((WINDOWS, 3 * CH, PLACES), BF16),
            vm((WINDOWS, CH, PLACES), BF16),
            vm((WINDOWS, 8, PLACES), F32),
            vm((WINDOWS, PLACES, CH), BF16),
            vm((WINDOWS, PLACES, CH), BF16),
            vm((WINDOWS, PLACES, CH), F32),
            vm((WINDOWS, 3 * CH, PLACES), BF16),
            vm((WINDOWS * HEADS, PLACES, PLACES), BF16),
            vm((WINDOWS, CH, PLACES), BF16),
            vm((WINDOWS, PLACES, CH), F32),
            vm((CH, 3 * CH), F32),
            vm((CH, CH), F32),
            vm((CH, HIDDEN), F32),
            vm((CH, HIDDEN), F32),
            vm((TILES, 16, 128), BF16),
            vm((TILES, 16, 128), BF16),
            all_reduce_scratch(EARLY),
            all_reduce_scratch(LATE),
            vm((8, 48, 256), BF16),
            vm((7, 48, 256), BF16),
            vm((8, 48, 256), BF16),
            sem((2, 3)),
            sem((2, 2, 3)),
            sem((4, 7)),
        ],
        compiler_params=pltpu.CompilerParams(
            vmem_limit_bytes=LIMIT, collective_id=0, has_side_effects=True
        ),
    )(*args)


def write_kernel(
    upd_ref, dtok_ref, full_ref, tab_ref, g1_ref, wqkv_ref, g2_ref, wup_ref,
    updo_ref, dtoko_ref, gain1_ref, qkv_ref, proj_ref, gain2_ref, up_ref, down_ref, table_ref,
):
    updo_ref[...] = upd_ref[...]
    dtoko_ref[...] = dtok_ref[...]

    def get(tile):
        return full_ref[tile : tile + 12].reshape(192, 128).astype(F32)

    for i in range(6):
        up_ref[:, 128 * i : 128 * i + 128] = get(12 * i)
        down_ref[:, 128 * i : 128 * i + 128] = get(72 + 12 * i)
    for i in range(4):
        qkv_ref[:, 128 * i : 128 * i + 128] = get(144 + 12 * i)
    mixed = get(192)
    qkv_ref[:, 512:576] = mixed[:, 0:64]
    proj_ref[...] = jnp.concatenate([mixed[:, 64:128], get(204)], axis=1)
    for weight, d_weight, gain, out in (
        (wqkv_ref, qkv_ref, g1_ref, gain1_ref),
        (wup_ref, up_ref, g2_ref, gain2_ref),
    ):
        sums = jnp.sum(weight[...].astype(F32) * d_weight[...], axis=1, keepdims=True)
        row = jnp.transpose(jnp.broadcast_to(sums, (CH, 128)))[0]
        out[...] = row / gain[...].astype(F32)
    for hi in range(HI):
        wide = min(256, ENTRIES - hi * 256)
        block = tab_ref[hi // 2].astype(F32)[hi % 2 * ROWS : (hi % 2 + 1) * ROWS]
        for head in range(HEADS):
            table_ref[head, :, hi * 256 : hi * 256 + wide] = block[
                head * ZONES : (head + 1) * ZONES, 0:wide
            ]


def write_out(*args):
    sd = jax.ShapeDtypeStruct
    return pl.pallas_call(
        write_kernel,
        out_shape=[
            sd((8, 6, 24, CH), BF16),
            sd((8, 6, 24, CH), BF16),
            sd((CH,), F32),
            sd((CH, 3 * CH), F32),
            sd((CH, CH), F32),
            sd((CH,), F32),
            sd((CH, HIDDEN), F32),
            sd((CH, HIDDEN), F32),
            sd((HEADS, ZONES, ENTRIES), F32),
        ],
        in_specs=[VMEM_SPEC] * 8,
        out_specs=[VMEM_SPEC] * 9,
        compiler_params=pltpu.CompilerParams(vmem_limit_bytes=LIMIT),
    )(*args)


def per_device(
    tokens,
    lat_valid,
    gain_attn,
    w_qkv,
    w_proj,
    gain_mlp,
    w_up,
    w_down,
    bias_table,
    index_table,
    cotangent,
):
    levels, row_count, col_count, channels = tokens.shape
    grad_scale = float(levels * row_count * col_count * 128) ** (-0.5)
    parts = block_pass(
        grad_scale,
        lat_valid,
        tokens,
        cotangent,
        bias_table.transpose(1, 0, 2),
        index_table,
        gain_attn,
        w_qkv,
        w_proj,
        gain_mlp,
        w_up,
        w_down.T,
    )
    updated, d_tokens, d_gain1, d_qkv, d_proj, d_gain2, d_up, d_down, d_table = write_out(
        *parts, gain_attn, w_qkv, gain_mlp, w_up
    )
    d_table = d_table.transpose(1, 0, 2)
    return updated, d_tokens, d_gain1, d_qkv, d_proj, d_gain2, d_up, d_down.T, d_table


def solution(mesh):
    field = P(None, "lat", "lon", None)
    in_specs = (field, P("lat"), P(), P(), P(), P(), P(), P(), P("lat"), P(), field)
    out_specs = (field, field, P(), P(), P(), P(), P(), P(), P("lat"))
    return jax.shard_map(
        per_device, mesh=mesh, in_specs=in_specs, out_specs=out_specs, check_vma=False
    )
```

```python
import functools
import jax
import jax.numpy as jnp
from jax import lax
from jax.sharding import PartitionSpec as P
from jax.experimental import pallas as pl
from jax.experimental.pallas import tpu as pltpu

WIN_Z = 2
WIN_LAT = 6
WIN_LON = 12
PLACES = 144
HEADS = 6
WIDTH = 32
CH = 192
HIDDEN = 768
WINDOWS = 8
TOKENS = 1152
ZONES = 4
ROWS = ZONES * HEADS
ENTRIES = 3312
HI = 13
PAIRS = 7
GROUPS = 18
SPAN = 1152
LOG2E = 1.4426950408889634
SCALE = 32**-0.5
NORM_EPS = 1e-05
F32 = jnp.float32
BF16 = jnp.bfloat16


def dot(left, right, left_dim=1, right_dim=0):
    return lax.dot_general(
        left, right, (((left_dim,), (right_dim,)), ((), ())), preferred_element_type=F32
    )


def entry_lanes(idx_ref, group):
    start = pl.multiple_of(group * 8, 8)
    main = idx_ref[pl.ds(start, 8), 0:128]
    rest = idx_ref[pl.ds(start, 8), 128:256].astype(F32)
    rest = pltpu.roll(rest, 0, 1, stride=16, stride_axis=0)
    place = lax.broadcasted_iota(jnp.int32, (8, 128), 0)
    lane = lax.broadcasted_iota(jnp.int32, (8, 128), 1)
    rest = jnp.sum(jnp.where(lane // 16 == place, rest, 0.0), axis=0, keepdims=True)
    rows = [main[i : i + 1] for i in range(8)] + [rest.astype(jnp.int32)]
    return jnp.concatenate(rows, axis=1)


def low_onehot(entries):
    low = jnp.broadcast_to((entries & 255).astype(F32).astype(BF16), (256, SPAN))
    at = lax.broadcasted_iota(jnp.int32, (256, SPAN), 0).astype(F32).astype(BF16)
    return jnp.where(low == at, jnp.ones((), BF16), jnp.zeros((), BF16))


def transposed_index(idx_in, idx_ref):
    idx_ref[:, 128:256] = jnp.zeros((PLACES, 128), jnp.int32)
    idx_ref[:, 0:PLACES] = jnp.transpose(idx_in[...].astype(F32)).astype(jnp.int32)


def region_of(place, last_zone, last_band):
    depth = place // (WIN_LAT * WIN_LON)
    row = place // WIN_LON % WIN_LAT
    level = jnp.where(depth >= WIN_Z - WIN_Z // 2, 2, 1) * last_zone
    band = jnp.where(row >= WIN_LAT - WIN_LAT // 2, 2, 1) * last_band
    return 3 * level + band


def gather_bias(table_ref, idx_in, bias_ref, idx_ref, t2_ref, hot_ref):
    last_band = (lax.axis_index("lat") == 15).astype(jnp.int32)
    transposed_index(idx_in, idx_ref)
    for hi in range(HI):
        wide = min(256, ENTRIES - hi * 256)
        for head in range(HEADS):
            part = table_ref[head, :, hi * 256 : hi * 256 + wide] * LOG2E
            if wide < 256:
                part = jnp.concatenate([part, jnp.zeros((ZONES, 256 - wide), F32)], axis=1)
            t2_ref[hi * ROWS + head * ZONES : hi * ROWS + (head + 1) * ZONES, :] = part

    def step(group, carry):
        entries = entry_lanes(idx_ref, group)
        onehot = low_onehot(entries)
        hot_ref[group] = onehot
        found = dot(t2_ref[...].astype(BF16), onehot)
        high = jnp.broadcast_to(entries >> 8, (ROWS, SPAN))
        bias = jnp.where(high == 0, found[0:ROWS], 0.0)
        for hi in range(1, HI):
            bias = jnp.where(high == hi, found[hi * ROWS : (hi + 1) * ROWS], bias)
        lane = lax.broadcasted_iota(jnp.int32, (ROWS, 128), 1)
        zone3 = (lax.broadcasted_iota(jnp.int32, (ROWS, 128), 0) % ZONES == ZONES - 1).astype(
            jnp.int32
        )
        main_region = region_of(lane, zone3, last_band)
        rest_region = region_of((lane & 15) + 128, zone3, last_band)
        rest = bias[:, 1024:1152]
        for i in range(8):
            key = group * 8 + i
            key_region = region_of(jnp.full((ROWS, 128), key, jnp.int32), zone3, last_band)
            main_i = jnp.where(
                main_region == key_region, bias[:, i * 128 : (i + 1) * 128], -1e30
            )
            rest_i = rest if i == 0 else pltpu.roll(rest, 128 - 16 * i, 1)
            rest_i = jnp.where(rest_region == key_region, rest_i, -1e30)
            bias_ref[0, pl.ds(key, ROWS, stride=PLACES), :] = main_i
            bias_ref[1, pl.ds(key, ROWS, stride=PLACES), :] = rest_i
        return carry

    return step


def scatter_step(ds_ref, idx_ref, hot_ref, acc_ref, group, carry):
    entries = entry_lanes(idx_ref, group)
    lane = lax.broadcasted_iota(jnp.int32, (ROWS, 128), 1)
    mains, rest = [], jnp.zeros((ROWS, 128), F32)
    for i in range(8):
        key = group * 8 + i
        mains.append(ds_ref[0, pl.ds(key, ROWS, stride=PLACES), :])
        rest_i = ds_ref[1, pl.ds(key, ROWS, stride=PLACES), :]
        if i:
            rest_i = pltpu.roll(rest_i, 16 * i, 1)
        rest = jnp.where(lane // 16 == i, rest_i, rest)
    grads = jnp.concatenate(mains + [rest], axis=1)
    grads = jnp.concatenate([grads, grads], axis=0).astype(BF16)
    high = jnp.broadcast_to((entries >> 8).astype(F32), (ROWS, SPAN))
    high = jnp.concatenate([high, high - 1.0], axis=0).astype(BF16)
    zero = jnp.zeros((), BF16)
    parts = [jnp.where(high == jnp.full((), 2 * i, BF16), grads, zero) for i in range(PAIRS)]
    acc_ref[...] += dot(jnp.concatenate(parts, axis=0), hot_ref[group], 1, 1)
    return carry


def normed(values):
    center = values - jnp.mean(values, axis=-1, keepdims=True)
    rscale = lax.rsqrt(jnp.mean(center * center, axis=-1, keepdims=True) + NORM_EPS)
    return center * rscale, rscale


def norm_back(unit, rscale, gain, incoming):
    scaled = incoming * gain
    d_inputs = rscale * (
        scaled
        - jnp.mean(scaled, axis=-1, keepdims=True)
        - unit * jnp.mean(scaled * unit, axis=-1, keepdims=True)
    )
    return d_inputs


VMEM_SPEC = pl.BlockSpec(memory_space=pltpu.VMEM)
LIMIT = 60 * 1024 * 1024


def vm(shape, dtype):
    return pltpu.VMEM(shape, dtype)


MESH = pl.DeviceIdType.MESH
BAND_ROWS, SIDE_ROWS = 224, 80


def remote(src, dst, send, recv, device):
    return pltpu.make_async_remote_copy(
        src_ref=src, dst_ref=dst, send_sem=send, recv_sem=recv, device_id=device, device_id_type=MESH
    )


def places():
    lat, lon = lax.axis_index("lat"), lax.axis_index("lon")
    up, down = lax.rem(lat + 1, 16), lax.rem(lat + 15, 16)
    right, left = lax.rem(lon + 1, 8), lax.rem(lon + 7, 8)
    after = [(up, lon), (lat, right), (up, right)]
    before = [(down, lon), (lat, left), (down, left)]
    return after, before


def spot_of(zone, piece, count):
    at = (zone % 2 * 6 + piece) * count
    return slice(at, at + count), slice(zone // 2 * CH, (zone // 2 + 1) * CH)


def cut_pieces(field, f, valid, win, band, side, corner):
    for zone in range(ZONES):
        for depth in range(2):
            level = (2 * zone + depth + 1) % 8
            for i in range(6):
                row = field[level, i].astype(F32) * valid[i]
                piece = depth * 3 + i % 3
                if i < 3:
                    band[f, *spot_of(zone, piece, 18)] = row[6:24]
                    corner[f, *spot_of(zone, piece, 6)] = row[0:6]
                else:
                    side[f, *spot_of(zone, piece, 6)] = row[0:6]
                    at = (depth * 6 + i - 3) * 12
                    win[f, 2 * zone, at : at + 12] = row[6:18]
                    win[f, 2 * zone + 1, at : at + 6] = row[18:24]


def add_pieces(win, band, side, corner):
    for f in range(2):
        band_v = band[f].astype(F32)
        side_v = side[f].astype(F32)
        corner_v = corner[f].astype(F32)
        for zone in range(ZONES):
            for depth in range(2):
                for i in range(3):
                    piece = depth * 3 + i
                    at = (depth * 6 + i) * 12
                    win[f, 2 * zone + 1, at + 6 : at + 12] = side_v[spot_of(zone, piece, 6)]
                    at = (depth * 6 + i + 3) * 12
                    rows = band_v[spot_of(zone, piece, 18)]
                    win[f, 2 * zone, at : at + 12] = rows[0:12]
                    win[f, 2 * zone + 1, at : at + 6] = rows[12:18]
                    win[f, 2 * zone + 1, at + 6 : at + 12] = corner_v[spot_of(zone, piece, 6)]


def cut_back(field, f, grid, band, side, corner):
    for zone in range(ZONES):
        near = field[2 * zone]
        far = field[2 * zone + 1]
        for depth in range(2):
            level = (2 * zone + depth + 1) % 8
            for i in range(6):
                at = (depth * 6 + i) * 12
                piece = depth * 3 + i % 3
                if i < 3:
                    grid[f, level, i + 3, 6:18] = near[at : at + 12]
                    grid[f, level, i + 3, 18:24] = far[at : at + 6]
                    side[f, *spot_of(zone, piece, 6)] = far[at + 6 : at + 12]
                else:
                    rows, lanes = spot_of(zone, piece, 18)
                    band[f, rows.start : rows.start + 12, lanes] = near[at : at + 12]
                    band[f, rows.start + 12 : rows.stop, lanes] = far[at : at + 6]
                    corner[f, *spot_of(zone, piece, 6)] = far[at + 6 : at + 12]


def add_back(f, grid, band, side, corner):
    band_v = band[f].astype(F32)
    side_v = side[f].astype(F32)
    corner_v = corner[f].astype(F32)
    for zone in range(ZONES):
        for depth in range(2):
            level = (2 * zone + depth + 1) % 8
            for i in range(3):
                piece = depth * 3 + i
                grid[f, level, i, 6:24] = band_v[spot_of(zone, piece, 18)]
                grid[f, level, i, 0:6] = corner_v[spot_of(zone, piece, 6)]
                grid[f, level, i + 3, 0:6] = side_v[spot_of(zone, piece, 6)]


def piece_scratch():
    out = []
    for kind in (F32, BF16, BF16, BF16, BF16):
        for rows in (BAND_ROWS, SIDE_ROWS, SIDE_ROWS):
            out.append(vm((2, rows, 2 * CH), kind))
    return out


TILES = 224
EARLY = (0, 64, 4)
LATE = (128, 48, 3)


class AllReduce:
    def __init__(self, plan, part, full, spot, bufs):
        self.base, self.half, self.count = plan
        self.part, self.full, self.spot = part, full, spot
        self.core_r, self.plane_r, self.depth_r = bufs[:3]
        self.core_sems, self.plane_sems, self.depth_sems = bufs[3:]
        self.mine = self.base + spot.core * self.half
        self.own = pl.ds(self.mine + spot.seat * self.count, self.count)

    def core_copy(self):
        other = self.base + (1 - self.spot.core) * self.half
        source = self.part.at[pl.ds(other, self.half)]
        return remote(
            source, self.core_r, self.core_sems.at[0], self.core_sems.at[1], self.spot.sibling
        )

    def core_back(self):
        region = self.full.at[pl.ds(self.mine, self.half)]
        return remote(
            region, region, self.core_sems.at[2], self.core_sems.at[3], self.spot.sibling
        )

    def scatter(self):
        copies = []
        for i, (seat, device) in enumerate(self.spot.plane):
            source = self.part.at[pl.ds(self.mine + seat * self.count, self.count)]
            sems = self.plane_sems
            copies.append(
                remote(source, self.plane_r.at[i], sems.at[0, i], sems.at[1, i], device)
            )
        return copies

    def gather(self):
        region, sems = self.full.at[self.own], self.plane_sems
        return [
            remote(region, region, sems.at[2, i], sems.at[3, i], device)
            for i, (_, device) in enumerate(self.spot.plane)
        ]

    def depth(self):
        source, sems = self.part.at[self.own], self.depth_sems
        target = self.depth_r.at[self.spot.z]
        return [
            remote(source, target, sems.at[0, d], sems.at[1, d], self.spot.along_z[d])
            for d in range(3)
        ]

    def step(self, number):
        if number == 0:
            self.core_copy().start()
        elif number == 1:
            self.core_copy().wait()
            half = pl.ds(self.mine, self.half)
            total = self.part[half].astype(F32) + self.core_r[...].astype(F32)
            self.part[half] = total.astype(BF16)
            start(self.scatter())
        elif number == 2:
            finish(self.scatter())
            total = self.part[self.own].astype(F32)
            for i in range(15):
                total += self.plane_r[i].astype(F32)
            total = total.astype(BF16)
            self.part[self.own] = total
            self.depth_r[pl.ds(self.spot.z, 1)] = total[None]
            start(self.depth())
        elif number == 3:
            finish(self.depth())
            total = self.depth_r[0].astype(F32)
            for d in range(1, 4):
                total += self.depth_r[d].astype(F32)
            self.full[self.own] = total.astype(BF16)
            start(self.gather())
        elif number == 4:
            finish(self.gather())
            self.core_back().start()
        else:
            self.core_back().wait()


def all_reduce_scratch(plan):
    _, half, count = plan
    sem = pltpu.SemaphoreType.DMA
    return [
        vm((half, 16, 128), BF16),
        vm((15, count, 16, 128), BF16),
        vm((4, count, 16, 128), BF16),
        sem((4,)),
        sem((4, 15)),
        sem((2, 3)),
    ]


def start(copies):
    for copy in copies:
        copy.start()


def finish(copies):
    for copy in copies:
        copy.wait()


class Spot:
    def __init__(self):
        lat, lon = lax.axis_index("lat"), lax.axis_index("lon")
        self.lat, self.lon = lat, lon
        self.core, self.x, z_lo = lat % 2, lat // 2 % 4, lat // 8
        self.y, z_hi = lon % 4, lon // 4
        self.z = z_hi * 2 + z_lo
        self.sibling = self.device(core=1 - self.core)
        self.seat = self.x * 4 + self.y
        self.plane = []
        for d in range(1, 16):
            x, y = lax.rem(self.x + d // 4, 4), lax.rem(self.y + d % 4, 4)
            self.plane.append((x * 4 + y, self.device(x=x, y=y)))
        self.along_z = [self.device(z=lax.rem(self.z + d, 4)) for d in range(1, 4)]
        self.along_lon = [(lat, lax.rem(lon + d, 8)) for d in range(1, 8)]
        self.after, self.before = places()
        far = [(lat, (1 - z_hi) * 4 + lax.rem(self.y + d, 4)) for d in range(1, 4)]
        self.all = [self.sibling] + [device for _, device in self.plane] + self.along_z + far
        self.all += [self.after[0], self.after[2], self.before[0], self.before[2]]

    def device(self, core=None, x=None, y=None, z=None):
        core = self.core if core is None else core
        x = self.x if x is None else x
        y = self.y if y is None else y
        z = self.z if z is None else z
        return (z % 2 * 4 + x) * 2 + core, z // 2 * 4 + y


def put(part, tile, value):
    part[tile : tile + 12] = value.astype(BF16).reshape(12, 16, 128)


def block_kernel(
    grad_scale, valid_ref, tok_ref, cot_ref, table_ref, idx_in, g1_ref, wqkv_ref, wproj_ref,
    g2_ref, wup_ref, wdown_ref,
    updo_ref, dtoko_ref, full_ref, tab_ref,
    idx_ref, t2_ref, hot_ref, bias_ref, acc_ref, win, grid,
    band, side, corner, band_s, side_s, corner_s, band_r, side_r, corner_r,
    band_s2, side_s2, corner_s2, band_r2, side_r2, corner_r2,
    wqkvt_s, soft_s, trip_s, mrg_s, inv_s, first_s, resid_s, dres_s, dtrip_s, dsoft_s, dmrg_s, upd_s,
    dqkv_s, dproj_s, dup_s, ddown_s,
    part, full, early_bufs, late_bufs, tab_s, tab_r, tab_full, halo_sems, back_sems, tab_sems,
):
    ds_ref = bias_ref
    spot = Spot()
    barrier = pltpu.get_barrier_semaphore()
    for device in spot.all:
        pl.semaphore_signal(barrier, inc=1, device_id=device, device_id_type=MESH)
    valid = [valid_ref[i].astype(F32) for i in range(6)]
    cut_pieces(tok_ref, 0, valid, win, band, side, corner)
    cut_pieces(cot_ref, 1, valid, win, band, side, corner)
    for source, target in ((band, band_s), (side, side_s), (corner, corner_s)):
        target[...] = source[...].astype(BF16)
    gather = gather_bias(table_ref, idx_in, bias_ref, idx_ref, t2_ref, hot_ref)
    lax.fori_loop(0, 10, gather, 0)
    pl.semaphore_wait(barrier, len(spot.all))
    pairs = ((band_s, band_r), (side_s, side_r), (corner_s, corner_r))
    halo = [
        remote(src, dst, halo_sems.at[0, i], halo_sems.at[1, i], spot.before[i])
        for i, (src, dst) in enumerate(pairs)
    ]
    start(halo)
    lax.fori_loop(10, GROUPS, gather, 0)
    wqkvt_s[...] = jnp.transpose(wqkv_ref[...].astype(F32)).astype(BF16)
    g1 = g1_ref[...].astype(F32).reshape(1, CH)
    g2 = g2_ref[...].astype(F32).reshape(1, CH)
    for ref in (dqkv_s, dproj_s, dup_s, ddown_s, acc_ref):
        ref[...] = jnp.zeros_like(ref)
    finish(halo)
    add_pieces(win, band_r, side_r, corner_r)

    def forward(zone, carry):
        windows = [zone * 2, zone * 2 + 1]
        triples, scores, softs = [], [], []
        for w in windows:
            first = (normed(win[0, w])[0] * g1).astype(BF16)
            first_s[w] = first
            triple = dot(wqkvt_s[...], first, 1, 1)
            queries = (triple[0:CH] * (SCALE * LOG2E)).astype(BF16)
            triples.append(jnp.concatenate([queries, triple[CH : 3 * CH].astype(BF16)], axis=0))
        for triple in triples:
            for h in range(HEADS):
                query = triple[h * WIDTH : (h + 1) * WIDTH]
                keys = triple[CH + h * WIDTH : CH + (h + 1) * WIDTH]
                at = pl.ds(pl.multiple_of((h * ZONES + zone) * PLACES, PLACES), PLACES)
                bias = jnp.concatenate([bias_ref[0, at, :], bias_ref[1, at, 0:16]], axis=1)
                scores.append(dot(keys, query, 0, 0) + bias)
        for score in scores:
            weights = jnp.exp2(score - jnp.max(score, axis=0, keepdims=True))
            softs.append((weights.astype(BF16), 1.0 / jnp.sum(weights, axis=0, keepdims=True)))
        for side, w in enumerate(windows):
            merged = []
            for h in range(HEADS):
                weights, inv = softs[side * HEADS + h]
                values = triples[side][2 * CH + h * WIDTH : 2 * CH + (h + 1) * WIDTH]
                merged.append((dot(values, weights) * inv).astype(BF16))
            merged = jnp.concatenate(merged, axis=0)
            mrg_s[w] = merged
            attended = dot(merged, wproj_ref[...], 0, 0).astype(BF16).astype(F32)
            resid_s[w] = (win[0, w] + attended).astype(BF16)
        for side, w in enumerate(windows):
            trip_s[w] = triples[side]
            for h in range(HEADS):
                weights, inv = softs[side * HEADS + h]
                soft_s[w * HEADS + h] = weights
                inv_s[w, h : h + 1] = inv
        return carry

    lax.fori_loop(0, ZONES, forward, 0)

    many = 4
    chunk = many * PLACES

    def feed_forward(c, carry):
        here = pl.ds(c * many, many)
        resid = resid_s[here].reshape(chunk, CH).astype(F32)
        up_f = win[1, here].reshape(chunk, CH)
        up = up_f.astype(BF16)
        unit, rscale = normed(resid)
        second = unit * g2
        pre = dot(second.astype(BF16), wup_ref[...])
        c0, c1 = 0.7978845608028654, 0.7978845608028654 * 0.044715
        sq = pre * pre
        tanh = jnp.tanh(pre * (c0 + c1 * sq))
        half = 0.5 + 0.5 * tanh
        hidden = (pre * half).astype(BF16)
        slope = half + half * (1.0 - tanh) * pre * (c0 + (3.0 * c1) * sq)
        upd_s[here] = (resid + dot(hidden, wdown_ref[...], 1, 1)).reshape(many, PLACES, CH)
        ddown_s[...] += dot(jnp.transpose(up_f).astype(BF16), hidden)
        d_pre = (slope * dot(up, wdown_ref[...])).astype(BF16)
        dup_s[...] += dot(jnp.transpose(second).astype(BF16), d_pre)
        d_norm = dot(d_pre, wup_ref[...], 1, 1)
        d_in = norm_back(unit, rscale, g2, d_norm)
        dres_s[here] = (d_in + up_f).reshape(many, PLACES, CH)
        return carry

    lax.fori_loop(0, WINDOWS // many, feed_forward, 0)

    for i in range(6):
        put(part, 12 * i, dup_s[:, 128 * i : 128 * i + 128] * grad_scale)
        put(part, 72 + 12 * i, ddown_s[:, 128 * i : 128 * i + 128] * grad_scale)
    early = AllReduce(EARLY, part, full, spot, early_bufs)
    late = AllReduce(LATE, part, full, spot, late_bufs)
    early.step(0)

    cut_back(upd_s, 0, grid, band, side, corner)
    back_pairs = ((band, band_s2, band_r2), (side, side_s2, side_r2), (corner, corner_s2, corner_r2))

    def back_copies(f):
        return [
            remote(
                src.at[f], dst.at[f], back_sems.at[0, f, i], back_sems.at[1, f, i], spot.after[i]
            )
            for i, (_, src, dst) in enumerate(back_pairs)
        ]

    for source, target, _ in back_pairs:
        target[0] = source[0].astype(BF16)
    start(back_copies(0))

    def backward_scores(zone, carry):
        windows = [zone * 2, zone * 2 + 1]
        leans, d_scores = [], []
        for w in windows:
            d_merged = dot(wproj_ref[...], dres_s[w].astype(BF16), 1, 1)
            for h in range(HEADS):
                at = slice(h * WIDTH, (h + 1) * WIDTH)
                d_m = d_merged[at] * inv_s[w, h : h + 1]
                lean = jnp.sum(d_m * mrg_s[w, at].astype(F32), axis=0, keepdims=True)
                leans.append((d_m.astype(BF16), lean))
        for side, w in enumerate(windows):
            for h in range(HEADS):
                d_m, lean = leans[side * HEADS + h]
                values = trip_s[w, 2 * CH + h * WIDTH : 2 * CH + (h + 1) * WIDTH]
                d_chances = dot(values, d_m, 0, 0)
                d_scores.append(soft_s[w * HEADS + h].astype(F32) * (d_chances - lean))
        for h in range(HEADS):
            at = pl.ds(pl.multiple_of((h * ZONES + zone) * PLACES, PLACES), PLACES)
            both = d_scores[h] + d_scores[HEADS + h]
            ds_ref[0, at, :] = both[:, 0:128]
            ds_ref[1, at, 0:16] = both[:, 128:PLACES]
        for side, w in enumerate(windows):
            for h in range(HEADS):
                dsoft_s[w * HEADS + h] = d_scores[side * HEADS + h].astype(BF16)
                dmrg_s[w, h * WIDTH : (h + 1) * WIDTH] = leans[side * HEADS + h][0]
        pl.when(zone == 1)(functools.partial(early.step, 1))
        return carry

    lax.fori_loop(0, ZONES, backward_scores, 0)

    def backward_triple(zone, carry):
        windows = [zone * 2, zone * 2 + 1]
        for w in windows:
            out = []
            for h in range(HEADS):
                keys = trip_s[w, CH + h * WIDTH : CH + (h + 1) * WIDTH]
                out.append((dot(keys, dsoft_s[w * HEADS + h]) * SCALE).astype(BF16))
            for h in range(HEADS):
                query = trip_s[w, h * WIDTH : (h + 1) * WIDTH]
                d_keys = dot(query, dsoft_s[w * HEADS + h], 1, 1)
                out.append((d_keys * (1 / LOG2E)).astype(BF16))
            for h in range(HEADS):
                d_m = dmrg_s[w, h * WIDTH : (h + 1) * WIDTH]
                out.append(dot(d_m, soft_s[w * HEADS + h], 1, 1).astype(BF16))
            d_triple = jnp.concatenate(out, axis=0)
            first_t = jnp.transpose(first_s[w].astype(F32)).astype(BF16)
            dqkv_s[...] += dot(first_t, d_triple, 1, 1)
            dproj_s[...] += dot(mrg_s[w], dres_s[w].astype(BF16))
            dtrip_s[w] = d_triple
        pl.when(zone == 2)(functools.partial(early.step, 2))
        return carry

    lax.fori_loop(0, ZONES, backward_triple, 0)

    for i in range(4):
        put(part, 144 + 12 * i, dqkv_s[:, 128 * i : 128 * i + 128] * grad_scale)
    mixed = jnp.concatenate([dqkv_s[:, 512:576], dproj_s[:, 0:64]], axis=1)
    put(part, 192, mixed * grad_scale)
    put(part, 204, dproj_s[:, 64:192] * grad_scale)
    part[216:TILES] = jnp.zeros((TILES - 216, 16, 128), BF16)
    late.step(0)
    def scatter_groups(turn, carry):
        step = functools.partial(scatter_step, ds_ref, idx_ref, hot_ref, acc_ref)
        lax.fori_loop(turn * 3, turn * 3 + 3, step, 0)
        pl.when(turn == 0)(functools.partial(late.step, 1))
        pl.when(turn == 2)(functools.partial(early.step, 3))
        pl.when(turn == 5)(functools.partial(late.step, 2))
        return carry

    lax.fori_loop(0, 6, scatter_groups, 0)

    lon = spot.lon
    for i in range(PAIRS):
        tab_s[i] = (acc_ref[48 * i : 48 * i + 48] * grad_scale).astype(BF16)
    tab_s[PAIRS] = jnp.zeros((48, 256), BF16)

    def table_scatter():
        return [
            remote(
                tab_s.at[lax.rem(lon + d + 1, 8)],
                tab_r.at[d],
                tab_sems.at[0, d],
                tab_sems.at[1, d],
                spot.along_lon[d],
            )
            for d in range(7)
        ]

    def table_gather():
        return [
            remote(
                tab_full.at[lon],
                tab_full.at[lon],
                tab_sems.at[2, d],
                tab_sems.at[3, d],
                spot.along_lon[d],
            )
            for d in range(7)
        ]

    start(table_scatter())
    early.step(4)

    def backward_norm(zone, carry):
        for w in (zone * 2, zone * 2 + 1):
            d_first = dot(dtrip_s[w], wqkvt_s[...], 0, 0).astype(BF16).astype(F32)
            unit, rscale = normed(win[0, w])
            d_in = norm_back(unit, rscale, g1, d_first)
            upd_s[w] = dres_s[w] + d_in
        return carry

    lax.fori_loop(0, ZONES, backward_norm, 0)
    cut_back(upd_s, 1, grid, band, side, corner)
    for source, target, _ in back_pairs:
        target[1] = source[1].astype(BF16)
    start(back_copies(1))
    late.step(3)
    finish(table_scatter())
    total = tab_s[lon].astype(F32)
    for d in range(7):
        total += tab_r[d].astype(F32)
    tab_full[lon] = total.astype(BF16)
    start(table_gather())
    finish(back_copies(0))
    add_back(0, grid, band_r2, side_r2, corner_r2)
    for i in range(6):
        updo_ref[:, i] = (grid[0, :, i] * valid[i]).astype(BF16)
    early.step(5)
    full_ref[0:128] = full[0:128]
    finish(back_copies(1))
    add_back(1, grid, band_r2, side_r2, corner_r2)
    for i in range(6):
        dtoko_ref[:, i] = (grid[1, :, i] * valid[i]).astype(BF16)
    late.step(4)
    finish(table_gather())
    tab_ref[...] = tab_full[...]
    late.step(5)
    full_ref[128:TILES] = full[128:TILES]


def block_pass(grad_scale, *args):
    sd = jax.ShapeDtypeStruct
    sem = pltpu.SemaphoreType.DMA
    return pl.pallas_call(
        functools.partial(block_kernel, grad_scale),
        out_shape=[
            sd((8, 6, 24, CH), BF16),
            sd((8, 6, 24, CH), BF16),
            sd((TILES, 16, 128), BF16),
            sd((8, 48, 256), BF16),
        ],
        in_specs=[pl.BlockSpec(memory_space=pltpu.SMEM)] + [VMEM_SPEC] * 10,
        out_specs=[VMEM_SPEC] * 4,
        scratch_shapes=[
            vm((PLACES, 256), jnp.int32),
            vm((HI * ROWS, 256), F32),
            vm((GROUPS, 256, SPAN), BF16),
            vm((2, ROWS * PLACES, 128), F32),
            vm((PAIRS * 48, 256), F32),
            vm((2, WINDOWS, PLACES, CH), F32),
            vm((2, 8, 6, 24, CH), F32),
            *piece_scratch(),
            vm((3 * CH, CH), BF16),
            vm((WINDOWS * HEADS, PLACES, PLACES), BF16),
            vm((WINDOWS, 3 * CH, PLACES), BF16),
            vm((WINDOWS, CH, PLACES), BF16),
            vm((WINDOWS, 8, PLACES), F32),
            vm((WINDOWS, PLACES, CH), BF16),
            vm((WINDOWS, PLACES, CH), BF16),
            vm((WINDOWS, PLACES, CH), F32),
            vm((WINDOWS, 3 * CH, PLACES), BF16),
            vm((WINDOWS * HEADS, PLACES, PLACES), BF16),
            vm((WINDOWS, CH, PLACES), BF16),
            vm((WINDOWS, PLACES, CH), F32),
            vm((CH, 3 * CH), F32),
            vm((CH, CH), F32),
            vm((CH, HIDDEN), F32),
            vm((CH, HIDDEN), F32),
            vm((TILES, 16, 128), BF16),
            vm((TILES, 16, 128), BF16),
            all_reduce_scratch(EARLY),
            all_reduce_scratch(LATE),
            vm((8, 48, 256), BF16),
            vm((7, 48, 256), BF16),
            vm((8, 48, 256), BF16),
            sem((2, 3)),
            sem((2, 2, 3)),
            sem((4, 7)),
        ],
        compiler_params=pltpu.CompilerParams(
            vmem_limit_bytes=LIMIT, collective_id=0, has_side_effects=True
        ),
    )(*args)


def write_kernel(
    upd_ref, dtok_ref, full_ref, tab_ref, g1_ref, wqkv_ref, g2_ref, wup_ref,
    updo_ref, dtoko_ref, gain1_ref, qkv_ref, proj_ref, gain2_ref, up_ref, down_ref, table_ref,
):
    updo_ref[...] = upd_ref[...]
    dtoko_ref[...] = dtok_ref[...]

    def get(tile):
        return full_ref[tile : tile + 12].reshape(192, 128).astype(F32)

    for i in range(6):
        up_ref[:, 128 * i : 128 * i + 128] = get(12 * i)
        down_ref[:, 128 * i : 128 * i + 128] = get(72 + 12 * i)
    for i in range(4):
        qkv_ref[:, 128 * i : 128 * i + 128] = get(144 + 12 * i)
    mixed = get(192)
    qkv_ref[:, 512:576] = mixed[:, 0:64]
    proj_ref[...] = jnp.concatenate([mixed[:, 64:128], get(204)], axis=1)
    for weight, d_weight, gain, out in (
        (wqkv_ref, qkv_ref, g1_ref, gain1_ref),
        (wup_ref, up_ref, g2_ref, gain2_ref),
    ):
        sums = jnp.sum(weight[...].astype(F32) * d_weight[...], axis=1, keepdims=True)
        row = jnp.transpose(jnp.broadcast_to(sums, (CH, 128)))[0]
        out[...] = row / gain[...].astype(F32)
    for hi in range(HI):
        wide = min(256, ENTRIES - hi * 256)
        block = tab_ref[hi // 2].astype(F32)[hi % 2 * ROWS : (hi % 2 + 1) * ROWS]
        for head in range(HEADS):
            table_ref[head, :, hi * 256 : hi * 256 + wide] = block[
                head * ZONES : (head + 1) * ZONES, 0:wide
            ]


def write_out(*args):
    sd = jax.ShapeDtypeStruct
    return pl.pallas_call(
        write_kernel,
        out_shape=[
            sd((8, 6, 24, CH), BF16),
            sd((8, 6, 24, CH), BF16),
            sd((CH,), F32),
            sd((CH, 3 * CH), F32),
            sd((CH, CH), F32),
            sd((CH,), F32),
            sd((CH, HIDDEN), F32),
            sd((CH, HIDDEN), F32),
            sd((HEADS, ZONES, ENTRIES), F32),
        ],
        in_specs=[VMEM_SPEC] * 8,
        out_specs=[VMEM_SPEC] * 9,
        compiler_params=pltpu.CompilerParams(vmem_limit_bytes=LIMIT),
    )(*args)


def per_device(
    tokens,
    lat_valid,
    gain_attn,
    w_qkv,
    w_proj,
    gain_mlp,
    w_up,
    w_down,
    bias_table,
    index_table,
    cotangent,
):
    levels, row_count, col_count, channels = tokens.shape
    grad_scale = float(levels * row_count * col_count * 128) ** (-0.5)
    parts = block_pass(
        grad_scale,
        lat_valid,
        tokens,
        cotangent,
        bias_table.transpose(1, 0, 2),
        index_table,
        gain_attn,
        w_qkv,
        w_proj,
        gain_mlp,
        w_up,
        w_down.T,
    )
    updated, d_tokens, d_gain1, d_qkv, d_proj, d_gain2, d_up, d_down, d_table = write_out(
        *parts, gain_attn, w_qkv, gain_mlp, w_up
    )
    d_table = d_table.transpose(1, 0, 2)
    return updated, d_tokens, d_gain1, d_qkv, d_proj, d_gain2, d_up, d_down.T, d_table


def solution(mesh):
    field = P(None, "lat", "lon", None)
    in_specs = (field, P("lat"), P(), P(), P(), P(), P(), P(), P("lat"), P(), field)
    out_specs = (field, field, P(), P(), P(), P(), P(), P(), P("lat"))
    return jax.shard_map(
        per_device, mesh=mesh, in_specs=in_specs, out_specs=out_specs, check_vma=False
    )
```

```python
import functools
import jax
import jax.numpy as jnp
from jax import lax
from jax.sharding import PartitionSpec as P
from jax.experimental import pallas as pl
from jax.experimental.pallas import tpu as pltpu

WIN_Z = 2
WIN_LAT = 6
WIN_LON = 12
PLACES = 144
HEADS = 6
WIDTH = 32
CH = 192
HIDDEN = 768
WINDOWS = 8
TOKENS = 1152
ZONES = 4
ROWS = ZONES * HEADS
ENTRIES = 3312
HI = 13
PAIRS = 7
GROUPS = 18
SPAN = 1152
LOG2E = 1.4426950408889634
SCALE = 32**-0.5
NORM_EPS = 1e-05
F32 = jnp.float32
BF16 = jnp.bfloat16


def dot(left, right, left_dim=1, right_dim=0):
    return lax.dot_general(
        left, right, (((left_dim,), (right_dim,)), ((), ())), preferred_element_type=F32
    )


def entry_lanes(idx_ref, group):
    start = pl.multiple_of(group * 8, 8)
    main = idx_ref[pl.ds(start, 8), 0:128]
    rest = idx_ref[pl.ds(start, 8), 128:256].astype(F32)
    rest = pltpu.roll(rest, 0, 1, stride=16, stride_axis=0)
    place = lax.broadcasted_iota(jnp.int32, (8, 128), 0)
    lane = lax.broadcasted_iota(jnp.int32, (8, 128), 1)
    rest = jnp.sum(jnp.where(lane // 16 == place, rest, 0.0), axis=0, keepdims=True)
    rows = [main[i : i + 1] for i in range(8)] + [rest.astype(jnp.int32)]
    return jnp.concatenate(rows, axis=1)


def low_onehot(entries):
    low = jnp.broadcast_to((entries & 255).astype(F32).astype(BF16), (256, SPAN))
    at = lax.broadcasted_iota(jnp.int32, (256, SPAN), 0).astype(F32).astype(BF16)
    return jnp.where(low == at, jnp.ones((), BF16), jnp.zeros((), BF16))


def transposed_index(idx_in, idx_ref):
    idx_ref[:, 128:256] = jnp.zeros((PLACES, 128), jnp.int32)
    idx_ref[:, 0:PLACES] = jnp.transpose(idx_in[...].astype(F32)).astype(jnp.int32)


def region_of(place, last_zone, last_band):
    depth = place // (WIN_LAT * WIN_LON)
    row = place // WIN_LON % WIN_LAT
    level = jnp.where(depth >= WIN_Z - WIN_Z // 2, 2, 1) * last_zone
    band = jnp.where(row >= WIN_LAT - WIN_LAT // 2, 2, 1) * last_band
    return 3 * level + band


def gather_bias(table_ref, idx_in, bias_ref, idx_ref, t2_ref, hot_ref):
    last_band = (lax.axis_index("lat") == 15).astype(jnp.int32)
    transposed_index(idx_in, idx_ref)
    for hi in range(HI):
        wide = min(256, ENTRIES - hi * 256)
        for head in range(HEADS):
            part = table_ref[head, :, hi * 256 : hi * 256 + wide] * LOG2E
            if wide < 256:
                part = jnp.concatenate([part, jnp.zeros((ZONES, 256 - wide), F32)], axis=1)
            t2_ref[hi * ROWS + head * ZONES : hi * ROWS + (head + 1) * ZONES, :] = part

    def step(group, carry):
        entries = entry_lanes(idx_ref, group)
        onehot = low_onehot(entries)
        hot_ref[group] = onehot
        found = dot(t2_ref[...].astype(BF16), onehot)
        high = jnp.broadcast_to(entries >> 8, (ROWS, SPAN))
        bias = jnp.where(high == 0, found[0:ROWS], 0.0)
        for hi in range(1, HI):
            bias = jnp.where(high == hi, found[hi * ROWS : (hi + 1) * ROWS], bias)
        lane = lax.broadcasted_iota(jnp.int32, (ROWS, 128), 1)
        zone3 = (lax.broadcasted_iota(jnp.int32, (ROWS, 128), 0) % ZONES == ZONES - 1).astype(
            jnp.int32
        )
        main_region = region_of(lane, zone3, last_band)
        rest_region = region_of((lane & 15) + 128, zone3, last_band)
        rest = bias[:, 1024:1152]
        for i in range(8):
            key = group * 8 + i
            key_region = region_of(jnp.full((ROWS, 128), key, jnp.int32), zone3, last_band)
            main_i = jnp.where(
                main_region == key_region, bias[:, i * 128 : (i + 1) * 128], -1e30
            )
            rest_i = rest if i == 0 else pltpu.roll(rest, 128 - 16 * i, 1)
            rest_i = jnp.where(rest_region == key_region, rest_i, -1e30)
            bias_ref[0, pl.ds(key, ROWS, stride=PLACES), :] = main_i
            bias_ref[1, pl.ds(key, ROWS, stride=PLACES), :] = rest_i
        return carry

    return step


def scatter_step(ds_ref, idx_ref, hot_ref, acc_ref, group, carry):
    entries = entry_lanes(idx_ref, group)
    lane = lax.broadcasted_iota(jnp.int32, (ROWS, 128), 1)
    mains, rest = [], jnp.zeros((ROWS, 128), F32)
    for i in range(8):
        key = group * 8 + i
        mains.append(ds_ref[0, pl.ds(key, ROWS, stride=PLACES), :])
        rest_i = ds_ref[1, pl.ds(key, ROWS, stride=PLACES), :]
        if i:
            rest_i = pltpu.roll(rest_i, 16 * i, 1)
        rest = jnp.where(lane // 16 == i, rest_i, rest)
    grads = jnp.concatenate(mains + [rest], axis=1)
    grads = jnp.concatenate([grads, grads], axis=0).astype(BF16)
    high = jnp.broadcast_to((entries >> 8).astype(F32), (ROWS, SPAN))
    high = jnp.concatenate([high, high - 1.0], axis=0).astype(BF16)
    zero = jnp.zeros((), BF16)
    parts = [jnp.where(high == jnp.full((), 2 * i, BF16), grads, zero) for i in range(PAIRS)]
    acc_ref[...] += dot(jnp.concatenate(parts, axis=0), hot_ref[group], 1, 1)
    return carry


def normed(values):
    center = values - jnp.mean(values, axis=-1, keepdims=True)
    rscale = lax.rsqrt(jnp.mean(center * center, axis=-1, keepdims=True) + NORM_EPS)
    return center * rscale, rscale


def norm_back(unit, rscale, gain, incoming):
    scaled = incoming * gain
    d_inputs = rscale * (
        scaled
        - jnp.mean(scaled, axis=-1, keepdims=True)
        - unit * jnp.mean(scaled * unit, axis=-1, keepdims=True)
    )
    return d_inputs


VMEM_SPEC = pl.BlockSpec(memory_space=pltpu.VMEM)
LIMIT = 60 * 1024 * 1024


def vm(shape, dtype):
    return pltpu.VMEM(shape, dtype)


MESH = pl.DeviceIdType.MESH
BAND_ROWS, SIDE_ROWS = 224, 80


def remote(src, dst, send, recv, device):
    return pltpu.make_async_remote_copy(
        src_ref=src, dst_ref=dst, send_sem=send, recv_sem=recv, device_id=device, device_id_type=MESH
    )


def places():
    lat, lon = lax.axis_index("lat"), lax.axis_index("lon")
    up, down = lax.rem(lat + 1, 16), lax.rem(lat + 15, 16)
    right, left = lax.rem(lon + 1, 8), lax.rem(lon + 7, 8)
    after = [(up, lon), (lat, right), (up, right)]
    before = [(down, lon), (lat, left), (down, left)]
    return after, before


def spot_of(zone, piece, count):
    at = (zone % 2 * 6 + piece) * count
    return slice(at, at + count), slice(zone // 2 * CH, (zone // 2 + 1) * CH)


def cut_pieces(field, f, valid, win, band, side, corner):
    for zone in range(ZONES):
        for depth in range(2):
            level = (2 * zone + depth + 1) % 8
            for i in range(6):
                row = field[level, i].astype(F32) * valid[i]
                piece = depth * 3 + i % 3
                if i < 3:
                    band[f, *spot_of(zone, piece, 18)] = row[6:24]
                    corner[f, *spot_of(zone, piece, 6)] = row[0:6]
                else:
                    side[f, *spot_of(zone, piece, 6)] = row[0:6]
                    at = (depth * 6 + i - 3) * 12
                    win[f, 2 * zone, at : at + 12] = row[6:18]
                    win[f, 2 * zone + 1, at : at + 6] = row[18:24]


def add_pieces(win, band, side, corner):
    for f in range(2):
        band_v = band[f].astype(F32)
        side_v = side[f].astype(F32)
        corner_v = corner[f].astype(F32)
        for zone in range(ZONES):
            for depth in range(2):
                for i in range(3):
                    piece = depth * 3 + i
                    at = (depth * 6 + i) * 12
                    win[f, 2 * zone + 1, at + 6 : at + 12] = side_v[spot_of(zone, piece, 6)]
                    at = (depth * 6 + i + 3) * 12
                    rows = band_v[spot_of(zone, piece, 18)]
                    win[f, 2 * zone, at : at + 12] = rows[0:12]
                    win[f, 2 * zone + 1, at : at + 6] = rows[12:18]
                    win[f, 2 * zone + 1, at + 6 : at + 12] = corner_v[spot_of(zone, piece, 6)]


def cut_back(field, f, grid, band, side, corner):
    for zone in range(ZONES):
        near = field[2 * zone]
        far = field[2 * zone + 1]
        for depth in range(2):
            level = (2 * zone + depth + 1) % 8
            for i in range(6):
                at = (depth * 6 + i) * 12
                piece = depth * 3 + i % 3
                if i < 3:
                    grid[f, level, i + 3, 6:18] = near[at : at + 12]
                    grid[f, level, i + 3, 18:24] = far[at : at + 6]
                    side[f, *spot_of(zone, piece, 6)] = far[at + 6 : at + 12]
                else:
                    rows, lanes = spot_of(zone, piece, 18)
                    band[f, rows.start : rows.start + 12, lanes] = near[at : at + 12]
                    band[f, rows.start + 12 : rows.stop, lanes] = far[at : at + 6]
                    corner[f, *spot_of(zone, piece, 6)] = far[at + 6 : at + 12]


def add_back(f, grid, band, side, corner):
    band_v = band[f].astype(F32)
    side_v = side[f].astype(F32)
    corner_v = corner[f].astype(F32)
    for zone in range(ZONES):
        for depth in range(2):
            level = (2 * zone + depth + 1) % 8
            for i in range(3):
                piece = depth * 3 + i
                grid[f, level, i, 6:24] = band_v[spot_of(zone, piece, 18)]
                grid[f, level, i, 0:6] = corner_v[spot_of(zone, piece, 6)]
                grid[f, level, i + 3, 0:6] = side_v[spot_of(zone, piece, 6)]


def piece_scratch():
    out = []
    for kind in (F32, BF16, BF16, BF16, BF16):
        for rows in (BAND_ROWS, SIDE_ROWS, SIDE_ROWS):
            out.append(vm((2, rows, 2 * CH), kind))
    return out


TILES = 224
EARLY = (0, 64, 4)
LATE = (128, 48, 3)


class AllReduce:
    def __init__(self, plan, part, full, spot, bufs):
        self.base, self.half, self.count = plan
        self.part, self.full, self.spot = part, full, spot
        self.core_r, self.plane_r, self.depth_r = bufs[:3]
        self.core_sems, self.plane_sems, self.depth_sems = bufs[3:]
        self.mine = self.base + spot.core * self.half
        self.own = pl.ds(self.mine + spot.seat * self.count, self.count)

    def core_copy(self):
        other = self.base + (1 - self.spot.core) * self.half
        source = self.part.at[pl.ds(other, self.half)]
        return remote(
            source, self.core_r, self.core_sems.at[0], self.core_sems.at[1], self.spot.sibling
        )

    def core_back(self):
        region = self.full.at[pl.ds(self.mine, self.half)]
        return remote(
            region, region, self.core_sems.at[2], self.core_sems.at[3], self.spot.sibling
        )

    def scatter(self):
        copies = []
        for i, (seat, device) in enumerate(self.spot.plane):
            source = self.part.at[pl.ds(self.mine + seat * self.count, self.count)]
            sems = self.plane_sems
            copies.append(
                remote(source, self.plane_r.at[i], sems.at[0, i], sems.at[1, i], device)
            )
        return copies

    def gather(self):
        region, sems = self.full.at[self.own], self.plane_sems
        return [
            remote(region, region, sems.at[2, i], sems.at[3, i], device)
            for i, (_, device) in enumerate(self.spot.plane)
        ]

    def depth(self):
        source, sems = self.part.at[self.own], self.depth_sems
        target = self.depth_r.at[self.spot.z]
        return [
            remote(source, target, sems.at[0, d], sems.at[1, d], self.spot.along_z[d])
            for d in range(3)
        ]

    def step(self, number):
        if number == 0:
            self.core_copy().start()
        elif number == 1:
            self.core_copy().wait()
            half = pl.ds(self.mine, self.half)
            total = self.part[half].astype(F32) + self.core_r[...].astype(F32)
            self.part[half] = total.astype(BF16)
            start(self.scatter())
        elif number == 2:
            finish(self.scatter())
            total = self.part[self.own].astype(F32)
            for i in range(15):
                total += self.plane_r[i].astype(F32)
            total = total.astype(BF16)
            self.part[self.own] = total
            self.depth_r[pl.ds(self.spot.z, 1)] = total[None]
            start(self.depth())
        elif number == 3:
            finish(self.depth())
            total = self.depth_r[0].astype(F32)
            for d in range(1, 4):
                total += self.depth_r[d].astype(F32)
            self.full[self.own] = total.astype(BF16)
            start(self.gather())
        elif number == 4:
            finish(self.gather())
            self.core_back().start()
        else:
            self.core_back().wait()


def all_reduce_scratch(plan):
    _, half, count = plan
    sem = pltpu.SemaphoreType.DMA
    return [
        vm((half, 16, 128), BF16),
        vm((15, count, 16, 128), BF16),
        vm((4, count, 16, 128), BF16),
        sem((4,)),
        sem((4, 15)),
        sem((2, 3)),
    ]


def start(copies):
    for copy in copies:
        copy.start()


def finish(copies):
    for copy in copies:
        copy.wait()


class Spot:
    def __init__(self):
        lat, lon = lax.axis_index("lat"), lax.axis_index("lon")
        self.lat, self.lon = lat, lon
        self.core, self.x, z_lo = lat % 2, lat // 2 % 4, lat // 8
        self.y, z_hi = lon % 4, lon // 4
        self.z = z_hi * 2 + z_lo
        self.sibling = self.device(core=1 - self.core)
        self.seat = self.x * 4 + self.y
        self.plane = []
        for d in range(1, 16):
            x, y = lax.rem(self.x + d // 4, 4), lax.rem(self.y + d % 4, 4)
            self.plane.append((x * 4 + y, self.device(x=x, y=y)))
        self.along_z = [self.device(z=lax.rem(self.z + d, 4)) for d in range(1, 4)]
        self.along_lon = [(lat, lax.rem(lon + d, 8)) for d in range(1, 8)]
        self.after, self.before = places()
        far = [(lat, (1 - z_hi) * 4 + lax.rem(self.y + d, 4)) for d in range(1, 4)]
        self.all = [self.sibling] + [device for _, device in self.plane] + self.along_z + far
        self.all += [self.after[0], self.after[2], self.before[0], self.before[2]]

    def device(self, core=None, x=None, y=None, z=None):
        core = self.core if core is None else core
        x = self.x if x is None else x
        y = self.y if y is None else y
        z = self.z if z is None else z
        return (z % 2 * 4 + x) * 2 + core, z // 2 * 4 + y


def put(part, tile, value):
    part[tile : tile + 12] = value.astype(BF16).reshape(12, 16, 128)


def block_kernel(
    grad_scale, valid_ref, tok_ref, cot_ref, table_ref, idx_in, g1_ref, wqkv_ref, wproj_ref,
    g2_ref, wup_ref, wdown_ref,
    updo_ref, dtoko_ref, full_ref, tab_ref,
    idx_ref, t2_ref, hot_ref, bias_ref, acc_ref, win, grid,
    band, side, corner, band_s, side_s, corner_s, band_r, side_r, corner_r,
    band_s2, side_s2, corner_s2, band_r2, side_r2, corner_r2,
    wqkvt_s, soft_s, trip_s, mrg_s, inv_s, first_s, resid_s, dres_s, dtrip_s, dsoft_s, dmrg_s, upd_s,
    dqkv_s, dproj_s, dup_s, ddown_s,
    part, full, early_bufs, late_bufs, tab_s, tab_r, tab_full, halo_sems, back_sems, tab_sems,
):
    ds_ref = bias_ref
    spot = Spot()
    barrier = pltpu.get_barrier_semaphore()
    for device in spot.all:
        pl.semaphore_signal(barrier, inc=1, device_id=device, device_id_type=MESH)
    valid = [valid_ref[i].astype(F32) for i in range(6)]
    cut_pieces(tok_ref, 0, valid, win, band, side, corner)
    cut_pieces(cot_ref, 1, valid, win, band, side, corner)
    for source, target in ((band, band_s), (side, side_s), (corner, corner_s)):
        target[...] = source[...].astype(BF16)
    gather = gather_bias(table_ref, idx_in, bias_ref, idx_ref, t2_ref, hot_ref)
    lax.fori_loop(0, 10, gather, 0, unroll=2)
    pl.semaphore_wait(barrier, len(spot.all))
    pairs = ((band_s, band_r), (side_s, side_r), (corner_s, corner_r))
    halo = [
        remote(src, dst, halo_sems.at[0, i], halo_sems.at[1, i], spot.before[i])
        for i, (src, dst) in enumerate(pairs)
    ]
    start(halo)
    lax.fori_loop(10, GROUPS, gather, 0, unroll=2)
    wqkvt_s[...] = jnp.transpose(wqkv_ref[...].astype(F32)).astype(BF16)
    g1 = g1_ref[...].astype(F32).reshape(1, CH)
    g2 = g2_ref[...].astype(F32).reshape(1, CH)
    for ref in (dqkv_s, dproj_s, dup_s, ddown_s, acc_ref):
        ref[...] = jnp.zeros_like(ref)
    finish(halo)
    add_pieces(win, band_r, side_r, corner_r)

    def forward(zone, carry):
        windows = [zone * 2, zone * 2 + 1]
        triples, scores, softs = [], [], []
        for w in windows:
            first = (normed(win[0, w])[0] * g1).astype(BF16)
            first_s[w] = first
            triple = dot(wqkvt_s[...], first, 1, 1)
            queries = (triple[0:CH] * (SCALE * LOG2E)).astype(BF16)
            triples.append(jnp.concatenate([queries, triple[CH : 3 * CH].astype(BF16)], axis=0))
        for triple in triples:
            for h in range(HEADS):
                query = triple[h * WIDTH : (h + 1) * WIDTH]
                keys = triple[CH + h * WIDTH : CH + (h + 1) * WIDTH]
                at = pl.ds(pl.multiple_of((h * ZONES + zone) * PLACES, PLACES), PLACES)
                bias = jnp.concatenate([bias_ref[0, at, :], bias_ref[1, at, 0:16]], axis=1)
                scores.append(dot(keys, query, 0, 0) + bias)
        for score in scores:
            weights = jnp.exp2(score - jnp.max(score, axis=0, keepdims=True))
            softs.append((weights.astype(BF16), 1.0 / jnp.sum(weights, axis=0, keepdims=True)))
        for side, w in enumerate(windows):
            merged = []
            for h in range(HEADS):
                weights, inv = softs[side * HEADS + h]
                values = triples[side][2 * CH + h * WIDTH : 2 * CH + (h + 1) * WIDTH]
                merged.append((dot(values, weights) * inv).astype(BF16))
            merged = jnp.concatenate(merged, axis=0)
            mrg_s[w] = merged
            attended = dot(merged, wproj_ref[...], 0, 0).astype(BF16).astype(F32)
            resid_s[w] = (win[0, w] + attended).astype(BF16)
        for side, w in enumerate(windows):
            trip_s[w] = triples[side]
            for h in range(HEADS):
                weights, inv = softs[side * HEADS + h]
                soft_s[w * HEADS + h] = weights
                inv_s[w, h : h + 1] = inv
        return carry


    many = 2
    chunk = many * PLACES

    def feed_forward(c, carry):
        here = pl.ds(c * many, many)
        resid = resid_s[here].reshape(chunk, CH).astype(F32)
        up_f = win[1, here].reshape(chunk, CH)
        up = up_f.astype(BF16)
        unit, rscale = normed(resid)
        second = unit * g2
        pre = dot(second.astype(BF16), wup_ref[...])
        c0, c1 = 0.7978845608028654, 0.7978845608028654 * 0.044715
        sq = pre * pre
        tanh = jnp.tanh(pre * (c0 + c1 * sq))
        half = 0.5 + 0.5 * tanh
        hidden = (pre * half).astype(BF16)
        slope = half + half * (1.0 - tanh) * pre * (c0 + (3.0 * c1) * sq)
        upd_s[here] = (resid + dot(hidden, wdown_ref[...], 1, 1)).reshape(many, PLACES, CH)
        ddown_s[...] += dot(jnp.transpose(up_f).astype(BF16), hidden)
        d_pre = (slope * dot(up, wdown_ref[...])).astype(BF16)
        dup_s[...] += dot(jnp.transpose(second).astype(BF16), d_pre)
        d_norm = dot(d_pre, wup_ref[...], 1, 1)
        d_in = norm_back(unit, rscale, g2, d_norm)
        dres_s[here] = (d_in + up_f).reshape(many, PLACES, CH)
        return carry

    def feed_and_forward(zone, carry):
        feed_forward(zone - 1, carry)
        return forward(zone, carry)

    forward(0, 0)
    lax.fori_loop(1, ZONES, feed_and_forward, 0)
    feed_forward(ZONES - 1, 0)

    for i in range(6):
        put(part, 12 * i, dup_s[:, 128 * i : 128 * i + 128] * grad_scale)
        put(part, 72 + 12 * i, ddown_s[:, 128 * i : 128 * i + 128] * grad_scale)
    early = AllReduce(EARLY, part, full, spot, early_bufs)
    late = AllReduce(LATE, part, full, spot, late_bufs)
    early.step(0)

    cut_back(upd_s, 0, grid, band, side, corner)
    back_pairs = ((band, band_s2, band_r2), (side, side_s2, side_r2), (corner, corner_s2, corner_r2))

    def back_copies(f):
        return [
            remote(
                src.at[f], dst.at[f], back_sems.at[0, f, i], back_sems.at[1, f, i], spot.after[i]
            )
            for i, (_, src, dst) in enumerate(back_pairs)
        ]

    for source, target, _ in back_pairs:
        target[0] = source[0].astype(BF16)
    start(back_copies(0))

    def backward_scores(zone, carry):
        windows = [zone * 2, zone * 2 + 1]
        leans, d_scores = [], []
        for w in windows:
            d_merged = dot(wproj_ref[...], dres_s[w].astype(BF16), 1, 1)
            for h in range(HEADS):
                at = slice(h * WIDTH, (h + 1) * WIDTH)
                d_m = d_merged[at] * inv_s[w, h : h + 1]
                lean = jnp.sum(d_m * mrg_s[w, at].astype(F32), axis=0, keepdims=True)
                leans.append((d_m.astype(BF16), lean))
        for side, w in enumerate(windows):
            for h in range(HEADS):
                d_m, lean = leans[side * HEADS + h]
                values = trip_s[w, 2 * CH + h * WIDTH : 2 * CH + (h + 1) * WIDTH]
                d_chances = dot(values, d_m, 0, 0)
                d_scores.append(soft_s[w * HEADS + h].astype(F32) * (d_chances - lean))
        for h in range(HEADS):
            at = pl.ds(pl.multiple_of((h * ZONES + zone) * PLACES, PLACES), PLACES)
            both = d_scores[h] + d_scores[HEADS + h]
            ds_ref[0, at, :] = both[:, 0:128]
            ds_ref[1, at, 0:16] = both[:, 128:PLACES]
        for side, w in enumerate(windows):
            for h in range(HEADS):
                dsoft_s[w * HEADS + h] = d_scores[side * HEADS + h].astype(BF16)
                dmrg_s[w, h * WIDTH : (h + 1) * WIDTH] = leans[side * HEADS + h][0]
        pl.when(zone == 1)(functools.partial(early.step, 1))
        return carry

    lax.fori_loop(0, ZONES, backward_scores, 0)

    def backward_triple(zone, carry):
        windows = [zone * 2, zone * 2 + 1]
        for w in windows:
            out = []
            for h in range(HEADS):
                keys = trip_s[w, CH + h * WIDTH : CH + (h + 1) * WIDTH]
                out.append((dot(keys, dsoft_s[w * HEADS + h]) * SCALE).astype(BF16))
            for h in range(HEADS):
                query = trip_s[w, h * WIDTH : (h + 1) * WIDTH]
                d_keys = dot(query, dsoft_s[w * HEADS + h], 1, 1)
                out.append((d_keys * (1 / LOG2E)).astype(BF16))
            for h in range(HEADS):
                d_m = dmrg_s[w, h * WIDTH : (h + 1) * WIDTH]
                out.append(dot(d_m, soft_s[w * HEADS + h], 1, 1).astype(BF16))
            d_triple = jnp.concatenate(out, axis=0)
            first_t = jnp.transpose(first_s[w].astype(F32)).astype(BF16)
            dqkv_s[...] += dot(first_t, d_triple, 1, 1)
            dproj_s[...] += dot(mrg_s[w], dres_s[w].astype(BF16))
            dtrip_s[w] = d_triple
        pl.when(zone == 2)(functools.partial(early.step, 2))
        return carry

    lax.fori_loop(0, ZONES, backward_triple, 0)

    for i in range(4):
        put(part, 144 + 12 * i, dqkv_s[:, 128 * i : 128 * i + 128] * grad_scale)
    mixed = jnp.concatenate([dqkv_s[:, 512:576], dproj_s[:, 0:64]], axis=1)
    put(part, 192, mixed * grad_scale)
    put(part, 204, dproj_s[:, 64:192] * grad_scale)
    part[216:TILES] = jnp.zeros((TILES - 216, 16, 128), BF16)
    late.step(0)
    def scatter_groups(turn, carry):
        step = functools.partial(scatter_step, ds_ref, idx_ref, hot_ref, acc_ref)
        for i in range(3):
            step(turn * 3 + i, 0)
        pl.when(turn == 0)(functools.partial(late.step, 1))
        pl.when(turn == 2)(functools.partial(early.step, 3))
        pl.when(turn == 5)(functools.partial(late.step, 2))
        return carry

    lax.fori_loop(0, 6, scatter_groups, 0)

    lon = spot.lon
    for i in range(PAIRS):
        tab_s[i] = (acc_ref[48 * i : 48 * i + 48] * grad_scale).astype(BF16)
    tab_s[PAIRS] = jnp.zeros((48, 256), BF16)

    def table_scatter():
        return [
            remote(
                tab_s.at[lax.rem(lon + d + 1, 8)],
                tab_r.at[d],
                tab_sems.at[0, d],
                tab_sems.at[1, d],
                spot.along_lon[d],
            )
            for d in range(7)
        ]

    def table_gather():
        return [
            remote(
                tab_full.at[lon],
                tab_full.at[lon],
                tab_sems.at[2, d],
                tab_sems.at[3, d],
                spot.along_lon[d],
            )
            for d in range(7)
        ]

    start(table_scatter())
    early.step(4)

    def backward_norm(zone, carry):
        for w in (zone * 2, zone * 2 + 1):
            d_first = dot(dtrip_s[w], wqkvt_s[...], 0, 0).astype(BF16).astype(F32)
            unit, rscale = normed(win[0, w])
            d_in = norm_back(unit, rscale, g1, d_first)
            upd_s[w] = dres_s[w] + d_in
        return carry

    lax.fori_loop(0, ZONES, backward_norm, 0)
    cut_back(upd_s, 1, grid, band, side, corner)
    for source, target, _ in back_pairs:
        target[1] = source[1].astype(BF16)
    start(back_copies(1))
    late.step(3)
    finish(table_scatter())
    total = tab_s[lon].astype(F32)
    for d in range(7):
        total += tab_r[d].astype(F32)
    tab_full[lon] = total.astype(BF16)
    start(table_gather())
    finish(back_copies(0))
    add_back(0, grid, band_r2, side_r2, corner_r2)
    for i in range(6):
        updo_ref[:, i] = (grid[0, :, i] * valid[i]).astype(BF16)
    early.step(5)
    full_ref[0:128] = full[0:128]
    finish(back_copies(1))
    add_back(1, grid, band_r2, side_r2, corner_r2)
    for i in range(6):
        dtoko_ref[:, i] = (grid[1, :, i] * valid[i]).astype(BF16)
    late.step(4)
    finish(table_gather())
    tab_ref[...] = tab_full[...]
    late.step(5)
    full_ref[128:TILES] = full[128:TILES]


def block_pass(grad_scale, *args):
    sd = jax.ShapeDtypeStruct
    sem = pltpu.SemaphoreType.DMA
    return pl.pallas_call(
        functools.partial(block_kernel, grad_scale),
        out_shape=[
            sd((8, 6, 24, CH), BF16),
            sd((8, 6, 24, CH), BF16),
            sd((TILES, 16, 128), BF16),
            sd((8, 48, 256), BF16),
        ],
        in_specs=[pl.BlockSpec(memory_space=pltpu.SMEM)] + [VMEM_SPEC] * 10,
        out_specs=[VMEM_SPEC] * 4,
        scratch_shapes=[
            vm((PLACES, 256), jnp.int32),
            vm((HI * ROWS, 256), F32),
            vm((GROUPS, 256, SPAN), BF16),
            vm((2, ROWS * PLACES, 128), F32),
            vm((PAIRS * 48, 256), F32),
            vm((2, WINDOWS, PLACES, CH), F32),
            vm((2, 8, 6, 24, CH), F32),
            *piece_scratch(),
            vm((3 * CH, CH), BF16),
            vm((WINDOWS * HEADS, PLACES, PLACES), BF16),
            vm((WINDOWS, 3 * CH, PLACES), BF16),
            vm((WINDOWS, CH, PLACES), BF16),
            vm((WINDOWS, 8, PLACES), F32),
            vm((WINDOWS, PLACES, CH), BF16),
            vm((WINDOWS, PLACES, CH), BF16),
            vm((WINDOWS, PLACES, CH), F32),
            vm((WINDOWS, 3 * CH, PLACES), BF16),
            vm((WINDOWS * HEADS, PLACES, PLACES), BF16),
            vm((WINDOWS, CH, PLACES), BF16),
            vm((WINDOWS, PLACES, CH), F32),
            vm((CH, 3 * CH), F32),
            vm((CH, CH), F32),
            vm((CH, HIDDEN), F32),
            vm((CH, HIDDEN), F32),
            vm((TILES, 16, 128), BF16),
            vm((TILES, 16, 128), BF16),
            all_reduce_scratch(EARLY),
            all_reduce_scratch(LATE),
            vm((8, 48, 256), BF16),
            vm((7, 48, 256), BF16),
            vm((8, 48, 256), BF16),
            sem((2, 3)),
            sem((2, 2, 3)),
            sem((4, 7)),
        ],
        compiler_params=pltpu.CompilerParams(
            vmem_limit_bytes=LIMIT, collective_id=0, has_side_effects=True
        ),
    )(*args)


def write_kernel(
    upd_ref, dtok_ref, full_ref, tab_ref, g1_ref, wqkv_ref, g2_ref, wup_ref,
    updo_ref, dtoko_ref, gain1_ref, qkv_ref, proj_ref, gain2_ref, up_ref, down_ref, table_ref,
):
    updo_ref[...] = upd_ref[...]
    dtoko_ref[...] = dtok_ref[...]

    def get(tile):
        return full_ref[tile : tile + 12].reshape(192, 128).astype(F32)

    for i in range(6):
        up_ref[:, 128 * i : 128 * i + 128] = get(12 * i)
        down_ref[:, 128 * i : 128 * i + 128] = get(72 + 12 * i)
    for i in range(4):
        qkv_ref[:, 128 * i : 128 * i + 128] = get(144 + 12 * i)
    mixed = get(192)
    qkv_ref[:, 512:576] = mixed[:, 0:64]
    proj_ref[...] = jnp.concatenate([mixed[:, 64:128], get(204)], axis=1)
    for weight, d_weight, gain, out in (
        (wqkv_ref, qkv_ref, g1_ref, gain1_ref),
        (wup_ref, up_ref, g2_ref, gain2_ref),
    ):
        sums = jnp.sum(weight[...].astype(F32) * d_weight[...], axis=1, keepdims=True)
        row = jnp.transpose(jnp.broadcast_to(sums, (CH, 128)))[0]
        out[...] = row / gain[...].astype(F32)
    for hi in range(HI):
        wide = min(256, ENTRIES - hi * 256)
        block = tab_ref[hi // 2].astype(F32)[hi % 2 * ROWS : (hi % 2 + 1) * ROWS]
        for head in range(HEADS):
            table_ref[head, :, hi * 256 : hi * 256 + wide] = block[
                head * ZONES : (head + 1) * ZONES, 0:wide
            ]


def write_out(*args):
    sd = jax.ShapeDtypeStruct
    return pl.pallas_call(
        write_kernel,
        out_shape=[
            sd((8, 6, 24, CH), BF16),
            sd((8, 6, 24, CH), BF16),
            sd((CH,), F32),
            sd((CH, 3 * CH), F32),
            sd((CH, CH), F32),
            sd((CH,), F32),
            sd((CH, HIDDEN), F32),
            sd((CH, HIDDEN), F32),
            sd((HEADS, ZONES, ENTRIES), F32),
        ],
        in_specs=[VMEM_SPEC] * 8,
        out_specs=[VMEM_SPEC] * 9,
        compiler_params=pltpu.CompilerParams(vmem_limit_bytes=LIMIT),
    )(*args)


def per_device(
    tokens,
    lat_valid,
    gain_attn,
    w_qkv,
    w_proj,
    gain_mlp,
    w_up,
    w_down,
    bias_table,
    index_table,
    cotangent,
):
    levels, row_count, col_count, channels = tokens.shape
    grad_scale = float(levels * row_count * col_count * 128) ** (-0.5)
    parts = block_pass(
        grad_scale,
        lat_valid,
        tokens,
        cotangent,
        bias_table.transpose(1, 0, 2),
        index_table,
        gain_attn,
        w_qkv,
        w_proj,
        gain_mlp,
        w_up,
        w_down.T,
    )
    updated, d_tokens, d_gain1, d_qkv, d_proj, d_gain2, d_up, d_down, d_table = write_out(
        *parts, gain_attn, w_qkv, gain_mlp, w_up
    )
    d_table = d_table.transpose(1, 0, 2)
    return updated, d_tokens, d_gain1, d_qkv, d_proj, d_gain2, d_up, d_down.T, d_table


def solution(mesh):
    field = P(None, "lat", "lon", None)
    in_specs = (field, P("lat"), P(), P(), P(), P(), P(), P(), P("lat"), P(), field)
    out_specs = (field, field, P(), P(), P(), P(), P(), P(), P("lat"))
    return jax.shard_map(
        per_device, mesh=mesh, in_specs=in_specs, out_specs=out_specs, check_vma=False
    )
```

```python
import functools
import jax
import jax.numpy as jnp
from jax import lax
from jax.sharding import PartitionSpec as P
from jax.experimental import pallas as pl
from jax.experimental.pallas import tpu as pltpu

WIN_Z = 2
WIN_LAT = 6
WIN_LON = 12
PLACES = 144
HEADS = 6
WIDTH = 32
CH = 192
HIDDEN = 768
WINDOWS = 8
TOKENS = 1152
ZONES = 4
ROWS = ZONES * HEADS
ENTRIES = 3312
HI = 13
PAIRS = 7
GROUPS = 18
SPAN = 1152
LOG2E = 1.4426950408889634
SCALE = 32**-0.5
NORM_EPS = 1e-05
F32 = jnp.float32
BF16 = jnp.bfloat16


def dot(left, right, left_dim=1, right_dim=0):
    return lax.dot_general(
        left, right, (((left_dim,), (right_dim,)), ((), ())), preferred_element_type=F32
    )


def entry_lanes(idx_ref, group):
    start = pl.multiple_of(group * 8, 8)
    main = idx_ref[pl.ds(start, 8), 0:128]
    rest = idx_ref[pl.ds(start, 8), 128:256].astype(F32)
    rest = pltpu.roll(rest, 0, 1, stride=16, stride_axis=0)
    place = lax.broadcasted_iota(jnp.int32, (8, 128), 0)
    lane = lax.broadcasted_iota(jnp.int32, (8, 128), 1)
    rest = jnp.sum(jnp.where(lane // 16 == place, rest, 0.0), axis=0, keepdims=True)
    rows = [main[i : i + 1] for i in range(8)] + [rest.astype(jnp.int32)]
    return jnp.concatenate(rows, axis=1)


def low_onehot(entries):
    low = jnp.broadcast_to((entries & 255).astype(F32).astype(BF16), (256, SPAN))
    at = lax.broadcasted_iota(jnp.int32, (256, SPAN), 0).astype(F32).astype(BF16)
    return jnp.where(low == at, jnp.ones((), BF16), jnp.zeros((), BF16))


def transposed_index(idx_in, idx_ref):
    idx_ref[:, 128:256] = jnp.zeros((PLACES, 128), jnp.int32)
    idx_ref[:, 0:PLACES] = jnp.transpose(idx_in[...].astype(F32)).astype(jnp.int32)


def region_of(place, last_zone, last_band):
    depth = place // (WIN_LAT * WIN_LON)
    row = place // WIN_LON % WIN_LAT
    level = jnp.where(depth >= WIN_Z - WIN_Z // 2, 2, 1) * last_zone
    band = jnp.where(row >= WIN_LAT - WIN_LAT // 2, 2, 1) * last_band
    return 3 * level + band


def gather_bias(table_ref, idx_in, bias_ref, idx_ref, t2_ref, hot_ref):
    last_band = (lax.axis_index("lat") == 15).astype(jnp.int32)
    transposed_index(idx_in, idx_ref)
    for hi in range(HI):
        wide = min(256, ENTRIES - hi * 256)
        for head in range(HEADS):
            part = table_ref[head, :, hi * 256 : hi * 256 + wide] * LOG2E
            if wide < 256:
                part = jnp.concatenate([part, jnp.zeros((ZONES, 256 - wide), F32)], axis=1)
            t2_ref[hi * ROWS + head * ZONES : hi * ROWS + (head + 1) * ZONES, :] = part

    def step(group, carry):
        entries = entry_lanes(idx_ref, group)
        onehot = low_onehot(entries)
        hot_ref[group] = onehot
        found = dot(t2_ref[...].astype(BF16), onehot)
        high = jnp.broadcast_to(entries >> 8, (ROWS, SPAN))
        bias = jnp.where(high == 0, found[0:ROWS], 0.0)
        for hi in range(1, HI):
            bias = jnp.where(high == hi, found[hi * ROWS : (hi + 1) * ROWS], bias)
        lane = lax.broadcasted_iota(jnp.int32, (ROWS, 128), 1)
        zone3 = (lax.broadcasted_iota(jnp.int32, (ROWS, 128), 0) % ZONES == ZONES - 1).astype(
            jnp.int32
        )
        main_region = region_of(lane, zone3, last_band)
        rest_region = region_of((lane & 15) + 128, zone3, last_band)
        rest = bias[:, 1024:1152]
        for i in range(8):
            key = group * 8 + i
            key_region = region_of(jnp.full((ROWS, 128), key, jnp.int32), zone3, last_band)
            main_i = jnp.where(
                main_region == key_region, bias[:, i * 128 : (i + 1) * 128], -1e30
            )
            rest_i = rest if i == 0 else pltpu.roll(rest, 128 - 16 * i, 1)
            rest_i = jnp.where(rest_region == key_region, rest_i, -1e30)
            bias_ref[0, pl.ds(key, ROWS, stride=PLACES), :] = main_i
            bias_ref[1, pl.ds(key, ROWS, stride=PLACES), :] = rest_i
        return carry

    return step


def scatter_step(ds_ref, idx_ref, hot_ref, acc_ref, group, carry):
    entries = entry_lanes(idx_ref, group)
    lane = lax.broadcasted_iota(jnp.int32, (ROWS, 128), 1)
    mains, rest = [], jnp.zeros((ROWS, 128), F32)
    for i in range(8):
        key = group * 8 + i
        mains.append(ds_ref[0, pl.ds(key, ROWS, stride=PLACES), :])
        rest_i = ds_ref[1, pl.ds(key, ROWS, stride=PLACES), :]
        if i:
            rest_i = pltpu.roll(rest_i, 16 * i, 1)
        rest = jnp.where(lane // 16 == i, rest_i, rest)
    grads = jnp.concatenate(mains + [rest], axis=1)
    grads = jnp.concatenate([grads, grads], axis=0).astype(BF16)
    high = jnp.broadcast_to((entries >> 8).astype(F32), (ROWS, SPAN))
    high = jnp.concatenate([high, high - 1.0], axis=0).astype(BF16)
    zero = jnp.zeros((), BF16)
    parts = [jnp.where(high == jnp.full((), 2 * i, BF16), grads, zero) for i in range(PAIRS)]
    acc_ref[...] += dot(jnp.concatenate(parts, axis=0), hot_ref[group], 1, 1)
    return carry


def normed(values):
    center = values - jnp.mean(values, axis=-1, keepdims=True)
    rscale = lax.rsqrt(jnp.mean(center * center, axis=-1, keepdims=True) + NORM_EPS)
    return center * rscale, rscale


def norm_back(unit, rscale, gain, incoming):
    scaled = incoming * gain
    d_inputs = rscale * (
        scaled
        - jnp.mean(scaled, axis=-1, keepdims=True)
        - unit * jnp.mean(scaled * unit, axis=-1, keepdims=True)
    )
    return d_inputs


VMEM_SPEC = pl.BlockSpec(memory_space=pltpu.VMEM)
LIMIT = 60 * 1024 * 1024


def vm(shape, dtype):
    return pltpu.VMEM(shape, dtype)


MESH = pl.DeviceIdType.MESH
BAND_ROWS, SIDE_ROWS = 224, 80


def remote(src, dst, send, recv, device):
    return pltpu.make_async_remote_copy(
        src_ref=src, dst_ref=dst, send_sem=send, recv_sem=recv, device_id=device, device_id_type=MESH
    )


def places():
    lat, lon = lax.axis_index("lat"), lax.axis_index("lon")
    up, down = lax.rem(lat + 1, 16), lax.rem(lat + 15, 16)
    right, left = lax.rem(lon + 1, 8), lax.rem(lon + 7, 8)
    after = [(up, lon), (lat, right), (up, right)]
    before = [(down, lon), (lat, left), (down, left)]
    return after, before


def spot_of(zone, piece, count):
    at = (zone % 2 * 6 + piece) * count
    return slice(at, at + count), slice(zone // 2 * CH, (zone // 2 + 1) * CH)


def cut_pieces(field, f, valid, win, band, side, corner):
    for zone in range(ZONES):
        for depth in range(2):
            level = (2 * zone + depth + 1) % 8
            for i in range(6):
                row = field[level, i].astype(F32) * valid[i]
                piece = depth * 3 + i % 3
                if i < 3:
                    band[f, *spot_of(zone, piece, 18)] = row[6:24]
                    corner[f, *spot_of(zone, piece, 6)] = row[0:6]
                else:
                    side[f, *spot_of(zone, piece, 6)] = row[0:6]
                    at = (depth * 6 + i - 3) * 12
                    win[f, 2 * zone, at : at + 12] = row[6:18]
                    win[f, 2 * zone + 1, at : at + 6] = row[18:24]


def add_pieces(f, win, band, side, corner):
    band_v = band[f].astype(F32)
    side_v = side[f].astype(F32)
    corner_v = corner[f].astype(F32)
    for zone in range(ZONES):
        for depth in range(2):
            for i in range(3):
                piece = depth * 3 + i
                at = (depth * 6 + i) * 12
                win[f, 2 * zone + 1, at + 6 : at + 12] = side_v[spot_of(zone, piece, 6)]
                at = (depth * 6 + i + 3) * 12
                rows = band_v[spot_of(zone, piece, 18)]
                win[f, 2 * zone, at : at + 12] = rows[0:12]
                win[f, 2 * zone + 1, at : at + 6] = rows[12:18]
                win[f, 2 * zone + 1, at + 6 : at + 12] = corner_v[spot_of(zone, piece, 6)]


def cut_back(field, f, grid, band, side, corner):
    for zone in range(ZONES):
        near = field[2 * zone]
        far = field[2 * zone + 1]
        for depth in range(2):
            level = (2 * zone + depth + 1) % 8
            for i in range(6):
                at = (depth * 6 + i) * 12
                piece = depth * 3 + i % 3
                if i < 3:
                    grid[f, level, i + 3, 6:18] = near[at : at + 12]
                    grid[f, level, i + 3, 18:24] = far[at : at + 6]
                    side[f, *spot_of(zone, piece, 6)] = far[at + 6 : at + 12]
                else:
                    rows, lanes = spot_of(zone, piece, 18)
                    band[f, rows.start : rows.start + 12, lanes] = near[at : at + 12]
                    band[f, rows.start + 12 : rows.stop, lanes] = far[at : at + 6]
                    corner[f, *spot_of(zone, piece, 6)] = far[at + 6 : at + 12]


def add_back(f, grid, band, side, corner):
    band_v = band[f].astype(F32)
    side_v = side[f].astype(F32)
    corner_v = corner[f].astype(F32)
    for zone in range(ZONES):
        for depth in range(2):
            level = (2 * zone + depth + 1) % 8
            for i in range(3):
                piece = depth * 3 + i
                grid[f, level, i, 6:24] = band_v[spot_of(zone, piece, 18)]
                grid[f, level, i, 0:6] = corner_v[spot_of(zone, piece, 6)]
                grid[f, level, i + 3, 0:6] = side_v[spot_of(zone, piece, 6)]


def piece_scratch():
    out = []
    for kind in (F32, BF16, BF16, BF16, BF16):
        for rows in (BAND_ROWS, SIDE_ROWS, SIDE_ROWS):
            out.append(vm((2, rows, 2 * CH), kind))
    return out


TILES = 224
EARLY = (0, 64, 4)
LATE = (128, 48, 3)


class AllReduce:
    def __init__(self, plan, part, full, spot, bufs):
        self.base, self.half, self.count = plan
        self.part, self.full, self.spot = part, full, spot
        self.core_r, self.plane_r, self.depth_r = bufs[:3]
        self.core_sems, self.plane_sems, self.depth_sems = bufs[3:]
        self.mine = self.base + spot.core * self.half
        self.own = pl.ds(self.mine + spot.seat * self.count, self.count)

    def core_copy(self):
        other = self.base + (1 - self.spot.core) * self.half
        source = self.part.at[pl.ds(other, self.half)]
        return remote(
            source, self.core_r, self.core_sems.at[0], self.core_sems.at[1], self.spot.sibling
        )

    def core_back(self):
        region = self.full.at[pl.ds(self.mine, self.half)]
        return remote(
            region, region, self.core_sems.at[2], self.core_sems.at[3], self.spot.sibling
        )

    def scatter(self):
        copies = []
        for i, (seat, device) in enumerate(self.spot.plane):
            source = self.part.at[pl.ds(self.mine + seat * self.count, self.count)]
            sems = self.plane_sems
            copies.append(
                remote(source, self.plane_r.at[i], sems.at[0, i], sems.at[1, i], device)
            )
        return copies

    def gather(self):
        region, sems = self.full.at[self.own], self.plane_sems
        return [
            remote(region, region, sems.at[2, i], sems.at[3, i], device)
            for i, (_, device) in enumerate(self.spot.plane)
        ]

    def depth(self):
        source, sems = self.part.at[self.own], self.depth_sems
        target = self.depth_r.at[self.spot.z]
        return [
            remote(source, target, sems.at[0, d], sems.at[1, d], self.spot.along_z[d])
            for d in range(3)
        ]

    def step(self, number):
        if number == 0:
            self.core_copy().start()
        elif number == 1:
            self.core_copy().wait()
            half = pl.ds(self.mine, self.half)
            total = self.part[half].astype(F32) + self.core_r[...].astype(F32)
            self.part[half] = total.astype(BF16)
            start(self.scatter())
        elif number == 2:
            finish(self.scatter())
            total = self.part[self.own].astype(F32)
            for i in range(15):
                total += self.plane_r[i].astype(F32)
            total = total.astype(BF16)
            self.part[self.own] = total
            self.depth_r[pl.ds(self.spot.z, 1)] = total[None]
            start(self.depth())
        elif number == 3:
            finish(self.depth())
            total = self.depth_r[0].astype(F32)
            for d in range(1, 4):
                total += self.depth_r[d].astype(F32)
            self.full[self.own] = total.astype(BF16)
            start(self.gather())
        elif number == 4:
            finish(self.gather())
            self.core_back().start()
        else:
            self.core_back().wait()


def all_reduce_scratch(plan):
    _, half, count = plan
    sem = pltpu.SemaphoreType.DMA
    return [
        vm((half, 16, 128), BF16),
        vm((15, count, 16, 128), BF16),
        vm((4, count, 16, 128), BF16),
        sem((4,)),
        sem((4, 15)),
        sem((2, 3)),
    ]


def start(copies):
    for copy in copies:
        copy.start()


def finish(copies):
    for copy in copies:
        copy.wait()


class Spot:
    def __init__(self):
        lat, lon = lax.axis_index("lat"), lax.axis_index("lon")
        self.lat, self.lon = lat, lon
        self.core, self.x, z_lo = lat % 2, lat // 2 % 4, lat // 8
        self.y, z_hi = lon % 4, lon // 4
        self.z = z_hi * 2 + z_lo
        self.sibling = self.device(core=1 - self.core)
        self.seat = self.x * 4 + self.y
        self.plane = []
        for d in range(1, 16):
            x, y = lax.rem(self.x + d // 4, 4), lax.rem(self.y + d % 4, 4)
            self.plane.append((x * 4 + y, self.device(x=x, y=y)))
        self.along_z = [self.device(z=lax.rem(self.z + d, 4)) for d in range(1, 4)]
        self.along_lon = [(lat, lax.rem(lon + d, 8)) for d in range(1, 8)]
        self.after, self.before = places()
        far = [(lat, (1 - z_hi) * 4 + lax.rem(self.y + d, 4)) for d in range(1, 4)]
        self.all = [self.sibling] + [device for _, device in self.plane] + self.along_z + far
        self.all += [self.after[0], self.after[2], self.before[0], self.before[2]]

    def device(self, core=None, x=None, y=None, z=None):
        core = self.core if core is None else core
        x = self.x if x is None else x
        y = self.y if y is None else y
        z = self.z if z is None else z
        return (z % 2 * 4 + x) * 2 + core, z // 2 * 4 + y


def put(part, tile, value):
    part[tile : tile + 12] = value.astype(BF16).reshape(12, 16, 128)


def block_kernel(
    grad_scale, valid_ref, tok_ref, cot_ref, table_ref, idx_in, g1_ref, wqkv_ref, wproj_ref,
    g2_ref, wup_ref, wdown_ref,
    updo_ref, dtoko_ref, full_ref, tab_ref,
    idx_ref, t2_ref, hot_ref, bias_ref, acc_ref, win, grid,
    band, side, corner, band_s, side_s, corner_s, band_r, side_r, corner_r,
    band_s2, side_s2, corner_s2, band_r2, side_r2, corner_r2,
    wqkvt_s, soft_s, trip_s, mrg_s, inv_s, first_s, resid_s, dres_s, dtrip_s, dsoft_s, dmrg_s, upd_s,
    dqkv_s, dproj_s, dup_s, ddown_s,
    part, full, early_bufs, late_bufs, tab_s, tab_r, tab_full, halo_sems, back_sems, tab_sems,
):
    ds_ref = bias_ref
    spot = Spot()
    barrier = pltpu.get_barrier_semaphore()
    for device in spot.all:
        pl.semaphore_signal(barrier, inc=1, device_id=device, device_id_type=MESH)
    valid = [valid_ref[i].astype(F32) for i in range(6)]
    cut_pieces(tok_ref, 0, valid, win, band, side, corner)
    cut_pieces(cot_ref, 1, valid, win, band, side, corner)
    for source, target in ((band, band_s), (side, side_s), (corner, corner_s)):
        target[...] = source[...].astype(BF16)
    gather = gather_bias(table_ref, idx_in, bias_ref, idx_ref, t2_ref, hot_ref)
    lax.fori_loop(0, 10, gather, 0, unroll=2)
    pl.semaphore_wait(barrier, len(spot.all))
    pairs = ((band_s, band_r), (side_s, side_r), (corner_s, corner_r))
    halo = [
        [
            remote(
                src.at[f], dst.at[f], halo_sems.at[0, f, i], halo_sems.at[1, f, i], spot.before[i]
            )
            for i, (src, dst) in enumerate(pairs)
        ]
        for f in range(2)
    ]
    start(halo[0])
    lax.fori_loop(10, 14, gather, 0, unroll=2)
    start(halo[1])
    lax.fori_loop(14, GROUPS, gather, 0, unroll=2)
    wqkvt_s[...] = jnp.transpose(wqkv_ref[...].astype(F32)).astype(BF16)
    g1 = g1_ref[...].astype(F32).reshape(1, CH)
    g2 = g2_ref[...].astype(F32).reshape(1, CH)
    for ref in (dqkv_s, dproj_s, dup_s, ddown_s, acc_ref):
        ref[...] = jnp.zeros_like(ref)
    finish(halo[0])
    add_pieces(0, win, band_r, side_r, corner_r)

    def forward(zone, carry):
        windows = [zone * 2, zone * 2 + 1]
        triples, scores, softs = [], [], []
        for w in windows:
            first = (normed(win[0, w])[0] * g1).astype(BF16)
            first_s[w] = first
            triple = dot(wqkvt_s[...], first, 1, 1)
            queries = (triple[0:CH] * (SCALE * LOG2E)).astype(BF16)
            triples.append(jnp.concatenate([queries, triple[CH : 3 * CH].astype(BF16)], axis=0))
        for triple in triples:
            for h in range(HEADS):
                query = triple[h * WIDTH : (h + 1) * WIDTH]
                keys = triple[CH + h * WIDTH : CH + (h + 1) * WIDTH]
                at = pl.ds(pl.multiple_of((h * ZONES + zone) * PLACES, PLACES), PLACES)
                bias = jnp.concatenate([bias_ref[0, at, :], bias_ref[1, at, 0:16]], axis=1)
                scores.append(dot(keys, query, 0, 0) + bias)
        for score in scores:
            weights = jnp.exp2(score - jnp.max(score, axis=0, keepdims=True))
            softs.append((weights.astype(BF16), 1.0 / jnp.sum(weights, axis=0, keepdims=True)))
        for side, w in enumerate(windows):
            merged = []
            for h in range(HEADS):
                weights, inv = softs[side * HEADS + h]
                values = triples[side][2 * CH + h * WIDTH : 2 * CH + (h + 1) * WIDTH]
                merged.append((dot(values, weights) * inv).astype(BF16))
            merged = jnp.concatenate(merged, axis=0)
            mrg_s[w] = merged
            attended = dot(merged, wproj_ref[...], 0, 0).astype(BF16).astype(F32)
            resid_s[w] = (win[0, w] + attended).astype(BF16)
        for side, w in enumerate(windows):
            trip_s[w] = triples[side]
            for h in range(HEADS):
                weights, inv = softs[side * HEADS + h]
                soft_s[w * HEADS + h] = weights
                inv_s[w, h : h + 1] = inv
        return carry


    many = 2
    chunk = many * PLACES

    def feed_forward(c, carry):
        here = pl.ds(c * many, many)
        resid = resid_s[here].reshape(chunk, CH).astype(F32)
        up_f = win[1, here].reshape(chunk, CH)
        up = up_f.astype(BF16)
        unit, rscale = normed(resid)
        second = unit * g2
        pre = dot(second.astype(BF16), wup_ref[...])
        c0, c1 = 0.7978845608028654, 0.7978845608028654 * 0.044715
        sq = pre * pre
        tanh = jnp.tanh(pre * (c0 + c1 * sq))
        half = 0.5 + 0.5 * tanh
        hidden = (pre * half).astype(BF16)
        slope = half + half * (1.0 - tanh) * pre * (c0 + (3.0 * c1) * sq)
        upd_s[here] = (resid + dot(hidden, wdown_ref[...], 1, 1)).reshape(many, PLACES, CH)
        ddown_s[...] += dot(jnp.transpose(up_f).astype(BF16), hidden)
        d_pre = (slope * dot(up, wdown_ref[...])).astype(BF16)
        dup_s[...] += dot(jnp.transpose(second).astype(BF16), d_pre)
        d_norm = dot(d_pre, wup_ref[...], 1, 1)
        d_in = norm_back(unit, rscale, g2, d_norm)
        dres_s[here] = (d_in + up_f).reshape(many, PLACES, CH)
        return carry

    def feed_and_forward(zone, carry):
        feed_forward(zone - 1, carry)
        return forward(zone, carry)

    forward(0, 0)
    finish(halo[1])
    add_pieces(1, win, band_r, side_r, corner_r)
    lax.fori_loop(1, ZONES, feed_and_forward, 0)
    feed_forward(ZONES - 1, 0)

    for i in range(6):
        put(part, 12 * i, dup_s[:, 128 * i : 128 * i + 128] * grad_scale)
        put(part, 72 + 12 * i, ddown_s[:, 128 * i : 128 * i + 128] * grad_scale)
    early = AllReduce(EARLY, part, full, spot, early_bufs)
    late = AllReduce(LATE, part, full, spot, late_bufs)
    early.step(0)

    cut_back(upd_s, 0, grid, band, side, corner)
    back_pairs = ((band, band_s2, band_r2), (side, side_s2, side_r2), (corner, corner_s2, corner_r2))

    def back_copies(f):
        return [
            remote(
                src.at[f], dst.at[f], back_sems.at[0, f, i], back_sems.at[1, f, i], spot.after[i]
            )
            for i, (_, src, dst) in enumerate(back_pairs)
        ]

    for source, target, _ in back_pairs:
        target[0] = source[0].astype(BF16)
    start(back_copies(0))

    def backward_scores(zone, carry):
        windows = [zone * 2, zone * 2 + 1]
        leans, d_scores = [], []
        for w in windows:
            d_merged = dot(wproj_ref[...], dres_s[w].astype(BF16), 1, 1)
            for h in range(HEADS):
                at = slice(h * WIDTH, (h + 1) * WIDTH)
                d_m = d_merged[at] * inv_s[w, h : h + 1]
                lean = jnp.sum(d_m * mrg_s[w, at].astype(F32), axis=0, keepdims=True)
                leans.append((d_m.astype(BF16), lean))
        for side, w in enumerate(windows):
            for h in range(HEADS):
                d_m, lean = leans[side * HEADS + h]
                values = trip_s[w, 2 * CH + h * WIDTH : 2 * CH + (h + 1) * WIDTH]
                d_chances = dot(values, d_m, 0, 0)
                d_scores.append(soft_s[w * HEADS + h].astype(F32) * (d_chances - lean))
        for h in range(HEADS):
            at = pl.ds(pl.multiple_of((h * ZONES + zone) * PLACES, PLACES), PLACES)
            both = d_scores[h] + d_scores[HEADS + h]
            ds_ref[0, at, :] = both[:, 0:128]
            ds_ref[1, at, 0:16] = both[:, 128:PLACES]
        for side, w in enumerate(windows):
            for h in range(HEADS):
                dsoft_s[w * HEADS + h] = d_scores[side * HEADS + h].astype(BF16)
                dmrg_s[w, h * WIDTH : (h + 1) * WIDTH] = leans[side * HEADS + h][0]
        pl.when(zone == 1)(functools.partial(early.step, 1))
        return carry

    lax.fori_loop(0, ZONES, backward_scores, 0)

    def backward_triple(zone, carry):
        windows = [zone * 2, zone * 2 + 1]
        for w in windows:
            out = []
            for h in range(HEADS):
                keys = trip_s[w, CH + h * WIDTH : CH + (h + 1) * WIDTH]
                out.append((dot(keys, dsoft_s[w * HEADS + h]) * SCALE).astype(BF16))
            for h in range(HEADS):
                query = trip_s[w, h * WIDTH : (h + 1) * WIDTH]
                d_keys = dot(query, dsoft_s[w * HEADS + h], 1, 1)
                out.append((d_keys * (1 / LOG2E)).astype(BF16))
            for h in range(HEADS):
                d_m = dmrg_s[w, h * WIDTH : (h + 1) * WIDTH]
                out.append(dot(d_m, soft_s[w * HEADS + h], 1, 1).astype(BF16))
            d_triple = jnp.concatenate(out, axis=0)
            first_t = jnp.transpose(first_s[w].astype(F32)).astype(BF16)
            dqkv_s[...] += dot(first_t, d_triple, 1, 1)
            dproj_s[...] += dot(mrg_s[w], dres_s[w].astype(BF16))
            dtrip_s[w] = d_triple
        pl.when(zone == 2)(functools.partial(early.step, 2))
        return carry

    lax.fori_loop(0, ZONES, backward_triple, 0)

    for i in range(4):
        put(part, 144 + 12 * i, dqkv_s[:, 128 * i : 128 * i + 128] * grad_scale)
    mixed = jnp.concatenate([dqkv_s[:, 512:576], dproj_s[:, 0:64]], axis=1)
    put(part, 192, mixed * grad_scale)
    put(part, 204, dproj_s[:, 64:192] * grad_scale)
    part[216:TILES] = jnp.zeros((TILES - 216, 16, 128), BF16)
    late.step(0)
    def scatter_groups(turn, carry):
        step = functools.partial(scatter_step, ds_ref, idx_ref, hot_ref, acc_ref)
        for i in range(3):
            step(turn * 3 + i, 0)
        pl.when(turn == 0)(functools.partial(late.step, 1))
        pl.when(turn == 2)(functools.partial(early.step, 3))
        pl.when(turn == 5)(functools.partial(late.step, 2))
        return carry

    lax.fori_loop(0, 6, scatter_groups, 0)

    lon = spot.lon
    for i in range(PAIRS):
        tab_s[i] = (acc_ref[48 * i : 48 * i + 48] * grad_scale).astype(BF16)
    tab_s[PAIRS] = jnp.zeros((48, 256), BF16)

    def table_scatter():
        return [
            remote(
                tab_s.at[lax.rem(lon + d + 1, 8)],
                tab_r.at[d],
                tab_sems.at[0, d],
                tab_sems.at[1, d],
                spot.along_lon[d],
            )
            for d in range(7)
        ]

    def table_gather():
        return [
            remote(
                tab_full.at[lon],
                tab_full.at[lon],
                tab_sems.at[2, d],
                tab_sems.at[3, d],
                spot.along_lon[d],
            )
            for d in range(7)
        ]

    start(table_scatter())
    early.step(4)

    def backward_norm(zone, carry):
        for w in (zone * 2, zone * 2 + 1):
            d_first = dot(dtrip_s[w], wqkvt_s[...], 0, 0).astype(BF16).astype(F32)
            unit, rscale = normed(win[0, w])
            d_in = norm_back(unit, rscale, g1, d_first)
            upd_s[w] = dres_s[w] + d_in
        pl.when(zone == 2)(functools.partial(late.step, 3))
        return carry

    lax.fori_loop(0, ZONES, backward_norm, 0)
    cut_back(upd_s, 1, grid, band, side, corner)
    for source, target, _ in back_pairs:
        target[1] = source[1].astype(BF16)
    start(back_copies(1))
    finish(table_scatter())
    total = tab_s[lon].astype(F32)
    for d in range(7):
        total += tab_r[d].astype(F32)
    tab_full[lon] = total.astype(BF16)
    start(table_gather())
    finish(back_copies(0))
    add_back(0, grid, band_r2, side_r2, corner_r2)
    for i in range(6):
        updo_ref[:, i] = (grid[0, :, i] * valid[i]).astype(BF16)
    early.step(5)
    full_ref[0:128] = full[0:128]
    finish(back_copies(1))
    add_back(1, grid, band_r2, side_r2, corner_r2)
    for i in range(6):
        dtoko_ref[:, i] = (grid[1, :, i] * valid[i]).astype(BF16)
    late.step(4)
    finish(table_gather())
    tab_ref[...] = tab_full[...]
    late.step(5)
    full_ref[128:TILES] = full[128:TILES]


def block_pass(grad_scale, *args):
    sd = jax.ShapeDtypeStruct
    sem = pltpu.SemaphoreType.DMA
    return pl.pallas_call(
        functools.partial(block_kernel, grad_scale),
        out_shape=[
            sd((8, 6, 24, CH), BF16),
            sd((8, 6, 24, CH), BF16),
            sd((TILES, 16, 128), BF16),
            sd((8, 48, 256), BF16),
        ],
        in_specs=[pl.BlockSpec(memory_space=pltpu.SMEM)] + [VMEM_SPEC] * 10,
        out_specs=[VMEM_SPEC] * 4,
        scratch_shapes=[
            vm((PLACES, 256), jnp.int32),
            vm((HI * ROWS, 256), F32),
            vm((GROUPS, 256, SPAN), BF16),
            vm((2, ROWS * PLACES, 128), F32),
            vm((PAIRS * 48, 256), F32),
            vm((2, WINDOWS, PLACES, CH), F32),
            vm((2, 8, 6, 24, CH), F32),
            *piece_scratch(),
            vm((3 * CH, CH), BF16),
            vm((WINDOWS * HEADS, PLACES, PLACES), BF16),
            vm((WINDOWS, 3 * CH, PLACES), BF16),
            vm((WINDOWS, CH, PLACES), BF16),
            vm((WINDOWS, 8, PLACES), F32),
            vm((WINDOWS, PLACES, CH), BF16),
            vm((WINDOWS, PLACES, CH), BF16),
            vm((WINDOWS, PLACES, CH), F32),
            vm((WINDOWS, 3 * CH, PLACES), BF16),
            vm((WINDOWS * HEADS, PLACES, PLACES), BF16),
            vm((WINDOWS, CH, PLACES), BF16),
            vm((WINDOWS, PLACES, CH), F32),
            vm((CH, 3 * CH), F32),
            vm((CH, CH), F32),
            vm((CH, HIDDEN), F32),
            vm((CH, HIDDEN), F32),
            vm((TILES, 16, 128), BF16),
            vm((TILES, 16, 128), BF16),
            all_reduce_scratch(EARLY),
            all_reduce_scratch(LATE),
            vm((8, 48, 256), BF16),
            vm((7, 48, 256), BF16),
            vm((8, 48, 256), BF16),
            sem((2, 2, 3)),
            sem((2, 2, 3)),
            sem((4, 7)),
        ],
        compiler_params=pltpu.CompilerParams(
            vmem_limit_bytes=LIMIT, collective_id=0, has_side_effects=True
        ),
    )(*args)


def write_kernel(
    upd_ref, dtok_ref, full_ref, tab_ref, g1_ref, wqkv_ref, g2_ref, wup_ref,
    updo_ref, dtoko_ref, gain1_ref, qkv_ref, proj_ref, gain2_ref, up_ref, down_ref, table_ref,
):
    updo_ref[...] = upd_ref[...]
    dtoko_ref[...] = dtok_ref[...]

    def get(tile):
        return full_ref[tile : tile + 12].reshape(192, 128).astype(F32)

    for i in range(6):
        up_ref[:, 128 * i : 128 * i + 128] = get(12 * i)
        down_ref[:, 128 * i : 128 * i + 128] = get(72 + 12 * i)
    for i in range(4):
        qkv_ref[:, 128 * i : 128 * i + 128] = get(144 + 12 * i)
    mixed = get(192)
    qkv_ref[:, 512:576] = mixed[:, 0:64]
    proj_ref[...] = jnp.concatenate([mixed[:, 64:128], get(204)], axis=1)
    for weight, d_weight, gain, out in (
        (wqkv_ref, qkv_ref, g1_ref, gain1_ref),
        (wup_ref, up_ref, g2_ref, gain2_ref),
    ):
        sums = jnp.sum(weight[...].astype(F32) * d_weight[...], axis=1, keepdims=True)
        row = jnp.transpose(jnp.broadcast_to(sums, (CH, 128)))[0]
        out[...] = row / gain[...].astype(F32)
    for hi in range(HI):
        wide = min(256, ENTRIES - hi * 256)
        block = tab_ref[hi // 2].astype(F32)[hi % 2 * ROWS : (hi % 2 + 1) * ROWS]
        for head in range(HEADS):
            table_ref[head, :, hi * 256 : hi * 256 + wide] = block[
                head * ZONES : (head + 1) * ZONES, 0:wide
            ]


def write_out(*args):
    sd = jax.ShapeDtypeStruct
    return pl.pallas_call(
        write_kernel,
        out_shape=[
            sd((8, 6, 24, CH), BF16),
            sd((8, 6, 24, CH), BF16),
            sd((CH,), F32),
            sd((CH, 3 * CH), F32),
            sd((CH, CH), F32),
            sd((CH,), F32),
            sd((CH, HIDDEN), F32),
            sd((CH, HIDDEN), F32),
            sd((HEADS, ZONES, ENTRIES), F32),
        ],
        in_specs=[VMEM_SPEC] * 8,
        out_specs=[VMEM_SPEC] * 9,
        compiler_params=pltpu.CompilerParams(vmem_limit_bytes=LIMIT),
    )(*args)


def per_device(
    tokens,
    lat_valid,
    gain_attn,
    w_qkv,
    w_proj,
    gain_mlp,
    w_up,
    w_down,
    bias_table,
    index_table,
    cotangent,
):
    levels, row_count, col_count, channels = tokens.shape
    grad_scale = float(levels * row_count * col_count * 128) ** (-0.5)
    parts = block_pass(
        grad_scale,
        lat_valid,
        tokens,
        cotangent,
        bias_table.transpose(1, 0, 2),
        index_table,
        gain_attn,
        w_qkv,
        w_proj,
        gain_mlp,
        w_up,
        w_down.T,
    )
    updated, d_tokens, d_gain1, d_qkv, d_proj, d_gain2, d_up, d_down, d_table = write_out(
        *parts, gain_attn, w_qkv, gain_mlp, w_up
    )
    d_table = d_table.transpose(1, 0, 2)
    return updated, d_tokens, d_gain1, d_qkv, d_proj, d_gain2, d_up, d_down.T, d_table


def solution(mesh):
    field = P(None, "lat", "lon", None)
    in_specs = (field, P("lat"), P(), P(), P(), P(), P(), P(), P("lat"), P(), field)
    out_specs = (field, field, P(), P(), P(), P(), P(), P(), P("lat"))
    return jax.shard_map(
        per_device, mesh=mesh, in_specs=in_specs, out_specs=out_specs, check_vma=False
    )
```
